128 devices in a mesh: row: 8 (over y_hi, x), col: 16 (over y_lo, z, core).
Axes of the slice: x: 4, y: 4 (y_hi: 2, y_lo: 2; y = y_hi * 2 + y_lo), z: 4, core: 2. Of those that a mesh axis runs over, the one named last changes fastest.
Arguments:
- pair_in: bfloat16 [256, 256, 128], P('row', 'col'), may hold values from -6 to 6
- token_mask: int32 [256], replicated, may hold values 0 or 1
- cotangent: bfloat16 [256, 256, 128], P('row', 'col'), may hold values from -6 to 6
- gain_in: float32 [2, 128], replicated, may hold values from 0.1 to 1.9
- proj_w: bfloat16 [2, 128, 512], replicated, may hold values from -0.5 to 0.5
- gate_w: bfloat16 [2, 128, 128], replicated, may hold values from -0.5 to 0.5
- gain_mid: float32 [2, 128], replicated, may hold values from 0.1 to 1.9
- out_w: bfloat16 [2, 128, 128], replicated, may hold values from -0.5 to 0.5
Outputs:
- pair_out: bfloat16 [256, 256, 128], P('row', 'col')
- pair_grad: bfloat16 [256, 256, 128], P('row', 'col')
- gain_in_grad: float32 [2, 128], replicated
- proj_w_grad: float32 [2, 128, 512], replicated
- gate_w_grad: float32 [2, 128, 128], replicated
- gain_mid_grad: float32 [2, 128], replicated
- out_w_grad: float32 [2, 128, 128], replicated
The draws below stay inside these ranges and needn't reach their ends.
Inputs may be any that keep to these rules, and one draw needn't show every extreme that they name: token_mask holds only 0 and 1.
All inputs are finite; a program needn't handle non-finite values.
Results may differ from the reference program's by a relative error of at most 0.023.
Values may be sent and summed in bfloat16 or wider, within the bound.
No kernel may reach another device: no remote copies, remote signals or barrier semaphores. Data moves between devices by JAX's collectives and lax.ppermute only.
A program may use at most 128 MiB of HBM per device.

```python
import jax
import jax.numpy as jnp
from jax import lax

C = 128
CH = 128
N = 256


def with_ends(array, key, least, high):
    shape = array.shape
    index_at = [jax.random.randint(jax.random.fold_in(key, axis), (), 0, shape[axis]) for axis in range(len(shape))]
    array = array.at[tuple(index_at)].set(least)
    longest = shape.index(max(shape))
    index_at[longest] = (index_at[longest] + 1) % shape[longest]
    return array.at[tuple(index_at)].set(high)


def block_scale(stream_key, dims, pieces, low, high):
    loudness = 1.0
    for dim, parts in pieces:
        steps = jax.random.uniform(jax.random.fold_in(jax.random.fold_in(stream_key, 6), dim), (parts,), jnp.float32, low / len(pieces), high / len(pieces))
        loudness = loudness * jnp.repeat(jnp.exp(steps), dims[dim] // parts).reshape((-1,) + (1,) * (len(dims) - 1 - dim))
    return loudness


def bell_draw(key, extent, scale, most, split=(), dtype=jnp.bfloat16):
    level = block_scale(key, extent, split, -0.22, 0.18) if split else 1.0
    drawn = jax.random.normal(key, extent, jnp.float32) * scale * level
    return jnp.minimum(jnp.maximum(drawn, -most), most).astype(dtype)


def setup_inputs(seed: int = 0) -> dict:
    streams_of = jax.random.split(jax.random.key(seed), 9)
    return {
        "pair_in": bell_draw(streams_of[0], (N, N, C), 1.0, 6.0, ((0, 8), (1, 16))),
        "token_mask": with_ends((jax.random.randint(streams_of[1], (N,), 0, 8) < 7).astype(jnp.int32), jax.random.fold_in(streams_of[1], 1), 0, 1),
        "cotangent": bell_draw(streams_of[2], (N, N, C), 1.0, 6.0, ((0, 8), (1, 16))),
        "gain_in": jnp.clip(1.0 + 0.18 * jax.random.normal(streams_of[3], (2, C), jnp.float32), 0.1, 1.9),
        "proj_w": bell_draw(streams_of[4], (2, C, 4 * CH), C ** -0.5, 0.5),
        "gate_w": bell_draw(streams_of[5], (2, C, C), C ** -0.5, 0.5),
        "gain_mid": jnp.clip(1.0 + 0.18 * jax.random.normal(streams_of[6], (2, CH), jnp.float32), 0.1, 1.9),
        "out_w": bell_draw(streams_of[7], (2, CH, C), CH ** -0.5, 0.5),
    }


def normalize(values, gain):
    average = lax.optimization_barrier(jnp.mean(values, axis=-1, keepdims=True))
    centered = values - average
    variance = lax.optimization_barrier(jnp.mean(centered * centered, axis=-1, keepdims=True))
    return centered * lax.rsqrt(variance + 1e-05) * gain

def project(pair_f, gain, proj_f, gate_f, pair_mask):
    normed = normalize(pair_f, gain)
    projected = jnp.einsum('ijc,cd->ijd', normed, proj_f, precision=lax.Precision.HIGHEST)
    hidden = projected.shape[-1] // 4
    weight_mask = pair_mask[:, :, None]
    left_f = jax.nn.sigmoid(projected[..., :hidden]) * projected[..., hidden:2 * hidden] * weight_mask
    right_f = jax.nn.sigmoid(projected[..., 2 * hidden:3 * hidden]) * projected[..., 3 * hidden:] * weight_mask
    gating = jax.nn.sigmoid(jnp.einsum('ijc,cd->ijd', normed, gate_f, precision=lax.Precision.HIGHEST))
    return (left_f, right_f, gating)

def finish(mixture, gating, pair_f, gain, out_f):
    update = jnp.einsum('ijc,cd->ijd', normalize(mixture, gain), out_f, precision=lax.Precision.HIGHEST)
    return pair_f + update * gating

def contract(layer_idx, left_b, right_b):
    left_f = left_b.astype(jnp.float32)
    right_f = right_b.astype(jnp.float32)
    if layer_idx == 0:
        return jnp.einsum('ikh,jkh->ijh', left_f, right_f)
    return jnp.einsum('kih,kjh->ijh', left_f, right_f)

def contract_back(layer_idx, dmix_b, left_b, right_b):
    dmix_f = dmix_b.astype(jnp.float32)
    left_f = left_b.astype(jnp.float32)
    right_f = right_b.astype(jnp.float32)
    if layer_idx == 0:
        return (jnp.einsum('ijh,jkh->ikh', dmix_f, right_f), jnp.einsum('ijh,ikh->jkh', dmix_f, left_f))
    return (jnp.einsum('kjh,ijh->kih', right_f, dmix_f), jnp.einsum('kih,ijh->kjh', left_f, dmix_f))

def reference(pair_in, token_mask, cotangent, gain_in, proj_w, gate_w, gain_mid, out_w):
    token_f = token_mask.astype(jnp.float32)
    pair_mask = token_f[:, None] * token_f[None, :]
    current = pair_in.astype(jnp.float32)
    stored = []
    rounded = pair_in
    for layer_idx in range(2):
        proj_f = proj_w[layer_idx].astype(jnp.float32)
        gate_f = gate_w[layer_idx].astype(jnp.float32)
        out_f = out_w[layer_idx].astype(jnp.float32)
        left_f, right_f, gating = project(current, gain_in[layer_idx], proj_f, gate_f, pair_mask)
        left_b = left_f.astype(jnp.bfloat16)
        right_b = right_f.astype(jnp.bfloat16)
        mixture = contract(layer_idx, left_b, right_b)
        stored.append((current, left_b, right_b, gating, mixture))
        rounded = finish(mixture, gating, current, gain_mid[layer_idx], out_f).astype(jnp.bfloat16)
        current = lax.optimization_barrier(rounded).astype(jnp.float32)
    grad_pair = cotangent.astype(jnp.float32)
    grads_gin = [None, None]
    grads_proj = [None, None]
    grads_gate = [None, None]
    grads_gmid = [None, None]
    grads_out = [None, None]
    for layer_idx in (1, 0):
        current, left_b, right_b, gating, mixture = stored[layer_idx]
        proj_f = proj_w[layer_idx].astype(jnp.float32)
        gate_f = gate_w[layer_idx].astype(jnp.float32)
        out_f = out_w[layer_idx].astype(jnp.float32)
        _, pull_back = jax.vjp(finish, mixture, gating, current, gain_mid[layer_idx], out_f)
        d_mixture, d_gating, d_direct, d_gain_mid, d_out = pull_back(grad_pair)
        dmix_b = d_mixture.astype(jnp.bfloat16)
        d_left, d_right = contract_back(layer_idx, dmix_b, left_b, right_b)

        def front(pair_f, gain, proj_in, gate_in):
            return project(pair_f, gain, proj_in, gate_in, pair_mask)
        _, pull_front = jax.vjp(front, current, gain_in[layer_idx], proj_f, gate_f)
        d_pre, d_gain_in, d_proj, d_gate = pull_front((d_left, d_right, d_gating))
        grad_pair = d_direct + d_pre
        grads_gin[layer_idx] = d_gain_in
        grads_proj[layer_idx] = d_proj
        grads_gate[layer_idx] = d_gate
        grads_gmid[layer_idx] = d_gain_mid
        grads_out[layer_idx] = d_out
    scale = 1.0 / N
    return (rounded, grad_pair.astype(jnp.bfloat16), jnp.stack(grads_gin) * scale, jnp.stack(grads_proj) * scale, jnp.stack(grads_gate) * scale, jnp.stack(grads_gmid) * scale, jnp.stack(grads_out) * scale)
```

```python
import functools

import jax
import jax.numpy as jnp
from jax import lax
from jax.experimental import pallas as pl
from jax.experimental.pallas import tpu as pltpu
from jax.sharding import PartitionSpec as P

F32 = jnp.float32
BF16 = jnp.bfloat16
C = 128
LANES = 128
ROWS = 32
COLS = 16
TOKENS = 256
PLACE = ROWS * COLS
TILES = PLACE // LANES
PEERS = 128
AXES = ("row", "col")


def mm(a, b, a_dim, b_dim):
    return lax.dot_general(
        a.astype(BF16), b.astype(BF16), (((a_dim,), (b_dim,)), ((), ())), preferred_element_type=F32
    )


def tile(t):
    return pl.ds(t * LANES, LANES)


def lane_index(rows):
    return lax.broadcasted_iota(jnp.int32, (rows, LANES), 1)


def swap_slots(parts):
    lane = lane_index(parts[0].shape[0])
    low = lane < 64
    even = (lane // 32) % 2 == 0
    turned = [pltpu.roll(part, 64, 1) for part in parts]
    first = [
        jnp.where(low, parts[0], turned[2]),
        jnp.where(low, parts[1], turned[3]),
        jnp.where(low, turned[0], parts[2]),
        jnp.where(low, turned[1], parts[3]),
    ]
    result = []
    for base in (0, 2):
        result.append(jnp.where(even, first[base], pltpu.roll(first[base + 1], 32, 1)))
        result.append(jnp.where(even, pltpu.roll(first[base], 96, 1), first[base + 1]))
    return result


def as_column(gain_ref, layer):
    return jnp.broadcast_to(gain_ref[pl.ds(layer, 1), :], (LANES, LANES)).T


def standardize(values):
    average = jnp.mean(values, axis=0, keepdims=True)
    centered = values - average
    variance = jnp.mean(centered * centered, axis=0, keepdims=True)
    scale = lax.rsqrt(variance + 1e-05)
    return centered * scale, scale


def standardize_back(d_unit, unit, scale):
    mean_d = jnp.mean(d_unit, axis=0, keepdims=True)
    mean_du = jnp.mean(d_unit * unit, axis=0, keepdims=True)
    return scale * (d_unit - mean_d - unit * mean_du)


def pairs_to_lanes(pairs_ref, spare):
    spare[...] = pairs_ref[...].astype(F32).reshape(PLACE, C)
    tiles = []
    for t in range(TILES):
        block = jnp.concatenate(
            [spare[pl.ds(4 * t + q, ROWS, COLS), :] for q in range(4)], axis=0
        )
        tiles.append(block.T)
    return tiles


def lanes_to_pairs(tiles, pairs_ref, spare):
    for t in range(TILES):
        block = tiles[t].T
        for q in range(4):
            spare[pl.ds(4 * t + q, ROWS, COLS), :] = block[q * ROWS : (q + 1) * ROWS, :]
    pairs_ref[...] = spare[...].reshape(ROWS, COLS, C).astype(pairs_ref.dtype)


def put_operands(t, left, right, spare):
    low = lane_index(C) < 64
    spare[pl.ds(2 * t, C, 8), :] = jnp.where(low, left, pltpu.roll(right, 64, 1))
    spare[pl.ds(2 * t + 1, C, 8), :] = jnp.where(low, pltpu.roll(left, 64, 1), right)


def get_operands(t, spare):
    low = lane_index(C) < 64
    even = spare[pl.ds(2 * t, C, 8), :]
    odd = spare[pl.ds(2 * t + 1, C, 8), :]
    left = jnp.where(low, even, pltpu.roll(odd, 64, 1))
    right = jnp.where(low, pltpu.roll(even, 64, 1), odd)
    return left, right


def project_tile(values, gain, proj_ref, gate_ref, layer):
    unit, scale = standardize(values)
    normed = (unit * gain).astype(BF16)
    projected = mm(proj_ref[layer], normed, 0, 0)
    gating = jax.nn.sigmoid(mm(gate_ref[layer], normed, 0, 0))
    return unit, scale, normed, projected, gating


def send_front(t, projected, spare):
    left = jax.nn.sigmoid(projected[0:C]) * projected[C : 2 * C]
    right = jax.nn.sigmoid(projected[2 * C : 3 * C]) * projected[3 * C :]
    put_operands(t, left, right, spare)


def first_kernel(pair_ref, gain_in, proj, gate, send_ref, x_ref, gating_ref, spare, pairs):
    gain = as_column(gain_in, 0)
    tiles = pairs_to_lanes(pair_ref, pairs)
    for t in range(TILES):
        _, _, _, projected, gating = project_tile(tiles[t], gain, proj, gate, 0)
        x_ref[:, tile(t)] = tiles[t].astype(BF16)
        gating_ref[:, tile(t)] = gating
        send_front(t, projected, spare)
    send_ref[...] = spare[...].astype(BF16)


def middle_kernel(
    mix_ref, x_ref, gating_ref, gain_in, proj, gate, gain_mid, out_w,
    send_ref, next_ref, next_gating_ref, spare, mixed,
):
    mixed[...] = mix_ref[...].astype(F32)
    gain_a = as_column(gain_mid, 0)
    gain_b = as_column(gain_in, 1)
    for t in range(TILES):
        unit, _ = standardize(mixed[pl.ds(t, C, TILES), :])
        update = mm(out_w[0], unit * gain_a, 0, 0)
        rounded = (x_ref[:, tile(t)].astype(F32) + update * gating_ref[:, tile(t)]).astype(BF16)
        next_ref[:, tile(t)] = rounded
        _, _, _, projected, gating = project_tile(rounded.astype(F32), gain_b, proj, gate, 1)
        next_gating_ref[:, tile(t)] = gating
        send_front(t, projected, spare)
    send_ref[...] = spare[...].astype(BF16)


def finish_back(grad, gating, unit, scale, update, gain, out_w, layer):
    d_update = grad * gating
    d_gate_pre = grad * update * gating * (1.0 - gating)
    d_normed = mm(out_w[layer], d_update, 1, 0)
    d_mix = standardize_back(d_normed * gain, unit, scale)
    d_gain = jnp.sum(d_normed * unit, axis=1, keepdims=True)
    return d_update, d_gate_pre, d_mix, d_gain


def split_two(values):
    high = values.astype(BF16).astype(F32)
    return high, values - high


def turn_kernel(
    mix_ref, x_ref, gating_ref, cot_ref, gain_mid, out_w,
    pair_out_ref, send_ref, grad_ref, gate_pre_ref, spare, mixed, pairs, kept_n, kept_d,
):
    mixed[...] = mix_ref[...].astype(F32)
    gain = as_column(gain_mid, 1)
    cot = pairs_to_lanes(cot_ref, pairs)
    outs = []
    total_gain = jnp.zeros((C, 1), F32)
    for t in range(TILES):
        unit, scale = standardize(mixed[pl.ds(t, C, TILES), :])
        normed = (unit * gain).astype(BF16)
        update = mm(out_w[1], normed, 0, 0)
        gating = gating_ref[:, tile(t)]
        outs.append(x_ref[:, tile(t)].astype(F32) + update * gating)
        d_update, d_gate_pre, d_mix, d_gain = finish_back(
            cot[t], gating, unit, scale, update, gain, out_w, 1
        )
        grad_ref[:, tile(t)] = cot[t].astype(BF16)
        gate_pre_ref[:, tile(t)] = d_gate_pre.astype(BF16)
        kept_n[:, tile(t)] = normed
        kept_d[:, tile(t)] = d_update.astype(BF16)
        total_gain = total_gain + d_gain
        spare[pl.ds(t, C, 8), :] = d_mix
    spare[pl.ds(4, C, 8), :] = mm(kept_n[...], kept_d[...], 1, 1)
    high, low = split_two(total_gain)
    spare[pl.ds(5, C, 8), :] = jnp.broadcast_to(high, (C, LANES))
    spare[pl.ds(6, C, 8), :] = jnp.broadcast_to(low, (C, LANES))
    spare[pl.ds(7, C, 8), :] = jnp.zeros((C, LANES), F32)
    send_ref[...] = spare[...].astype(BF16)
    lanes_to_pairs(outs, pair_out_ref, pairs)


def front_back_tile(t, x_ref, gate_pre_ref, spare, gain, proj, gate, layer, kept_n, kept_p):
    unit, scale = standardize(x_ref[:, tile(t)].astype(F32))
    normed = (unit * gain).astype(BF16)
    projected = mm(proj[layer], normed, 0, 0)
    d_left, d_right = get_operands(t, spare)
    parts = []
    for base, d_out in ((0, d_left), (2, d_right)):
        opened = jax.nn.sigmoid(projected[base * C : (base + 1) * C])
        value = projected[(base + 1) * C : (base + 2) * C]
        d_value = d_out * opened
        parts.append((d_value * value * (1.0 - opened)).astype(BF16))
        parts.append(d_value.astype(BF16))
    parts.append(gate_pre_ref[:, tile(t)])
    d_projected = jnp.concatenate(parts[:4], axis=0)
    d_normed = mm(proj[layer], d_projected, 1, 0) + mm(gate[layer], parts[4], 1, 0)
    kept_n[:, tile(t)] = normed
    kept_p[:, tile(t)] = jnp.concatenate(parts, axis=0)
    d_gain = jnp.sum(d_normed * unit, axis=1, keepdims=True)
    return standardize_back(d_normed * gain, unit, scale), d_gain


def slot_lanes(columns):
    lane = lane_index(C)
    result = jnp.zeros((C, LANES), F32)
    for slot, column in enumerate(columns):
        high, low = split_two(column)
        result = jnp.where(lane // 16 == 2 * slot, high, result)
        result = jnp.where(lane // 16 == 2 * slot + 1, low, result)
    return result


def both_back_kernel(
    recv_ref, x_ref, grad_ref, gate_pre_ref, mix_ref, gating_ref,
    gain_in, proj, gate, gain_mid, out_w,
    send_ref, next_grad_ref, next_pre_ref, keep_ref,
    spare, mixed, kept_n, kept_p, kept_m, kept_d,
):
    spare[...] = recv_ref[...].astype(F32)
    mixed[...] = mix_ref[...].astype(F32)
    gain_a = as_column(gain_in, 1)
    gain_b = as_column(gain_mid, 0)
    total_in = jnp.zeros((C, 1), F32)
    total_mid = jnp.zeros((C, 1), F32)
    sent = []
    for t in range(TILES):
        d_x, d_gain = front_back_tile(
            t, x_ref, gate_pre_ref, spare, gain_a, proj, gate, 1, kept_n, kept_p
        )
        total_in = total_in + d_gain
        grad = grad_ref[:, tile(t)].astype(F32) + d_x
        next_grad_ref[:, tile(t)] = grad
        unit, scale = standardize(mixed[pl.ds(t, C, TILES), :])
        normed = (unit * gain_b).astype(BF16)
        update = mm(out_w[0], normed, 0, 0)
        d_update, d_gate_pre, d_mix, d_gain = finish_back(
            grad, gating_ref[:, tile(t)], unit, scale, update, gain_b, out_w, 0
        )
        next_pre_ref[:, tile(t)] = d_gate_pre.astype(BF16)
        kept_m[:, tile(t)] = normed
        kept_d[:, tile(t)] = d_update.astype(BF16)
        total_mid = total_mid + d_gain
        sent.append(d_mix)
    for t in range(TILES):
        spare[pl.ds(t, C, 8), :] = sent[t]
    weights = mm(kept_n[...], kept_p[...], 1, 1)
    for e in range(4):
        spare[pl.ds(4 + e, C, 8), :] = weights[:, e * C : (e + 1) * C]
    send_ref[...] = spare[...].astype(BF16)
    keep_ref[0] = mm(kept_m[...], kept_d[...], 1, 1)
    keep_ref[1] = weights[:, 4 * C :]
    keep_ref[2] = jnp.concatenate([total_in, total_mid] + [jnp.zeros((C, 1), F32)] * 126, axis=1)


def last_back_kernel(
    recv_ref, x_ref, grad_ref, gate_pre_ref, keep_ref, gain_in, proj, gate,
    pair_grad_ref, send_ref, spare, pairs, kept_n, kept_p,
):
    spare[...] = recv_ref[...].astype(F32)
    gain = as_column(gain_in, 0)
    total = jnp.zeros((C, 1), F32)
    outs = []
    for t in range(TILES):
        d_x, d_gain = front_back_tile(
            t, x_ref, gate_pre_ref, spare, gain, proj, gate, 0, kept_n, kept_p
        )
        total = total + d_gain
        outs.append(grad_ref[:, tile(t)] + d_x)
    weights = mm(kept_n[...], kept_p[...], 1, 1)
    for e in range(5):
        spare[pl.ds(e, C, 8), :] = weights[:, e * C : (e + 1) * C]
    spare[pl.ds(5, C, 8), :] = keep_ref[0]
    spare[pl.ds(6, C, 8), :] = keep_ref[1]
    gains = keep_ref[2]
    spare[pl.ds(7, C, 8), :] = slot_lanes([total, gains[:, 1:2], gains[:, 0:1]])
    send_ref[...] = spare[...].astype(BF16)
    lanes_to_pairs(outs, pair_grad_ref, pairs)


def pair_mask(tok_ref):
    token = jnp.broadcast_to(tok_ref[...].astype(F32), (8, TOKENS))
    token = jnp.where(lax.broadcasted_iota(jnp.int32, (8, TOKENS), 0) == 0, token, 0.0)
    return mm(token, token, 0, 0)


def whole(spare, first):
    return jnp.concatenate([spare[first], spare[first + 1]], axis=1)


def product_kernel(layer, recv_ref, tok_ref, send_ref, left_ref, right_ref, spare):
    for hi in range(2):
        parts = [
            recv_ref[pl.ds((4 * hi + lo) * LANES, LANES), :].astype(F32) for lo in range(4)
        ]
        for slot, block in enumerate(swap_slots(parts)):
            spare[2 * (slot // 2) + hi, pl.ds(slot % 2, LANES, 2), :] = block
    mask = pair_mask(tok_ref)
    left = (whole(spare, 0) * mask).astype(BF16)
    right = (whole(spare, 2) * mask).astype(BF16)
    left_ref[...] = left
    right_ref[...] = right
    mixture = mm(right, left, layer, layer)
    for hi in range(2):
        spare[hi] = mixture[:, hi * LANES : (hi + 1) * LANES]
    for hi in range(2):
        parts = [spare[hi, pl.ds(q, 64, 4), :] for q in range(4)]
        for lo, block in enumerate(swap_slots(parts)):
            send_ref[pl.ds((4 * hi + lo) * 64, 64), :] = block.astype(BF16)


def product_back_kernel(
    layer, recv_ref, tok_ref, left_ref, right_ref, send_ref, sums_ref, arrived, spare
):
    arrived[...] = recv_ref[...].astype(F32)
    for hi in range(2):
        parts = [
            jnp.concatenate(
                [arrived[pl.ds((4 * hi + lo) * LANES + jm, COLS, 8), :] for jm in range(4)], axis=0
            )
            for lo in range(4)
        ]
        for q, block in enumerate(swap_slots(parts)):
            for jm in range(4):
                spare[hi, pl.ds(4 * jm + q, COLS, COLS), :] = block[jm * COLS : (jm + 1) * COLS, :]
    d_mix = whole(spare, 0).astype(BF16)
    left = left_ref[...]
    right = right_ref[...]
    if layer == 0:
        d_left = mm(right, d_mix, 1, 0)
        d_right = mm(left, d_mix, 1, 1)
    else:
        d_left = mm(d_mix, right, 0, 0)
        d_right = mm(d_mix, left, 1, 0)
    mask = pair_mask(tok_ref)
    for first, value in ((0, d_left * mask), (2, d_right * mask)):
        for hi in range(2):
            spare[first + hi] = value[:, hi * LANES : (hi + 1) * LANES]
    for hi in range(2):
        parts = [spare[2 * (slot // 2) + hi, pl.ds(slot % 2, LANES, 2), :] for slot in range(4)]
        for lo, block in enumerate(swap_slots(parts)):
            send_ref[pl.ds((4 * hi + lo) * LANES, LANES), :] = block.astype(BF16)
    for e in range(4):
        sums_ref[pl.ds(e, 1), :] = jnp.sum(arrived[pl.ds(4 + e, PEERS, 8), :], axis=0, keepdims=True)


def collect_kernel(recv_ref, first_ref, second_ref, send_ref, arrived):
    arrived[...] = recv_ref[...].astype(F32)
    rows = [
        jnp.sum(arrived[pl.ds(e, PEERS, 8), :], axis=0, keepdims=True) for e in range(8)
    ]
    gains = rows[7] + pltpu.roll(rows[7], LANES - 16, 1)
    lane = lane_index(1)
    gains = jnp.where(lane >= 96, first_ref[1:2, :] + first_ref[2:3, :], gains)
    high, low = split_two(gains)
    empty = jnp.zeros((1, LANES), F32)
    block = jnp.concatenate(
        rows[0:4]
        + [second_ref[e : e + 1, :] for e in range(4)]
        + [rows[4], rows[6], rows[5], first_ref[0:1, :], high, low, empty, empty],
        axis=0,
    ).astype(BF16)
    send_ref[...] = jnp.broadcast_to(block[None], (PEERS, 16, LANES)).reshape(PEERS * 16, LANES)


def spread_kernel(recv_ref, gin_ref, proj_ref, gate_ref, gmid_ref, out_ref, arrived):
    share = 1.0 / TOKENS
    arrived[...] = recv_ref[...].astype(F32) * share
    for m in range(2):
        for e in range(4):
            proj_ref[m, :, tile(e)] = arrived[pl.ds(4 * m + e, C, 16), :]
        gate_ref[m] = arrived[pl.ds(8 + m, C, 16), :]
        out_ref[m] = arrived[pl.ds(10 + m, C, 16), :]
    gains = (arrived[pl.ds(12, C, 16), :] + arrived[pl.ds(13, C, 16), :]).T
    gin_ref[...] = jnp.concatenate([gains[0:1], gains[64:65]], axis=0)
    gmid_ref[...] = jnp.concatenate([gains[32:33], gains[96:97]], axis=0)


def run(kernel, outs, scratch, args):
    return pl.pallas_call(
        kernel,
        out_shape=[jax.ShapeDtypeStruct(shape, dtype) for shape, dtype in outs],
        in_specs=[pl.BlockSpec(memory_space=pltpu.VMEM)] * len(args),
        out_specs=[pl.BlockSpec(memory_space=pltpu.VMEM)] * len(outs),
        scratch_shapes=[pltpu.VMEM(shape, dtype) for shape, dtype in scratch],
        compiler_params=pltpu.CompilerParams(vmem_limit_bytes=24 * 1024 * 1024),
    )(*args)


def exchange(values):
    return lax.all_to_all(values, AXES, 0, 0, tiled=True)


def local(pair_in, token_mask, cotangent, gain_in, proj_w, gate_w, gain_mid, out_w):
    tok = token_mask.reshape(1, TOKENS)
    operand = ((PEERS * 8, LANES), BF16)
    single = ((PEERS * 4, LANES), BF16)
    plane = (C, PLACE)
    square = (TOKENS, TOKENS)
    spare = ((PEERS * 8, LANES), F32)
    pairs = ((PLACE, C), F32)
    mixed = ((PEERS * 4, LANES), F32)
    quarter = ((4, TOKENS, LANES), F32)
    kept = (plane, BF16)
    kept_p = ((5 * C, PLACE), BF16)
    pair_shape = (ROWS, COLS, C)

    send, x0, gating0 = run(
        first_kernel, [operand, (plane, BF16), (plane, F32)], [spare, pairs],
        (pair_in, gain_in, proj_w, gate_w),
    )
    send, left0, right0 = run(
        functools.partial(product_kernel, 0), [single, (square, BF16), (square, BF16)], [quarter],
        (exchange(send), tok),
    )
    mix0 = exchange(send)
    send, x1, gating1 = run(
        middle_kernel, [operand, (plane, BF16), (plane, F32)], [spare, mixed],
        (mix0, x0, gating0, gain_in, proj_w, gate_w, gain_mid, out_w),
    )
    send, left1, right1 = run(
        functools.partial(product_kernel, 1), [single, (square, BF16), (square, BF16)], [quarter],
        (exchange(send), tok),
    )
    mix1 = exchange(send)
    pair_out, send, grad1, pre1 = run(
        turn_kernel, [(pair_shape, BF16), operand, (plane, BF16), (plane, BF16)],
        [spare, mixed, pairs, kept, kept],
        (mix1, x1, gating1, cotangent, gain_mid, out_w),
    )
    send, sums1 = run(
        functools.partial(product_back_kernel, 1), [operand, ((4, LANES), F32)], [spare, quarter],
        (exchange(send), tok, left1, right1),
    )
    send, grad0, pre0, keep = run(
        both_back_kernel,
        [operand, (plane, F32), (plane, BF16), ((3, C, LANES), F32)],
        [spare, mixed, kept, kept_p, kept, kept],
        (exchange(send), x1, grad1, pre1, mix0, gating0, gain_in, proj_w, gate_w, gain_mid, out_w),
    )
    send, sums0 = run(
        functools.partial(product_back_kernel, 0), [operand, ((4, LANES), F32)], [spare, quarter],
        (exchange(send), tok, left0, right0),
    )
    pair_grad, send = run(
        last_back_kernel, [(pair_shape, BF16), operand], [spare, pairs, kept, kept_p],
        (exchange(send), x0, grad0, pre0, keep, gain_in, proj_w, gate_w),
    )
    (send,) = run(
        collect_kernel, [((PEERS * 16, LANES), BF16)], [spare], (exchange(send), sums1, sums0)
    )
    gin, proj, gate, gmid, out = run(
        spread_kernel,
        [((2, C), F32), ((2, C, 4 * C), F32), ((2, C, C), F32), ((2, C), F32), ((2, C, C), F32)],
        [((PEERS * 16, LANES), F32)],
        (exchange(send),),
    )
    return pair_out, pair_grad, gin, proj, gate, gmid, out


def solution(mesh):
    placed = (P("row", "col", None), P(), P("row", "col", None), P(), P(), P(), P(), P())
    return jax.shard_map(
        local,
        mesh=mesh,
        in_specs=placed,
        out_specs=(P("row", "col", None), P("row", "col", None), P(), P(), P(), P(), P()),
        check_vma=False,
    )
```

```python
import functools

import jax
import jax.numpy as jnp
from jax import lax
from jax.experimental import pallas as pl
from jax.experimental.pallas import tpu as pltpu
from jax.sharding import PartitionSpec as P

F32 = jnp.float32
BF16 = jnp.bfloat16
C = 128
LANES = 128
ROWS = 32
COLS = 16
TOKENS = 256
PLACE = ROWS * COLS
TILES = PLACE // LANES
PEERS = 128
AXES = ("row", "col")
SUMS = 12


def mm(a, b, a_dim, b_dim):
    return lax.dot_general(
        a.astype(BF16), b.astype(BF16), (((a_dim,), (b_dim,)), ((), ())), preferred_element_type=F32
    )


def tile(t):
    return pl.ds(t * LANES, LANES)


def lane_index(rows):
    return lax.broadcasted_iota(jnp.int32, (rows, LANES), 1)


def swap_slots(parts):
    lane = lane_index(parts[0].shape[0])
    low = lane < 64
    even = (lane // 32) % 2 == 0
    turned = [pltpu.roll(part, 64, 1) for part in parts]
    first = [
        jnp.where(low, parts[0], turned[2]),
        jnp.where(low, parts[1], turned[3]),
        jnp.where(low, turned[0], parts[2]),
        jnp.where(low, turned[1], parts[3]),
    ]
    result = []
    for base in (0, 2):
        result.append(jnp.where(even, first[base], pltpu.roll(first[base + 1], 32, 1)))
        result.append(jnp.where(even, pltpu.roll(first[base], 96, 1), first[base + 1]))
    return result


def as_column(gain_ref, layer):
    return jnp.broadcast_to(gain_ref[pl.ds(layer, 1), :], (LANES, LANES)).T


def as_row(column):
    return jnp.broadcast_to(column, (LANES, LANES)).T[0:1]


def standardize(values):
    average = jnp.mean(values, axis=0, keepdims=True)
    centered = values - average
    variance = jnp.mean(centered * centered, axis=0, keepdims=True)
    scale = lax.rsqrt(variance + 1e-05)
    return centered * scale, scale


def standardize_back(d_unit, unit, scale):
    mean_d = jnp.mean(d_unit, axis=0, keepdims=True)
    mean_du = jnp.mean(d_unit * unit, axis=0, keepdims=True)
    return scale * (d_unit - mean_d - unit * mean_du)


def pairs_to_lanes(pairs_ref, spare):
    spare[...] = pairs_ref[...].astype(F32).reshape(PLACE, C)
    tiles = []
    for t in range(TILES):
        block = jnp.concatenate(
            [spare[pl.ds(4 * t + q, ROWS, COLS), :] for q in range(4)], axis=0
        )
        tiles.append(block.T)
    return tiles


def lanes_to_pairs(tiles, pairs_ref, spare):
    for t in range(TILES):
        block = tiles[t].T
        for q in range(4):
            spare[pl.ds(4 * t + q, ROWS, COLS), :] = block[q * ROWS : (q + 1) * ROWS, :]
    pairs_ref[...] = spare[...].reshape(ROWS, COLS, C).astype(pairs_ref.dtype)


def put_operands(t, left, right, spare):
    low = lane_index(C) < 64
    spare[pl.ds(2 * t, C, 8), :] = jnp.where(low, left, pltpu.roll(right, 64, 1))
    spare[pl.ds(2 * t + 1, C, 8), :] = jnp.where(low, pltpu.roll(left, 64, 1), right)


def get_operands(t, spare):
    low = lane_index(C) < 64
    even = spare[pl.ds(2 * t, C, 8), :]
    odd = spare[pl.ds(2 * t + 1, C, 8), :]
    left = jnp.where(low, even, pltpu.roll(odd, 64, 1))
    right = jnp.where(low, pltpu.roll(even, 64, 1), odd)
    return left, right


def front_tile(t, values, gain, proj, gate, layer, spare, saved):
    unit_ref, scale_ref, normed_ref, fact_ref, gating_ref = saved
    unit, scale = standardize(values)
    normed = (unit * gain).astype(BF16)
    unit_ref[:, tile(t)] = unit
    scale_ref[:, tile(t)] = jnp.broadcast_to(scale, (8, LANES))
    normed_ref[:, tile(t)] = normed
    projected = mm(proj[layer], normed, 0, 0)
    operands = []
    for base in (0, 2):
        opened = jax.nn.sigmoid(projected[base * C : (base + 1) * C])
        value = projected[(base + 1) * C : (base + 2) * C]
        operand = opened * value
        operands.append(operand)
        fact_ref[pl.ds(base * C, C), tile(t)] = operand * (1.0 - opened)
        fact_ref[pl.ds((base + 1) * C, C), tile(t)] = opened
    put_operands(t, operands[0], operands[1], spare)
    gating_ref[:, tile(t)] = jax.nn.sigmoid(mm(gate[layer], normed, 0, 0))


def ready_kernel(ready_ref):
    ready_ref[...] = jnp.zeros((8, LANES), F32)


def first_kernel(
    ready_ref, pair_ref, proj, gate, out_w, gin, gmid, tok,
    send_ref, unit_ref, scale_ref, normed_ref, fact_ref, gating_ref, x_ref,
    proj_out, gate_out, out_out, gin_out, gmid_out, tok_out,
    spare, pairs,
):
    gain = as_column(gin, 0)
    tiles = pairs_to_lanes(pair_ref, pairs)
    saved = (unit_ref, scale_ref, normed_ref, fact_ref, gating_ref)
    for t in range(TILES):
        x_ref[:, tile(t)] = tiles[t].astype(BF16)
        front_tile(t, tiles[t], gain, proj, gate, 0, spare, saved)
    send_ref[...] = spare[...].astype(BF16)
    for given, kept in (
        (proj, proj_out), (gate, gate_out), (out_w, out_out),
        (gin, gin_out), (gmid, gmid_out), (tok, tok_out),
    ):
        kept[...] = given[...]


def middle_kernel(
    mix_ref, x_ref, gating0_ref, gin, gmid, proj, gate, out_w,
    send_ref, unit_ref, scale_ref, normed_ref, fact_ref, gating_ref, next_ref,
    mix_unit_ref, mix_scale_ref, mix_normed_ref, gate_fact_ref, spare, mixed,
):
    mixed[...] = mix_ref[...].astype(F32)
    gain_a = as_column(gmid, 0)
    gain_b = as_column(gin, 1)
    saved = (unit_ref, scale_ref, normed_ref, fact_ref, gating_ref)
    for t in range(TILES):
        unit, scale = standardize(mixed[pl.ds(t, C, TILES), :])
        normed = (unit * gain_a).astype(BF16)
        update = mm(out_w[0], normed, 0, 0)
        gating = gating0_ref[:, tile(t)]
        gated = update * gating
        rounded = (x_ref[:, tile(t)].astype(F32) + gated).astype(BF16)
        next_ref[:, tile(t)] = rounded
        mix_unit_ref[:, tile(t)] = unit
        mix_scale_ref[:, tile(t)] = jnp.broadcast_to(scale, (8, LANES))
        mix_normed_ref[:, tile(t)] = normed
        gate_fact_ref[:, tile(t)] = gated * (1.0 - gating)
        front_tile(t, rounded.astype(F32), gain_b, proj, gate, 1, spare, saved)
    send_ref[...] = spare[...].astype(BF16)


def turn_kernel(
    mix_ref, x_ref, gating_ref, normed_ref, cot_ref, gmid, gate, out_w,
    pair_out_ref, send_ref, grad_ref, d_gated_ref, weights_ref,
    mixed, pairs, kept_n, kept_g, kept_d,
):
    mixed[...] = mix_ref[...].astype(F32)
    gain = as_column(gmid, 1)
    cot = pairs_to_lanes(cot_ref, pairs)
    outs = []
    for t in range(TILES):
        unit, scale = standardize(mixed[pl.ds(t, C, TILES), :])
        normed = (unit * gain).astype(BF16)
        update = mm(out_w[1], normed, 0, 0)
        gating = gating_ref[:, tile(t)]
        d_update = cot[t] * gating
        rounded = d_update.astype(BF16)
        d_unit = mm(out_w[1], rounded, 1, 0) * gain
        mixed[pl.ds(t, C, TILES), :] = standardize_back(d_unit, unit, scale)
        outs.append(x_ref[:, tile(t)].astype(F32) + update * gating)
        gate_pre = (d_update * (1.0 - gating) * update).astype(BF16)
        grad_ref[:, tile(t)] = cot[t]
        kept_n[:, tile(t)] = normed
        kept_d[:, tile(t)] = rounded
        kept_g[:, tile(t)] = gate_pre
        d_gated_ref[:, tile(t)] = mm(gate[1], gate_pre, 1, 0)
    send_ref[...] = mixed[...].astype(BF16)
    weights_ref[0] = mm(normed_ref[...], kept_g[...], 1, 1)
    weights_ref[1] = mm(kept_n[...], kept_d[...], 1, 1)
    lanes_to_pairs(outs, pair_out_ref, pairs)


def projected_back(t, spare, fact_ref, kept_p):
    d_left, d_right = get_operands(t, spare)
    for part, d_out in enumerate((d_left, d_left, d_right, d_right)):
        rows = pl.ds(part * C, C)
        kept_p[rows, tile(t)] = (d_out * fact_ref[rows, tile(t)]).astype(BF16)


def both_back_kernel(
    recv_ref, fact_ref, d_gated1_ref, unit_ref, scale_ref, grad_ref, normed1_ref, weights1_ref,
    gating_ref, mix_unit_ref, mix_scale_ref, mix_normed_ref, gate_fact_ref, normed0_ref,
    gin, gmid, proj, gate, out_w,
    send_ref, next_grad_ref, d_gated_ref, rows_ref,
    spare, mixed, kept_p, kept_g, kept_d,
):
    spare[...] = recv_ref[...].astype(F32)
    gain_a = as_column(gin, 1)
    gain_b = as_column(gmid, 0)
    for t in range(TILES):
        projected_back(t, spare, fact_ref, kept_p)
        d_normed = mm(proj[1], kept_p[:, tile(t)], 1, 0) + d_gated1_ref[:, tile(t)]
        d_x = standardize_back(
            d_normed * gain_a, unit_ref[:, tile(t)], scale_ref[pl.ds(0, 1), tile(t)]
        )
        grad = grad_ref[:, tile(t)] + d_x
        d_update = (grad * gating_ref[:, tile(t)]).astype(BF16)
        next_grad_ref[:, tile(t)] = grad
        kept_d[:, tile(t)] = d_update
        mixed[pl.ds(t, C, TILES), :] = standardize_back(
            mm(out_w[0], d_update, 1, 0) * gain_b,
            mix_unit_ref[:, tile(t)],
            mix_scale_ref[pl.ds(0, 1), tile(t)],
        )
        gate_pre = (grad * gate_fact_ref[:, tile(t)]).astype(BF16)
        kept_g[:, tile(t)] = gate_pre
        d_gated_ref[:, tile(t)] = mm(gate[0], gate_pre, 1, 0)
    send_ref[...] = mixed[...].astype(BF16)
    first = mm(normed1_ref[...], kept_p[...], 1, 1)
    for e in range(4):
        rows_ref[pl.ds(4 + e, C, SUMS), :] = first[:, e * C : (e + 1) * C]
    rows_ref[pl.ds(8, C, SUMS), :] = mm(normed0_ref[...], kept_g[...], 1, 1)
    rows_ref[pl.ds(9, C, SUMS), :] = weights1_ref[0]
    rows_ref[pl.ds(10, C, SUMS), :] = mm(mix_normed_ref[...], kept_d[...], 1, 1)
    rows_ref[pl.ds(11, C, SUMS), :] = weights1_ref[1]


def last_back_kernel(
    recv_ref, fact_ref, normed_ref, rows_ref, d_gated_ref, unit_ref, scale_ref, grad_ref, gin, proj,
    send_ref, pair_grad_ref, spare, rows, kept_p, pairs,
):
    spare[...] = recv_ref[...].astype(F32)
    rows[...] = rows_ref[...]
    gain = as_column(gin, 0)
    outs = []
    for t in range(TILES):
        projected_back(t, spare, fact_ref, kept_p)
        d_normed = mm(proj[0], kept_p[:, tile(t)], 1, 0) + d_gated_ref[:, tile(t)]
        d_x = standardize_back(
            d_normed * gain, unit_ref[:, tile(t)], scale_ref[pl.ds(0, 1), tile(t)]
        )
        outs.append(grad_ref[:, tile(t)] + d_x)
    weights = mm(normed_ref[...], kept_p[...], 1, 1)
    for e in range(4):
        rows[pl.ds(e, C, SUMS), :] = weights[:, e * C : (e + 1) * C]
    send_ref[...] = rows[...].astype(BF16)
    lanes_to_pairs(outs, pair_grad_ref, pairs)


def pair_mask(tok_ref):
    token = jnp.broadcast_to(tok_ref[...].astype(F32), (8, TOKENS))
    token = jnp.where(lax.broadcasted_iota(jnp.int32, (8, TOKENS), 0) == 0, token, 0.0)
    return mm(token, token, 0, 0)


def whole(spare, first):
    return jnp.concatenate([spare[first], spare[first + 1]], axis=1)


def product_kernel(layer, recv_ref, tok_ref, send_ref, left_ref, right_ref, spare):
    for hi in range(2):
        parts = [
            recv_ref[pl.ds((4 * hi + lo) * LANES, LANES), :].astype(F32) for lo in range(4)
        ]
        for slot, block in enumerate(swap_slots(parts)):
            spare[2 * (slot // 2) + hi, pl.ds(slot % 2, LANES, 2), :] = block
    mask = pair_mask(tok_ref)
    left = (whole(spare, 0) * mask).astype(BF16)
    right = (whole(spare, 2) * mask).astype(BF16)
    left_ref[...] = left
    right_ref[...] = right
    mixture = mm(right, left, layer, layer)
    for hi in range(2):
        spare[hi] = mixture[:, hi * LANES : (hi + 1) * LANES]
    for hi in range(2):
        parts = [spare[hi, pl.ds(q, 64, 4), :] for q in range(4)]
        for lo, block in enumerate(swap_slots(parts)):
            send_ref[pl.ds((4 * hi + lo) * 64, 64), :] = block.astype(BF16)


def product_back_kernel(layer, recv_ref, tok_ref, left_ref, right_ref, send_ref, spare):
    for hi in range(2):
        parts = [recv_ref[pl.ds((4 * hi + lo) * 64, 64), :].astype(F32) for lo in range(4)]
        for q, block in enumerate(swap_slots(parts)):
            spare[hi, pl.ds(q, 64, 4), :] = block
    d_mix = whole(spare, 0).astype(BF16)
    left = left_ref[...]
    right = right_ref[...]
    if layer == 0:
        d_left = mm(right, d_mix, 1, 0)
        d_right = mm(left, d_mix, 1, 1)
    else:
        d_left = mm(d_mix, right, 0, 0)
        d_right = mm(d_mix, left, 1, 0)
    mask = pair_mask(tok_ref)
    for first, value in ((0, d_left * mask), (2, d_right * mask)):
        for hi in range(2):
            spare[first + hi] = value[:, hi * LANES : (hi + 1) * LANES]
    for hi in range(2):
        parts = [spare[2 * (slot // 2) + hi, pl.ds(slot % 2, LANES, 2), :] for slot in range(4)]
        for lo, block in enumerate(swap_slots(parts)):
            send_ref[pl.ds((4 * hi + lo) * LANES, LANES), :] = block.astype(BF16)


def collect_kernel(recv_ref, send_ref):
    twice = jnp.sum(recv_ref[...].astype(F32).reshape(PEERS // 2, 2 * SUMS, LANES), axis=0)
    total = twice[0:SUMS] + twice[SUMS:]
    both = jnp.concatenate([total, total], axis=0)
    send_ref[...] = (
        jnp.broadcast_to(both[None], (PEERS // 2, 2 * SUMS, LANES))
        .reshape(PEERS * SUMS, LANES)
        .astype(BF16)
    )


def spread_kernel(
    recv_ref, gin, gmid, proj, gate, out_w,
    gin_ref, proj_ref, gate_ref, gmid_ref, out_ref, rows,
):
    rows[...] = recv_ref[...].astype(F32) * (1.0 / TOKENS)
    for m in range(2):
        gated = rows[pl.ds(8 + m, C, SUMS), :]
        mixed = rows[pl.ds(10 + m, C, SUMS), :]
        gate_ref[m] = gated
        out_ref[m] = mixed
        total = gated * gate[m].astype(F32)
        for e in range(4):
            part = rows[pl.ds(4 * m + e, C, SUMS), :]
            proj_ref[m, :, tile(e)] = part
            total = total + part * proj[m, :, tile(e)].astype(F32)
        total_in = as_row(jnp.sum(total, axis=1, keepdims=True))
        total_mid = as_row(jnp.sum(mixed * out_w[m].astype(F32), axis=1, keepdims=True))
        gin_ref[pl.ds(m, 1), :] = total_in / gin[pl.ds(m, 1), :]
        gmid_ref[pl.ds(m, 1), :] = total_mid / gmid[pl.ds(m, 1), :]


def run(kernel, outs, scratch, args):
    return pl.pallas_call(
        kernel,
        out_shape=[jax.ShapeDtypeStruct(shape, dtype) for shape, dtype in outs],
        in_specs=[pl.BlockSpec(memory_space=pltpu.VMEM)] * len(args),
        out_specs=[pl.BlockSpec(memory_space=pltpu.VMEM)] * len(outs),
        scratch_shapes=[pltpu.VMEM(shape, dtype) for shape, dtype in scratch],
        compiler_params=pltpu.CompilerParams(vmem_limit_bytes=16 * 1024 * 1024),
        cost_estimate=pl.CostEstimate(flops=10**9, bytes_accessed=2**20, transcendentals=2**18),
    )(*args)


def exchange(values, rows):
    return lax.all_to_all(
        values.reshape(-1, rows, LANES), AXES, 0, 0, tiled=True
    ).reshape(values.shape)


def local(pair_in, token_mask, cotangent, gain_in, proj_w, gate_w, gain_mid, out_w):
    operand = ((PEERS * 8, LANES), BF16)
    single = ((PEERS * 4, LANES), BF16)
    sums = (PEERS * SUMS, LANES)
    plane = ((C, PLACE), F32)
    plane_b = ((C, PLACE), BF16)
    four = (4 * C, PLACE)
    scales = ((8, PLACE), F32)
    square = ((TOKENS, TOKENS), BF16)
    spare = ((PEERS * 8, LANES), F32)
    pairs = ((PLACE, C), F32)
    mixed = ((PEERS * 4, LANES), F32)
    quarter = ((4, TOKENS, LANES), F32)
    pair_shape = ((ROWS, COLS, C), BF16)
    tok_in = token_mask.reshape(1, TOKENS)

    saved = [plane, scales, plane_b, (four, F32), plane, plane_b]
    (ready,) = run(ready_kernel, [((8, LANES), F32)], [], ())
    send, unit0, scale0, normed0, fact0, gating0, x0, proj, gate, out, gin, gmid, tok = run(
        first_kernel,
        [operand]
        + saved
        + [(a.shape, a.dtype) for a in (proj_w, gate_w, out_w, gain_in, gain_mid, tok_in)],
        [spare, pairs],
        (ready, pair_in, proj_w, gate_w, out_w, gain_in, gain_mid, tok_in),
    )
    send, left0, right0 = run(
        functools.partial(product_kernel, 0), [single, square, square], [quarter],
        (exchange(send, 8), tok),
    )
    (
        send, unit1, scale1, normed1, fact1, gating1, x1,
        mix_unit0, mix_scale0, mix_normed0, gate_fact0,
    ) = run(
        middle_kernel, [operand] + saved + [plane, scales, plane_b, plane], [spare, mixed],
        (exchange(send, 4), x0, gating0, gin, gmid, proj, gate, out),
    )
    send, left1, right1 = run(
        functools.partial(product_kernel, 1), [single, square, square], [quarter],
        (exchange(send, 8), tok),
    )
    pair_out, send, grad1, d_gated1, weights1 = run(
        turn_kernel, [pair_shape, single, plane, plane, ((2, C, C), F32)],
        [mixed, pairs, plane_b, plane_b, plane_b],
        (exchange(send, 4), x1, gating1, normed1, cotangent, gmid, gate, out),
    )
    (send,) = run(
        functools.partial(product_back_kernel, 1), [operand], [quarter],
        (exchange(send, 4), tok, left1, right1),
    )
    send, grad0, d_gated0, rows = run(
        both_back_kernel, [single, plane, plane, (sums, F32)],
        [spare, mixed, (four, BF16), plane_b, plane_b],
        (
            exchange(send, 8), fact1, d_gated1, unit1, scale1, grad1, normed1, weights1,
            gating0, mix_unit0, mix_scale0, mix_normed0, gate_fact0, normed0,
            gin, gmid, proj, gate, out,
        ),
    )
    (send,) = run(
        functools.partial(product_back_kernel, 0), [operand], [quarter],
        (exchange(send, 4), tok, left0, right0),
    )
    send, pair_grad = run(
        last_back_kernel, [(sums, BF16), pair_shape], [spare, (sums, F32), (four, BF16), pairs],
        (exchange(send, 8), fact0, normed0, rows, d_gated0, unit0, scale0, grad0, gin, proj),
    )
    (send,) = run(collect_kernel, [(sums, BF16)], [], (exchange(send, 4),))
    gin_grad, proj_grad, gate_grad, gmid_grad, out_grad = run(
        spread_kernel,
        [(a.shape, F32) for a in (gain_in, proj_w, gate_w, gain_mid, out_w)],
        [(sums, F32)],
        (exchange(send, 4), gin, gmid, proj, gate, out),
    )
    return pair_out, pair_grad, gin_grad, proj_grad, gate_grad, gmid_grad, out_grad


def solution(mesh):
    placed = (P("row", "col", None), P(), P("row", "col", None), P(), P(), P(), P(), P())
    return jax.shard_map(
        local,
        mesh=mesh,
        in_specs=placed,
        out_specs=(P("row", "col", None), P("row", "col", None), P(), P(), P(), P(), P()),
        check_vma=False,
    )
```

```python
import functools

import jax
import jax.numpy as jnp
from jax import lax
from jax.experimental import pallas as pl
from jax.experimental.pallas import tpu as pltpu
from jax.sharding import PartitionSpec as P

F32 = jnp.float32
BF16 = jnp.bfloat16
C = 128
LANES = 128
ROWS = 32
COLS = 16
TOKENS = 256
PLACE = ROWS * COLS
TILES = PLACE // LANES
PEERS = 128
AXES = ("row", "col")
SUMS = 12


def mm(a, b, a_dim, b_dim):
    return lax.dot_general(
        a.astype(BF16), b.astype(BF16), (((a_dim,), (b_dim,)), ((), ())), preferred_element_type=F32
    )


def tile(t):
    return pl.ds(t * LANES, LANES)


def lane_index(rows):
    return lax.broadcasted_iota(jnp.int32, (rows, LANES), 1)


def swap_slots(parts):
    lane = lane_index(parts[0].shape[0])
    low = lane < 64
    even = (lane // 32) % 2 == 0
    turned = [pltpu.roll(part, 64, 1) for part in parts]
    first = [
        jnp.where(low, parts[0], turned[2]),
        jnp.where(low, parts[1], turned[3]),
        jnp.where(low, turned[0], parts[2]),
        jnp.where(low, turned[1], parts[3]),
    ]
    result = []
    for base in (0, 2):
        result.append(jnp.where(even, first[base], pltpu.roll(first[base + 1], 32, 1)))
        result.append(jnp.where(even, pltpu.roll(first[base], 96, 1), first[base + 1]))
    return result


def as_column(gain_ref, layer):
    return jnp.broadcast_to(gain_ref[pl.ds(layer, 1), :], (LANES, LANES)).T


def as_row(column):
    return jnp.broadcast_to(column, (LANES, LANES)).T[0:1]


def standardize(values):
    average = jnp.mean(values, axis=0, keepdims=True)
    centered = values - average
    variance = jnp.mean(centered * centered, axis=0, keepdims=True)
    scale = lax.rsqrt(variance + 1e-05)
    return centered * scale, scale


def standardize_back(d_unit, unit, scale):
    mean_d = jnp.mean(d_unit, axis=0, keepdims=True)
    mean_du = jnp.mean(d_unit * unit, axis=0, keepdims=True)
    return scale * (d_unit - mean_d - unit * mean_du)


def pairs_to_lanes(pairs_ref, spare):
    spare[...] = pairs_ref[...].astype(F32).reshape(PLACE, C)
    tiles = []
    for t in range(TILES):
        block = jnp.concatenate(
            [spare[pl.ds(4 * t + q, ROWS, COLS), :] for q in range(4)], axis=0
        )
        tiles.append(block.T)
    return tiles


def lanes_to_pairs(tiles, pairs_ref, spare):
    for t in range(TILES):
        block = tiles[t].T
        for q in range(4):
            spare[pl.ds(4 * t + q, ROWS, COLS), :] = block[q * ROWS : (q + 1) * ROWS, :]
    pairs_ref[...] = spare[...].reshape(ROWS, COLS, C).astype(pairs_ref.dtype)


def put_operands(t, left, right, spare):
    low = lane_index(C) < 64
    spare[pl.ds(2 * t, C, 8), :] = jnp.where(low, left, pltpu.roll(right, 64, 1))
    spare[pl.ds(2 * t + 1, C, 8), :] = jnp.where(low, pltpu.roll(left, 64, 1), right)


def get_operands(t, spare):
    low = lane_index(C) < 64
    even = spare[pl.ds(2 * t, C, 8), :]
    odd = spare[pl.ds(2 * t + 1, C, 8), :]
    left = jnp.where(low, even, pltpu.roll(odd, 64, 1))
    right = jnp.where(low, pltpu.roll(even, 64, 1), odd)
    return left, right


def front(tiles, gain, proj_t, gate_t, layer, spare, saved):
    unit_ref, scale_ref, normed_ref, fact_ref, gating_ref = saved
    for t, values in enumerate(tiles):
        unit, scale = standardize(values)
        unit_ref[:, tile(t)] = unit
        scale_ref[:, tile(t)] = jnp.broadcast_to(scale, (8, LANES))
        normed_ref[:, tile(t)] = (unit * gain).astype(BF16)
    normed = normed_ref[...]
    parts = []
    for base in (0, 2):
        closed = mm(proj_t[layer, pl.ds(base * C, C), :], normed, 1, 0)
        value = mm(proj_t[layer, pl.ds((base + 1) * C, C), :], normed, 1, 0)
        opened = jax.nn.sigmoid(closed)
        operand = opened * value
        fact_ref[pl.ds(base * C, C), :] = operand * (1.0 - opened)
        fact_ref[pl.ds((base + 1) * C, C), :] = opened
        parts.append(operand)
    for t in range(TILES):
        left, right = (part[:, t * LANES : (t + 1) * LANES] for part in parts)
        put_operands(t, left, right, spare)
    gating_ref[...] = jax.nn.sigmoid(mm(gate_t[layer], normed, 1, 0))


def ready_kernel(ready_ref):
    ready_ref[...] = jnp.zeros((8, LANES), F32)


def first_kernel(
    ready_ref, pair_ref, proj, gate, out_w, gin, gmid, tok,
    send_ref, unit_ref, scale_ref, normed_ref, fact_ref, gating_ref, x_ref,
    proj_out, gate_out, out_out, gin_out, gmid_out, tok_out, proj_t, gate_t, out_t,
    spare, pairs,
):
    for m in range(2):
        proj_t[m] = proj[m].T
        gate_t[m] = gate[m].T
        out_t[m] = out_w[m].T
    gain = as_column(gin, 0)
    tiles = pairs_to_lanes(pair_ref, pairs)
    saved = (unit_ref, scale_ref, normed_ref, fact_ref, gating_ref)
    for t in range(TILES):
        x_ref[:, tile(t)] = tiles[t].astype(BF16)
    front(tiles, gain, proj_t, gate_t, 0, spare, saved)
    send_ref[...] = spare[...].astype(BF16)
    for given, kept in (
        (proj, proj_out), (gate, gate_out), (out_w, out_out),
        (gin, gin_out), (gmid, gmid_out), (tok, tok_out),
    ):
        kept[...] = given[...]


def middle_kernel(
    mix_ref, x_ref, gating0_ref, gin, gmid, proj_t, gate_t, out_t,
    send_ref, unit_ref, scale_ref, normed_ref, fact_ref, gating_ref, next_ref,
    mix_unit_ref, mix_scale_ref, mix_normed_ref, gate_fact_ref, spare, mixed,
):
    mixed[...] = mix_ref[...].astype(F32)
    gain_a = as_column(gmid, 0)
    gain_b = as_column(gin, 1)
    saved = (unit_ref, scale_ref, normed_ref, fact_ref, gating_ref)
    for t in range(TILES):
        unit, scale = standardize(mixed[pl.ds(t, C, TILES), :])
        mix_unit_ref[:, tile(t)] = unit
        mix_scale_ref[:, tile(t)] = jnp.broadcast_to(scale, (8, LANES))
        mix_normed_ref[:, tile(t)] = (unit * gain_a).astype(BF16)
    update = mm(out_t[0], mix_normed_ref[...], 1, 0)
    tiles = []
    for t in range(TILES):
        gating = gating0_ref[:, tile(t)]
        gated = update[:, t * LANES : (t + 1) * LANES] * gating
        rounded = (x_ref[:, tile(t)].astype(F32) + gated).astype(BF16)
        next_ref[:, tile(t)] = rounded
        gate_fact_ref[:, tile(t)] = gated * (1.0 - gating)
        tiles.append(rounded.astype(F32))
    front(tiles, gain_b, proj_t, gate_t, 1, spare, saved)
    send_ref[...] = spare[...].astype(BF16)


def turn_kernel(
    mix_ref, x_ref, gating_ref, normed_ref, cot_ref, gmid, gate, out_w, out_t,
    pair_out_ref, send_ref, grad_ref, d_gated_ref, weights_ref,
    mixed, pairs, kept_n, kept_g, kept_d,
):
    mixed[...] = mix_ref[...].astype(F32)
    gain = as_column(gmid, 1)
    cot = pairs_to_lanes(cot_ref, pairs)
    units = []
    for t in range(TILES):
        units.append(standardize(mixed[pl.ds(t, C, TILES), :]))
        kept_n[:, tile(t)] = (units[t][0] * gain).astype(BF16)
        grad_ref[:, tile(t)] = cot[t]
        kept_d[:, tile(t)] = (cot[t] * gating_ref[:, tile(t)]).astype(BF16)
    d_normed = mm(out_w[1], kept_d[...], 1, 0)
    update = mm(out_t[1], kept_n[...], 1, 0)
    outs = []
    for t in range(TILES):
        piece = slice(t * LANES, (t + 1) * LANES)
        mixed[pl.ds(t, C, TILES), :] = standardize_back(d_normed[:, piece] * gain, *units[t])
        gating = gating_ref[:, tile(t)]
        gated = update[:, piece] * gating
        outs.append(x_ref[:, tile(t)].astype(F32) + gated)
        kept_g[:, tile(t)] = (cot[t] * gated * (1.0 - gating)).astype(BF16)
    d_gated_ref[...] = mm(gate[1], kept_g[...], 1, 0)
    send_ref[...] = mixed[...].astype(BF16)
    weights_ref[0] = mm(normed_ref[...], kept_g[...], 1, 1)
    weights_ref[1] = mm(kept_n[...], kept_d[...], 1, 1)
    lanes_to_pairs(outs, pair_out_ref, pairs)


def projected_back(t, spare, fact_ref, kept_p):
    d_left, d_right = get_operands(t, spare)
    for part, d_out in enumerate((d_left, d_left, d_right, d_right)):
        rows = pl.ds(part * C, C)
        kept_p[rows, tile(t)] = (d_out * fact_ref[rows, tile(t)]).astype(BF16)


def both_back_kernel(
    recv_ref, fact_ref, d_gated1_ref, unit_ref, scale_ref, grad_ref, normed1_ref, weights1_ref,
    gating_ref, mix_unit_ref, mix_scale_ref, mix_normed_ref, gate_fact_ref, normed0_ref,
    gin, gmid, proj, gate, out_w, ready_ref,
    send_ref, next_grad_ref, d_gated_ref, rows_ref, given_ref,
    spare, mixed, kept_p, kept_g, kept_d, sem,
):
    copy = pltpu.make_async_copy(ready_ref, given_ref, sem)
    copy.start()
    spare[...] = recv_ref[...].astype(F32)
    gain_a = as_column(gin, 1)
    gain_b = as_column(gmid, 0)
    for t in range(TILES):
        projected_back(t, spare, fact_ref, kept_p)
    d_normed = mm(proj[1], kept_p[...], 1, 0) + d_gated1_ref[...]
    for t in range(TILES):
        piece = slice(t * LANES, (t + 1) * LANES)
        d_x = standardize_back(
            d_normed[:, piece] * gain_a, unit_ref[:, tile(t)], scale_ref[pl.ds(0, 1), tile(t)]
        )
        grad = grad_ref[:, tile(t)] + d_x
        next_grad_ref[:, tile(t)] = grad
        kept_d[:, tile(t)] = (grad * gating_ref[:, tile(t)]).astype(BF16)
        kept_g[:, tile(t)] = (grad * gate_fact_ref[:, tile(t)]).astype(BF16)
    d_normed = mm(out_w[0], kept_d[...], 1, 0)
    for t in range(TILES):
        piece = slice(t * LANES, (t + 1) * LANES)
        mixed[pl.ds(t, C, TILES), :] = standardize_back(
            d_normed[:, piece] * gain_b,
            mix_unit_ref[:, tile(t)],
            mix_scale_ref[pl.ds(0, 1), tile(t)],
        )
    d_gated_ref[...] = mm(gate[0], kept_g[...], 1, 0)
    send_ref[...] = mixed[...].astype(BF16)
    first = mm(normed1_ref[...], kept_p[...], 1, 1)
    for e in range(4):
        rows_ref[pl.ds(4 + e, C, SUMS), :] = first[:, e * C : (e + 1) * C]
    rows_ref[pl.ds(8, C, SUMS), :] = mm(normed0_ref[...], kept_g[...], 1, 1)
    rows_ref[pl.ds(9, C, SUMS), :] = weights1_ref[0]
    rows_ref[pl.ds(10, C, SUMS), :] = mm(mix_normed_ref[...], kept_d[...], 1, 1)
    rows_ref[pl.ds(11, C, SUMS), :] = weights1_ref[1]
    copy.wait()


def last_back_kernel(
    recv_ref, fact_ref, normed_ref, rows_ref, d_gated_ref, unit_ref, scale_ref, grad_ref, gin, proj,
    send_ref, pair_grad_ref, spare, rows, kept_p, pairs,
):
    spare[...] = recv_ref[...].astype(F32)
    rows[...] = rows_ref[...]
    gain = as_column(gin, 0)
    outs = []
    for t in range(TILES):
        projected_back(t, spare, fact_ref, kept_p)
    d_normed = mm(proj[0], kept_p[...], 1, 0) + d_gated_ref[...]
    for t in range(TILES):
        d_x = standardize_back(
            d_normed[:, t * LANES : (t + 1) * LANES] * gain,
            unit_ref[:, tile(t)],
            scale_ref[pl.ds(0, 1), tile(t)],
        )
        outs.append(grad_ref[:, tile(t)] + d_x)
    weights = mm(normed_ref[...], kept_p[...], 1, 1)
    for e in range(4):
        rows[pl.ds(e, C, SUMS), :] = weights[:, e * C : (e + 1) * C]
    send_ref[...] = rows[...].astype(BF16)
    lanes_to_pairs(outs, pair_grad_ref, pairs)


def pair_mask(tok_ref):
    token = jnp.broadcast_to(tok_ref[...].astype(F32), (8, TOKENS))
    token = jnp.where(lax.broadcasted_iota(jnp.int32, (8, TOKENS), 0) == 0, token, 0.0)
    return mm(token, token, 0, 0)


def whole(spare, first):
    return jnp.concatenate([spare[first], spare[first + 1]], axis=1)


def product_kernel(layer, recv_ref, tok_ref, send_ref, left_ref, right_ref, spare):
    for hi in range(2):
        parts = [
            recv_ref[pl.ds((4 * hi + lo) * LANES, LANES), :].astype(F32) for lo in range(4)
        ]
        for slot, block in enumerate(swap_slots(parts)):
            spare[2 * (slot // 2) + hi, pl.ds(slot % 2, LANES, 2), :] = block
    mask = pair_mask(tok_ref)
    left = (whole(spare, 0) * mask).astype(BF16)
    right = (whole(spare, 2) * mask).astype(BF16)
    left_ref[...] = left
    right_ref[...] = right
    mixture = mm(right, left, layer, layer)
    for hi in range(2):
        spare[hi] = mixture[:, hi * LANES : (hi + 1) * LANES]
    for hi in range(2):
        parts = [spare[hi, pl.ds(q, 64, 4), :] for q in range(4)]
        for lo, block in enumerate(swap_slots(parts)):
            send_ref[pl.ds((4 * hi + lo) * 64, 64), :] = block.astype(BF16)


def product_back_kernel(
    layer, recv_ref, tok_ref, left_ref, right_ref, send_ref, spare
):
    for hi in range(2):
        parts = [recv_ref[pl.ds((4 * hi + lo) * 64, 64), :].astype(F32) for lo in range(4)]
        for q, block in enumerate(swap_slots(parts)):
            spare[hi, pl.ds(q, 64, 4), :] = block
    d_mix = whole(spare, 0).astype(BF16)
    left = left_ref[...]
    right = right_ref[...]
    if layer == 0:
        d_left = mm(right, d_mix, 1, 0)
        d_right = mm(left, d_mix, 1, 1)
    else:
        d_left = mm(d_mix, right, 0, 0)
        d_right = mm(d_mix, left, 1, 0)
    mask = pair_mask(tok_ref)
    for first, value in ((0, d_left * mask), (2, d_right * mask)):
        for hi in range(2):
            spare[first + hi] = value[:, hi * LANES : (hi + 1) * LANES]
    for hi in range(2):
        parts = [spare[2 * (slot // 2) + hi, pl.ds(slot % 2, LANES, 2), :] for slot in range(4)]
        for lo, block in enumerate(swap_slots(parts)):
            send_ref[pl.ds((4 * hi + lo) * LANES, LANES), :] = block.astype(BF16)


def collect_kernel(recv_ref, send_ref):
    twice = jnp.sum(recv_ref[...].astype(F32).reshape(PEERS // 2, 2 * SUMS, LANES), axis=0)
    total = twice[0:SUMS] + twice[SUMS:]
    both = jnp.concatenate([total, total], axis=0)
    send_ref[...] = (
        jnp.broadcast_to(both[None], (PEERS // 2, 2 * SUMS, LANES))
        .reshape(PEERS * SUMS, LANES)
        .astype(BF16)
    )


def spread_kernel(
    recv_ref, ready_ref, gin, gmid, proj, gate, out_w,
    given_ref, gin_ref, proj_ref, gate_ref, gmid_ref, out_ref,
    rows, gin_own, proj_own, gate_own, gmid_own, out_own, sems,
):
    copies = [pltpu.make_async_copy(ready_ref, given_ref, sems.at[0])]
    copies[0].start()

    def give(own, ref):
        copies.append(pltpu.make_async_copy(own, ref, sems.at[len(copies)]))
        copies[-1].start()

    rows[...] = recv_ref[...].astype(F32) * (1.0 / TOKENS)
    for m in range(2):
        for e in range(4):
            proj_own[m, :, tile(e)] = rows[pl.ds(4 * m + e, C, SUMS), :]
        give(proj_own.at[m], proj_ref.at[m])
        gate_own[m] = rows[pl.ds(8 + m, C, SUMS), :]
        give(gate_own.at[m], gate_ref.at[m])
        out_own[m] = rows[pl.ds(10 + m, C, SUMS), :]
        give(out_own.at[m], out_ref.at[m])
    for m in range(2):
        total = gate_own[m] * gate[m].astype(F32)
        for e in range(4):
            total = total + proj_own[m, :, tile(e)] * proj[m, :, tile(e)].astype(F32)
        total_in = as_row(jnp.sum(total, axis=1, keepdims=True))
        total_mid = as_row(jnp.sum(out_own[m] * out_w[m].astype(F32), axis=1, keepdims=True))
        gin_own[pl.ds(m, 1), :] = total_in / gin[pl.ds(m, 1), :]
        gmid_own[pl.ds(m, 1), :] = total_mid / gmid[pl.ds(m, 1), :]
    give(gin_own, gin_ref)
    give(gmid_own, gmid_ref)
    for copy in copies:
        copy.wait()


def run(kernel, outs, scratch, args, away=()):
    spaces = [pl.ANY if k in away else pltpu.VMEM for k in range(len(outs))]
    return pl.pallas_call(
        kernel,
        out_shape=[jax.ShapeDtypeStruct(shape, dtype) for shape, dtype in outs],
        in_specs=[pl.BlockSpec(memory_space=pltpu.VMEM)] * len(args),
        out_specs=[pl.BlockSpec(memory_space=space) for space in spaces],
        scratch_shapes=[
            pltpu.VMEM(shape, dtype) if shape else pltpu.SemaphoreType.DMA(dtype)
            for shape, dtype in scratch
        ],
        compiler_params=pltpu.CompilerParams(vmem_limit_bytes=16 * 1024 * 1024),
        cost_estimate=pl.CostEstimate(flops=10**9, bytes_accessed=2**20, transcendentals=2**18),
    )(*args)


def exchange(values, rows):
    return lax.all_to_all(
        values.reshape(-1, rows, LANES), AXES, 0, 0, tiled=True
    ).reshape(values.shape)


def local(pair_in, token_mask, cotangent, gain_in, proj_w, gate_w, gain_mid, out_w):
    operand = ((PEERS * 8, LANES), BF16)
    single = ((PEERS * 4, LANES), BF16)
    sums = (PEERS * SUMS, LANES)
    plane = ((C, PLACE), F32)
    plane_b = ((C, PLACE), BF16)
    four = (4 * C, PLACE)
    scales = ((8, PLACE), F32)
    square = ((TOKENS, TOKENS), BF16)
    spare = ((PEERS * 8, LANES), F32)
    pairs = ((PLACE, C), F32)
    mixed = ((PEERS * 4, LANES), F32)
    quarter = ((4, TOKENS, LANES), F32)
    pair_shape = ((ROWS, COLS, C), BF16)
    tok_in = token_mask.reshape(1, TOKENS)

    saved = [plane, scales, plane_b, (four, F32), plane, plane_b]
    (ready,) = run(ready_kernel, [((8, LANES), F32)], [], ())
    (
        send, unit0, scale0, normed0, fact0, gating0, x0,
        proj, gate, out, gin, gmid, tok, proj_t, gate_t, out_t,
    ) = run(
        first_kernel,
        [operand]
        + saved
        + [(a.shape, a.dtype) for a in (proj_w, gate_w, out_w, gain_in, gain_mid, tok_in)]
        + [((2, 4 * C, C), BF16), ((2, C, C), BF16), ((2, C, C), BF16)],
        [spare, pairs],
        (ready, pair_in, proj_w, gate_w, out_w, gain_in, gain_mid, tok_in),
    )
    send, left0, right0 = run(
        functools.partial(product_kernel, 0), [single, square, square], [quarter],
        (exchange(send, 8), tok),
    )
    (
        send, unit1, scale1, normed1, fact1, gating1, x1,
        mix_unit0, mix_scale0, mix_normed0, gate_fact0,
    ) = run(
        middle_kernel, [operand] + saved + [plane, scales, plane_b, plane], [spare, mixed],
        (exchange(send, 4), x0, gating0, gin, gmid, proj_t, gate_t, out_t),
    )
    send, left1, right1 = run(
        functools.partial(product_kernel, 1), [single, square, square], [quarter],
        (exchange(send, 8), tok),
    )
    ready_out, send, grad1, d_gated1, weights1 = run(
        turn_kernel, [pair_shape, single, plane, plane, ((2, C, C), F32)],
        [mixed, pairs, plane_b, plane_b, plane_b],
        (exchange(send, 4), x1, gating1, normed1, cotangent, gmid, gate, out, out_t),
    )
    (send,) = run(
        functools.partial(product_back_kernel, 1), [operand], [quarter],
        (exchange(send, 4), tok, left1, right1),
    )
    send, grad0, d_gated0, rows, pair_out = run(
        both_back_kernel, [single, plane, plane, (sums, F32), pair_shape],
        [spare, mixed, (four, BF16), plane_b, plane_b, (None, ())],
        (
            exchange(send, 8), fact1, d_gated1, unit1, scale1, grad1, normed1, weights1,
            gating0, mix_unit0, mix_scale0, mix_normed0, gate_fact0, normed0,
            gin, gmid, proj, gate, out, ready_out,
        ),
        (4,),
    )
    (send,) = run(
        functools.partial(product_back_kernel, 0), [operand], [quarter],
        (exchange(send, 4), tok, left0, right0),
    )
    send, ready_grad = run(
        last_back_kernel, [(sums, BF16), pair_shape], [spare, (sums, F32), (four, BF16), pairs],
        (exchange(send, 8), fact0, normed0, rows, d_gated0, unit0, scale0, grad0, gin, proj),
    )
    (send,) = run(collect_kernel, [(sums, BF16)], [], (exchange(send, 4),))
    grads = [(a.shape, F32) for a in (gain_in, proj_w, gate_w, gain_mid, out_w)]
    pair_grad, gin_grad, proj_grad, gate_grad, gmid_grad, out_grad = run(
        spread_kernel, [pair_shape] + grads, [(sums, F32)] + grads + [(None, (9,))],
        (exchange(send, 4), ready_grad, gin, gmid, proj, gate, out),
        range(6),
    )
    return pair_out, pair_grad, gin_grad, proj_grad, gate_grad, gmid_grad, out_grad


def solution(mesh):
    placed = (P("row", "col", None), P(), P("row", "col", None), P(), P(), P(), P(), P())
    return jax.shard_map(
        local,
        mesh=mesh,
        in_specs=placed,
        out_specs=(P("row", "col", None), P("row", "col", None), P(), P(), P(), P(), P()),
        check_vma=False,
    )
```

```python
import functools

import jax
import jax.numpy as jnp
from jax import lax
from jax.experimental import pallas as pl
from jax.experimental.pallas import tpu as pltpu
from jax.sharding import PartitionSpec as P

F32 = jnp.float32
BF16 = jnp.bfloat16
C = 128
LANES = 128
ROWS = 32
COLS = 16
TOKENS = 256
PLACE = ROWS * COLS
TILES = PLACE // LANES
PEERS = 128
AXES = ("row", "col")
SUMS = 12


def mm(a, b, a_dim, b_dim):
    return lax.dot_general(
        a.astype(BF16), b.astype(BF16), (((a_dim,), (b_dim,)), ((), ())), preferred_element_type=F32
    )


def tile(t):
    return pl.ds(t * LANES, LANES)


def lane_index(rows):
    return lax.broadcasted_iota(jnp.int32, (rows, LANES), 1)


def swap_slots(parts):
    lane = lane_index(parts[0].shape[0])
    low = lane < 64
    even = (lane // 32) % 2 == 0
    turned = [pltpu.roll(part, 64, 1) for part in parts]
    first = [
        jnp.where(low, parts[0], turned[2]),
        jnp.where(low, parts[1], turned[3]),
        jnp.where(low, turned[0], parts[2]),
        jnp.where(low, turned[1], parts[3]),
    ]
    result = []
    for base in (0, 2):
        result.append(jnp.where(even, first[base], pltpu.roll(first[base + 1], 32, 1)))
        result.append(jnp.where(even, pltpu.roll(first[base], 96, 1), first[base + 1]))
    return result


def as_column(gain_ref, layer):
    return jnp.broadcast_to(gain_ref[pl.ds(layer, 1), :], (LANES, LANES)).T


def standardize(values):
    average = jnp.mean(values, axis=0, keepdims=True)
    centered = values - average
    variance = jnp.mean(centered * centered, axis=0, keepdims=True)
    scale = lax.rsqrt(variance + 1e-05)
    return centered * scale, scale


def standardize_back(d_unit, unit, scale):
    mean_d = jnp.mean(d_unit, axis=0, keepdims=True)
    mean_du = jnp.mean(d_unit * unit, axis=0, keepdims=True)
    return scale * (d_unit - mean_d - unit * mean_du)


def pairs_to_lanes(pairs_ref, spare):
    spare[...] = pairs_ref[...].astype(F32).reshape(PLACE, C)
    tiles = []
    for t in range(TILES):
        block = jnp.concatenate(
            [spare[pl.ds(4 * t + q, ROWS, COLS), :] for q in range(4)], axis=0
        )
        tiles.append(block.T)
    return tiles


def lanes_to_pairs(tiles, pairs_ref, spare):
    for t in range(TILES):
        block = tiles[t].T
        for q in range(4):
            spare[pl.ds(4 * t + q, ROWS, COLS), :] = block[q * ROWS : (q + 1) * ROWS, :]
    pairs_ref[...] = spare[...].reshape(ROWS, COLS, C).astype(pairs_ref.dtype)


def put_operands(t, left, right, spare):
    low = lane_index(C) < 64
    spare[pl.ds(2 * t, C, 8), :] = jnp.where(low, left, pltpu.roll(right, 64, 1))
    spare[pl.ds(2 * t + 1, C, 8), :] = jnp.where(low, pltpu.roll(left, 64, 1), right)


def get_operands(t, spare):
    low = lane_index(C) < 64
    even = spare[pl.ds(2 * t, C, 8), :]
    odd = spare[pl.ds(2 * t + 1, C, 8), :]
    left = jnp.where(low, even, pltpu.roll(odd, 64, 1))
    right = jnp.where(low, pltpu.roll(even, 64, 1), odd)
    return left, right


def front(tiles, gain, proj_t, gate_t, layer, spare, saved):
    unit_ref, scale_ref, normed_ref, fact_ref, gating_ref = saved
    for t, values in enumerate(tiles):
        unit, scale = standardize(values)
        unit_ref[:, tile(t)] = unit
        scale_ref[:, tile(t)] = jnp.broadcast_to(scale, (8, LANES))
        normed_ref[:, tile(t)] = (unit * gain).astype(BF16)
    normed = normed_ref[...]
    parts = []
    for base in (0, 2):
        closed = mm(proj_t[layer, pl.ds(base * C, C), :], normed, 1, 0)
        value = mm(proj_t[layer, pl.ds((base + 1) * C, C), :], normed, 1, 0)
        opened = jax.nn.sigmoid(closed)
        operand = opened * value
        fact_ref[pl.ds(base * C, C), :] = operand * (1.0 - opened)
        fact_ref[pl.ds((base + 1) * C, C), :] = opened
        parts.append(operand)
    for t in range(TILES):
        left, right = (part[:, t * LANES : (t + 1) * LANES] for part in parts)
        put_operands(t, left, right, spare)
    gating_ref[...] = jax.nn.sigmoid(mm(gate_t[layer], normed, 1, 0))


def ready_kernel(ready_ref):
    ready_ref[...] = jnp.zeros((8, LANES), F32)


def first_kernel(
    ready_ref, pair_ref, proj, gate, out_w, gin, gmid, tok,
    send_ref, unit_ref, scale_ref, normed_ref, fact_ref, gating_ref, x_ref,
    proj_out, gate_out, out_out, gin_out, gmid_out, tok_out, proj_t, gate_t, out_t,
    spare, pairs,
):
    for m in range(2):
        proj_t[m] = proj[m].T
        gate_t[m] = gate[m].T
        out_t[m] = out_w[m].T
    gain = as_column(gin, 0)
    tiles = pairs_to_lanes(pair_ref, pairs)
    saved = (unit_ref, scale_ref, normed_ref, fact_ref, gating_ref)
    for t in range(TILES):
        x_ref[:, tile(t)] = tiles[t].astype(BF16)
    front(tiles, gain, proj_t, gate_t, 0, spare, saved)
    send_ref[...] = spare[...].astype(BF16)
    for given, kept in (
        (proj, proj_out), (gate, gate_out), (out_w, out_out),
        (gin, gin_out), (gmid, gmid_out), (tok, tok_out),
    ):
        kept[...] = given[...]


def middle_kernel(
    mix_ref, x_ref, gating0_ref, gin, gmid, proj_t, gate_t, out_t,
    send_ref, unit_ref, scale_ref, normed_ref, fact_ref, gating_ref, next_ref,
    mix_unit_ref, mix_scale_ref, mix_normed_ref, gate_fact_ref, spare, mixed,
):
    mixed[...] = mix_ref[...].astype(F32)
    gain_a = as_column(gmid, 0)
    gain_b = as_column(gin, 1)
    saved = (unit_ref, scale_ref, normed_ref, fact_ref, gating_ref)
    for t in range(TILES):
        unit, scale = standardize(mixed[pl.ds(t, C, TILES), :])
        mix_unit_ref[:, tile(t)] = unit
        mix_scale_ref[:, tile(t)] = jnp.broadcast_to(scale, (8, LANES))
        mix_normed_ref[:, tile(t)] = (unit * gain_a).astype(BF16)
    update = mm(out_t[0], mix_normed_ref[...], 1, 0)
    tiles = []
    for t in range(TILES):
        gating = gating0_ref[:, tile(t)]
        gated = update[:, t * LANES : (t + 1) * LANES] * gating
        rounded = (x_ref[:, tile(t)].astype(F32) + gated).astype(BF16)
        next_ref[:, tile(t)] = rounded
        gate_fact_ref[:, tile(t)] = gated * (1.0 - gating)
        tiles.append(rounded.astype(F32))
    front(tiles, gain_b, proj_t, gate_t, 1, spare, saved)
    send_ref[...] = spare[...].astype(BF16)


def turn_kernel(
    mix_ref, x_ref, gating_ref, normed_ref, cot_ref, gmid, gate, out_w, out_t,
    pair_out_ref, send_ref, grad_ref, d_gated_ref, weights_ref,
    mixed, pairs, kept_n, kept_g, kept_d,
):
    mixed[...] = mix_ref[...].astype(F32)
    gain = as_column(gmid, 1)
    cot = pairs_to_lanes(cot_ref, pairs)
    units = []
    for t in range(TILES):
        units.append(standardize(mixed[pl.ds(t, C, TILES), :]))
        kept_n[:, tile(t)] = (units[t][0] * gain).astype(BF16)
        grad_ref[:, tile(t)] = cot[t]
        kept_d[:, tile(t)] = (cot[t] * gating_ref[:, tile(t)]).astype(BF16)
    d_normed = mm(out_w[1], kept_d[...], 1, 0)
    update = mm(out_t[1], kept_n[...], 1, 0)
    outs = []
    for t in range(TILES):
        piece = slice(t * LANES, (t + 1) * LANES)
        mixed[pl.ds(t, C, TILES), :] = standardize_back(d_normed[:, piece] * gain, *units[t])
        gating = gating_ref[:, tile(t)]
        gated = update[:, piece] * gating
        outs.append(x_ref[:, tile(t)].astype(F32) + gated)
        kept_g[:, tile(t)] = (cot[t] * gated * (1.0 - gating)).astype(BF16)
    d_gated_ref[...] = mm(gate[1], kept_g[...], 1, 0)
    send_ref[...] = mixed[...].astype(BF16)
    weights_ref[0] = mm(normed_ref[...], kept_g[...], 1, 1)
    weights_ref[1] = mm(kept_n[...], kept_d[...], 1, 1)
    lanes_to_pairs(outs, pair_out_ref, pairs)


def projected_back(t, spare, fact_ref, kept_p):
    d_left, d_right = get_operands(t, spare)
    for part, d_out in enumerate((d_left, d_left, d_right, d_right)):
        rows = pl.ds(part * C, C)
        kept_p[rows, tile(t)] = (d_out * fact_ref[rows, tile(t)]).astype(BF16)


def both_back_kernel(
    recv_ref, fact_ref, d_gated1_ref, unit_ref, scale_ref, grad_ref, normed1_ref, weights1_ref,
    gating_ref, mix_unit_ref, mix_scale_ref, mix_normed_ref, gate_fact_ref, normed0_ref,
    gin, gmid, proj, gate, out_w,
    send_ref, next_grad_ref, d_gated_ref, rows_ref,
    spare, mixed, kept_p, kept_g, kept_d,
):
    spare[...] = recv_ref[...].astype(F32)
    gain_a = as_column(gin, 1)
    gain_b = as_column(gmid, 0)
    for t in range(TILES):
        projected_back(t, spare, fact_ref, kept_p)
    d_normed = mm(proj[1], kept_p[...], 1, 0) + d_gated1_ref[...]
    for t in range(TILES):
        piece = slice(t * LANES, (t + 1) * LANES)
        d_x = standardize_back(
            d_normed[:, piece] * gain_a, unit_ref[:, tile(t)], scale_ref[pl.ds(0, 1), tile(t)]
        )
        grad = grad_ref[:, tile(t)] + d_x
        next_grad_ref[:, tile(t)] = grad
        kept_d[:, tile(t)] = (grad * gating_ref[:, tile(t)]).astype(BF16)
        kept_g[:, tile(t)] = (grad * gate_fact_ref[:, tile(t)]).astype(BF16)
    d_normed = mm(out_w[0], kept_d[...], 1, 0)
    for t in range(TILES):
        piece = slice(t * LANES, (t + 1) * LANES)
        mixed[pl.ds(t, C, TILES), :] = standardize_back(
            d_normed[:, piece] * gain_b,
            mix_unit_ref[:, tile(t)],
            mix_scale_ref[pl.ds(0, 1), tile(t)],
        )
    d_gated_ref[...] = mm(gate[0], kept_g[...], 1, 0)
    send_ref[...] = mixed[...].astype(BF16)
    first = mm(normed1_ref[...], kept_p[...], 1, 1)
    for e in range(4):
        rows_ref[pl.ds(4 + e, C, SUMS), :] = first[:, e * C : (e + 1) * C]
    rows_ref[pl.ds(8, C, SUMS), :] = mm(normed0_ref[...], kept_g[...], 1, 1)
    rows_ref[pl.ds(9, C, SUMS), :] = weights1_ref[0]
    rows_ref[pl.ds(10, C, SUMS), :] = mm(mix_normed_ref[...], kept_d[...], 1, 1)
    rows_ref[pl.ds(11, C, SUMS), :] = weights1_ref[1]


def last_back_kernel(
    recv_ref, fact_ref, normed_ref, rows_ref, d_gated_ref, unit_ref, scale_ref, grad_ref, gin, proj,
    send_ref, pair_grad_ref, spare, rows, kept_p, pairs,
):
    spare[...] = recv_ref[...].astype(F32)
    rows[...] = rows_ref[...]
    gain = as_column(gin, 0)
    outs = []
    for t in range(TILES):
        projected_back(t, spare, fact_ref, kept_p)
    d_normed = mm(proj[0], kept_p[...], 1, 0) + d_gated_ref[...]
    for t in range(TILES):
        d_x = standardize_back(
            d_normed[:, t * LANES : (t + 1) * LANES] * gain,
            unit_ref[:, tile(t)],
            scale_ref[pl.ds(0, 1), tile(t)],
        )
        outs.append(grad_ref[:, tile(t)] + d_x)
    weights = mm(normed_ref[...], kept_p[...], 1, 1)
    for e in range(4):
        rows[pl.ds(e, C, SUMS), :] = weights[:, e * C : (e + 1) * C]
    send_ref[...] = rows[...].astype(BF16)
    lanes_to_pairs(outs, pair_grad_ref, pairs)


def pair_mask(tok_ref):
    token = jnp.broadcast_to(tok_ref[...].astype(F32), (8, TOKENS))
    token = jnp.where(lax.broadcasted_iota(jnp.int32, (8, TOKENS), 0) == 0, token, 0.0)
    return mm(token, token, 0, 0)


def whole(spare, first):
    return jnp.concatenate([spare[first], spare[first + 1]], axis=1)


def product_kernel(layer, recv_ref, tok_ref, send_ref, left_ref, right_ref, spare):
    for hi in range(2):
        parts = [
            recv_ref[pl.ds((4 * hi + lo) * LANES, LANES), :] for lo in range(4)
        ]
        for slot, block in enumerate(swap_slots(parts)):
            spare[2 * (slot // 2) + hi, pl.ds(slot % 2, LANES, 2), :] = block.astype(F32)
    mask = pair_mask(tok_ref)
    left = (whole(spare, 0) * mask).astype(BF16)
    right = (whole(spare, 2) * mask).astype(BF16)
    left_ref[...] = left
    right_ref[...] = right
    mixture = mm(right, left, layer, layer)
    for hi in range(2):
        spare[hi] = mixture[:, hi * LANES : (hi + 1) * LANES]
    for hi in range(2):
        parts = [spare[hi, pl.ds(q, 64, 4), :].astype(BF16) for q in range(4)]
        for lo, block in enumerate(swap_slots(parts)):
            send_ref[pl.ds((4 * hi + lo) * 64, 64), :] = block


def product_back_kernel(
    layer, recv_ref, tok_ref, left_ref, right_ref, send_ref, spare
):
    for hi in range(2):
        parts = [recv_ref[pl.ds((4 * hi + lo) * 64, 64), :] for lo in range(4)]
        for q, block in enumerate(swap_slots(parts)):
            spare[hi, pl.ds(q, 64, 4), :] = block.astype(F32)
    d_mix = whole(spare, 0).astype(BF16)
    left = left_ref[...]
    right = right_ref[...]
    if layer == 0:
        d_left = mm(right, d_mix, 1, 0)
        d_right = mm(left, d_mix, 1, 1)
    else:
        d_left = mm(d_mix, right, 0, 0)
        d_right = mm(d_mix, left, 1, 0)
    mask = pair_mask(tok_ref)
    for first, value in ((0, d_left * mask), (2, d_right * mask)):
        for hi in range(2):
            spare[first + hi] = value[:, hi * LANES : (hi + 1) * LANES]
    for hi in range(2):
        parts = [
            spare[2 * (slot // 2) + hi, pl.ds(slot % 2, LANES, 2), :].astype(BF16)
            for slot in range(4)
        ]
        for lo, block in enumerate(swap_slots(parts)):
            send_ref[pl.ds((4 * hi + lo) * LANES, LANES), :] = block


def collect_kernel(recv_ref, send_ref):
    twice = jnp.sum(recv_ref[...].astype(F32).reshape(PEERS // 2, 2 * SUMS, LANES), axis=0)
    total = twice[0:SUMS] + twice[SUMS:]
    both = jnp.concatenate([total, total], axis=0)
    send_ref[...] = (
        jnp.broadcast_to(both[None], (PEERS // 2, 2 * SUMS, LANES))
        .reshape(PEERS * SUMS, LANES)
        .astype(BF16)
    )


def spread_kernel(
    recv_ref, out_ready, grad_ready, gin, gmid, proj, gate, out_w,
    pair_out_ref, pair_grad_ref, gin_ref, proj_ref, gate_ref, gmid_ref, out_ref,
    rows, gin_own, proj_own, gate_own, gmid_own, out_own, sems,
):
    copies = []

    def give(own, ref):
        copies.append(pltpu.make_async_copy(own, ref, sems.at[len(copies)]))
        copies[-1].start()

    give(out_ready, pair_out_ref)
    give(grad_ready, pair_grad_ref)
    rows[...] = recv_ref[...].astype(F32) * (1.0 / TOKENS)
    lane = lane_index(C)
    totals = jnp.zeros((C, LANES), F32)
    for m in range(2):
        gated = rows[pl.ds(8 + m, C, SUMS), :]
        mixed = rows[pl.ds(10 + m, C, SUMS), :]
        total = gated * gate[m].astype(F32)
        for e in range(4):
            part = rows[pl.ds(4 * m + e, C, SUMS), :]
            proj_own[m, :, tile(e)] = part
            total = total + part * proj[m, :, tile(e)].astype(F32)
        give(proj_own.at[m], proj_ref.at[m])
        gate_own[m] = gated
        out_own[m] = mixed
        total_in = jnp.sum(total, axis=1, keepdims=True)
        total_mid = jnp.sum(mixed * out_w[m].astype(F32), axis=1, keepdims=True)
        totals = jnp.where(lane == m, total_in, jnp.where(lane == 2 + m, total_mid, totals))
    give(gate_own, gate_ref)
    give(out_own, out_ref)
    turned = totals.T
    gin_own[...] = turned[0:2] / gin[...]
    gmid_own[...] = turned[2:4] / gmid[...]
    give(gin_own, gin_ref)
    give(gmid_own, gmid_ref)
    for copy in copies:
        copy.wait()


def run(kernel, outs, scratch, args, away=()):
    spaces = [pl.ANY if k in away else pltpu.VMEM for k in range(len(outs))]
    return pl.pallas_call(
        kernel,
        out_shape=[jax.ShapeDtypeStruct(shape, dtype) for shape, dtype in outs],
        in_specs=[pl.BlockSpec(memory_space=pltpu.VMEM)] * len(args),
        out_specs=[pl.BlockSpec(memory_space=space) for space in spaces],
        scratch_shapes=[
            pltpu.VMEM(shape, dtype) if shape else pltpu.SemaphoreType.DMA(dtype)
            for shape, dtype in scratch
        ],
        compiler_params=pltpu.CompilerParams(vmem_limit_bytes=16 * 1024 * 1024),
        cost_estimate=pl.CostEstimate(flops=10**9, bytes_accessed=2**20, transcendentals=2**18),
    )(*args)


def exchange(values, rows):
    return lax.all_to_all(
        values.reshape(-1, rows, LANES), AXES, 0, 0, tiled=True
    ).reshape(values.shape)


def local(pair_in, token_mask, cotangent, gain_in, proj_w, gate_w, gain_mid, out_w):
    operand = ((PEERS * 8, LANES), BF16)
    single = ((PEERS * 4, LANES), BF16)
    sums = (PEERS * SUMS, LANES)
    plane = ((C, PLACE), F32)
    plane_b = ((C, PLACE), BF16)
    four = (4 * C, PLACE)
    scales = ((8, PLACE), F32)
    square = ((TOKENS, TOKENS), BF16)
    spare = ((PEERS * 8, LANES), F32)
    pairs = ((PLACE, C), F32)
    mixed = ((PEERS * 4, LANES), F32)
    quarter = ((4, TOKENS, LANES), F32)
    pair_shape = ((ROWS, COLS, C), BF16)
    tok_in = token_mask.reshape(1, TOKENS)

    saved = [plane, scales, plane_b, (four, F32), plane, plane_b]
    (ready,) = run(ready_kernel, [((8, LANES), F32)], [], ())
    (
        send, unit0, scale0, normed0, fact0, gating0, x0,
        proj, gate, out, gin, gmid, tok, proj_t, gate_t, out_t,
    ) = run(
        first_kernel,
        [operand]
        + saved
        + [(a.shape, a.dtype) for a in (proj_w, gate_w, out_w, gain_in, gain_mid, tok_in)]
        + [((2, 4 * C, C), BF16), ((2, C, C), BF16), ((2, C, C), BF16)],
        [spare, pairs],
        (ready, pair_in, proj_w, gate_w, out_w, gain_in, gain_mid, tok_in),
    )
    send, left0, right0 = run(
        functools.partial(product_kernel, 0), [single, square, square], [quarter],
        (exchange(send, 8), tok),
    )
    (
        send, unit1, scale1, normed1, fact1, gating1, x1,
        mix_unit0, mix_scale0, mix_normed0, gate_fact0,
    ) = run(
        middle_kernel, [operand] + saved + [plane, scales, plane_b, plane], [spare, mixed],
        (exchange(send, 4), x0, gating0, gin, gmid, proj_t, gate_t, out_t),
    )
    send, left1, right1 = run(
        functools.partial(product_kernel, 1), [single, square, square], [quarter],
        (exchange(send, 8), tok),
    )
    ready_out, send, grad1, d_gated1, weights1 = run(
        turn_kernel, [pair_shape, single, plane, plane, ((2, C, C), F32)],
        [mixed, pairs, plane_b, plane_b, plane_b],
        (exchange(send, 4), x1, gating1, normed1, cotangent, gmid, gate, out, out_t),
    )
    (send,) = run(
        functools.partial(product_back_kernel, 1), [operand], [quarter],
        (exchange(send, 4), tok, left1, right1),
    )
    send, grad0, d_gated0, rows = run(
        both_back_kernel, [single, plane, plane, (sums, F32)],
        [spare, mixed, (four, BF16), plane_b, plane_b],
        (
            exchange(send, 8), fact1, d_gated1, unit1, scale1, grad1, normed1, weights1,
            gating0, mix_unit0, mix_scale0, mix_normed0, gate_fact0, normed0,
            gin, gmid, proj, gate, out,
        ),
    )
    (send,) = run(
        functools.partial(product_back_kernel, 0), [operand], [quarter],
        (exchange(send, 4), tok, left0, right0),
    )
    send, ready_grad = run(
        last_back_kernel, [(sums, BF16), pair_shape], [spare, (sums, F32), (four, BF16), pairs],
        (exchange(send, 8), fact0, normed0, rows, d_gated0, unit0, scale0, grad0, gin, proj),
    )
    (send,) = run(collect_kernel, [(sums, BF16)], [], (exchange(send, 4),))
    grads = [(a.shape, F32) for a in (gain_in, proj_w, gate_w, gain_mid, out_w)]
    pair_out, pair_grad, gin_grad, proj_grad, gate_grad, gmid_grad, out_grad = run(
        spread_kernel, [pair_shape] * 2 + grads, [(sums, F32)] + grads + [(None, (8,))],
        (exchange(send, 4), ready_out, ready_grad, gin, gmid, proj, gate, out),
        range(7),
    )
    return pair_out, pair_grad, gin_grad, proj_grad, gate_grad, gmid_grad, out_grad


def solution(mesh):
    placed = (P("row", "col", None), P(), P("row", "col", None), P(), P(), P(), P(), P())
    return jax.shard_map(
        local,
        mesh=mesh,
        in_specs=placed,
        out_specs=(P("row", "col", None), P("row", "col", None), P(), P(), P(), P(), P()),
        check_vma=False,
    )
```

```python
import jax
import jax.numpy as jnp
from jax import lax
from jax.experimental import pallas as pl
from jax.experimental.pallas import tpu as pltpu
from jax.sharding import PartitionSpec as P

F32 = jnp.float32
BF16 = jnp.bfloat16
C = 128
LANES = 128
ROWS = 32
COLS = 16
TOKENS = 256
PLACE = ROWS * COLS
TILES = PLACE // LANES
PEERS = 128
AXES = ("row", "col")
SUMS = 12


def mm(a, b, a_dim, b_dim):
    return lax.dot_general(
        a.astype(BF16), b.astype(BF16), (((a_dim,), (b_dim,)), ((), ())), preferred_element_type=F32
    )


WIDE = PLACE // 2


def wide(h):
    return pl.ds(h * WIDE, WIDE)


def inner(h):
    return [(2 * h + k, slice(k * LANES, (k + 1) * LANES)) for k in range(2)]


def tile(t):
    return pl.ds(t * LANES, LANES)


def lane_index(rows):
    return lax.broadcasted_iota(jnp.int32, (rows, LANES), 1)


def swap_slots(parts):
    lane = lane_index(parts[0].shape[0])
    low = lane < 64
    even = (lane // 32) % 2 == 0
    turned = [pltpu.roll(part, 64, 1) for part in parts]
    first = [
        jnp.where(low, parts[0], turned[2]),
        jnp.where(low, parts[1], turned[3]),
        jnp.where(low, turned[0], parts[2]),
        jnp.where(low, turned[1], parts[3]),
    ]
    result = []
    for base in (0, 2):
        result.append(jnp.where(even, first[base], pltpu.roll(first[base + 1], 32, 1)))
        result.append(jnp.where(even, pltpu.roll(first[base], 96, 1), first[base + 1]))
    return result


def as_column(gain_ref, layer):
    return jnp.broadcast_to(gain_ref[pl.ds(layer, 1), :], (LANES, LANES)).T


def standardize(values):
    average = jnp.mean(values, axis=0, keepdims=True)
    centered = values - average
    variance = jnp.mean(centered * centered, axis=0, keepdims=True)
    scale = lax.rsqrt(variance + 1e-05)
    return centered * scale, scale


def standardize_back(d_unit, unit, scale):
    mean_d = jnp.mean(d_unit, axis=0, keepdims=True)
    mean_du = jnp.mean(d_unit * unit, axis=0, keepdims=True)
    return scale * (d_unit - mean_d - unit * mean_du)


def pairs_to_lanes(pairs_ref, spare):
    spare[...] = pairs_ref[...].astype(F32).reshape(PLACE, C)
    tiles = []
    for t in range(TILES):
        block = jnp.concatenate(
            [spare[pl.ds(4 * t + q, ROWS, COLS), :] for q in range(4)], axis=0
        )
        tiles.append(block.T)
    return tiles


def lanes_to_pairs(tiles, pairs_ref, spare):
    for t in range(TILES):
        block = tiles[t].T
        for q in range(4):
            spare[pl.ds(4 * t + q, ROWS, COLS), :] = block[q * ROWS : (q + 1) * ROWS, :]
    pairs_ref[...] = spare[...].reshape(ROWS, COLS, C).astype(pairs_ref.dtype)


def put_operands(t, left, right, spare):
    low = lane_index(C) < 64
    spare[pl.ds(2 * t, C, 8), :] = jnp.where(low, left, pltpu.roll(right, 64, 1))
    spare[pl.ds(2 * t + 1, C, 8), :] = jnp.where(low, pltpu.roll(left, 64, 1), right)


def get_operands(t, spare):
    low = lane_index(C) < 64
    even = spare[pl.ds(2 * t, C, 8), :]
    odd = spare[pl.ds(2 * t + 1, C, 8), :]
    left = jnp.where(low, even, pltpu.roll(odd, 64, 1))
    right = jnp.where(low, pltpu.roll(even, 64, 1), odd)
    return left, right


def front(h, tiles, gain, proj_t, gate_t, layer, spare, saved, valid):
    unit_ref, scale_ref, normed_ref, fact_ref, gating_ref = saved
    for (t, _), values in zip(inner(h), tiles):
        unit, scale = standardize(values)
        unit_ref[:, tile(t)] = unit
        scale_ref[:, tile(t)] = jnp.broadcast_to(scale, (8, LANES))
        normed_ref[:, tile(t)] = (unit * gain).astype(BF16)
    normed = normed_ref[:, wide(h)]
    parts = []
    for base in (0, 2):
        closed = mm(proj_t[layer, pl.ds(base * C, C), :], normed, 1, 0)
        value = mm(proj_t[layer, pl.ds((base + 1) * C, C), :], normed, 1, 0)
        opened = jax.nn.sigmoid(closed)
        operand = opened * value * valid
        fact_ref[pl.ds(base * C, C), wide(h)] = operand * (1.0 - opened)
        fact_ref[pl.ds((base + 1) * C, C), wide(h)] = opened * valid
        parts.append(operand)
    for t, piece in inner(h):
        put_operands(t, parts[0][:, piece], parts[1][:, piece], spare)
    gating_ref[:, wide(h)] = jax.nn.sigmoid(mm(gate_t[layer], normed, 1, 0))


def place_kernel(first_ref, second_ref):
    token = lax.broadcasted_iota(jnp.int32, (TOKENS, PLACE), 0)
    place = lax.broadcasted_iota(jnp.int32, (TOKENS, PLACE), 1)
    first = place % ROWS + ROWS * lax.axis_index("row")
    second = place // ROWS + COLS * lax.axis_index("col")
    first_ref[...] = (token == first).astype(F32).astype(BF16)
    second_ref[...] = (token == second).astype(F32).astype(BF16)


def first_kernel(
    first_ref, second_ref, tok, pair_ref, proj, gate, out_w, gin, gmid,
    send_ref, unit_ref, scale_ref, normed_ref, fact_ref, gating_ref, x_ref,
    proj_out, gate_out, out_out, gin_out, gmid_out, proj_t, gate_t, out_t,
    valid_ref, spare, pairs,
):
    token = jnp.broadcast_to(tok[...].astype(F32), (8, TOKENS))
    valid_ref[...] = mm(token, first_ref[...], 1, 0) * mm(token, second_ref[...], 1, 0)
    for m in range(2):
        proj_t[m] = proj[m].T
        gate_t[m] = gate[m].T
        out_t[m] = out_w[m].T
    gain = as_column(gin, 0)
    tiles = pairs_to_lanes(pair_ref, pairs)
    saved = (unit_ref, scale_ref, normed_ref, fact_ref, gating_ref)
    for t in range(TILES):
        x_ref[:, tile(t)] = tiles[t].astype(BF16)
    for h in range(2):
        valid = valid_ref[pl.ds(0, 1), wide(h)]
        front(h, tiles[2 * h : 2 * h + 2], gain, proj_t, gate_t, 0, spare, saved, valid)
    send_ref[...] = spare[...].astype(BF16)
    for given, kept in (
        (proj, proj_out), (gate, gate_out), (out_w, out_out),
        (gin, gin_out), (gmid, gmid_out),
    ):
        kept[...] = given[...]


def middle_kernel(
    mix_ref, x_ref, gating0_ref, valid_ref, gin, gmid, proj_t, gate_t, out_t,
    send_ref, unit_ref, scale_ref, normed_ref, fact_ref, gating_ref, next_ref,
    mix_unit_ref, mix_scale_ref, mix_normed_ref, gate_fact_ref, spare, mixed,
):
    mixed[...] = mix_ref[...].astype(F32)
    gain_a = as_column(gmid, 0)
    gain_b = as_column(gin, 1)
    saved = (unit_ref, scale_ref, normed_ref, fact_ref, gating_ref)
    updates = []
    for h in range(2):
        for t, _ in inner(h):
            unit, scale = standardize(mixed[pl.ds(t, C, TILES), :])
            mix_unit_ref[:, tile(t)] = unit
            mix_scale_ref[:, tile(t)] = jnp.broadcast_to(scale, (8, LANES))
            mix_normed_ref[:, tile(t)] = (unit * gain_a).astype(BF16)
        updates.append(mm(out_t[0], mix_normed_ref[:, wide(h)], 1, 0))
    for h in range(2):
        tiles = []
        for t, piece in inner(h):
            gating = gating0_ref[:, tile(t)]
            gated = updates[h][:, piece] * gating
            rounded = (x_ref[:, tile(t)].astype(F32) + gated).astype(BF16)
            next_ref[:, tile(t)] = rounded
            gate_fact_ref[:, tile(t)] = gated * (1.0 - gating)
            tiles.append(rounded.astype(F32))
        valid = valid_ref[pl.ds(0, 1), wide(h)]
        front(h, tiles, gain_b, proj_t, gate_t, 1, spare, saved, valid)
    send_ref[...] = spare[...].astype(BF16)


def turn_kernel(
    mix_ref, x_ref, gating_ref, normed_ref, cot_ref, gmid, gate, out_w, out_t,
    pair_out_ref, send_ref, grad_ref, d_gated_ref, weights_ref,
    mixed, pairs, kept_n, kept_g, kept_d,
):
    mixed[...] = mix_ref[...].astype(F32)
    gain = as_column(gmid, 1)
    cot = pairs_to_lanes(cot_ref, pairs)
    units, d_normed, update = [], [], []
    for h in range(2):
        for t, _ in inner(h):
            units.append(standardize(mixed[pl.ds(t, C, TILES), :]))
            kept_n[:, tile(t)] = (units[t][0] * gain).astype(BF16)
            grad_ref[:, tile(t)] = cot[t]
            kept_d[:, tile(t)] = (cot[t] * gating_ref[:, tile(t)]).astype(BF16)
        d_normed.append(mm(out_w[1], kept_d[:, wide(h)], 1, 0))
        update.append(mm(out_t[1], kept_n[:, wide(h)], 1, 0))
    outs = []
    for h in range(2):
        for t, piece in inner(h):
            mixed[pl.ds(t, C, TILES), :] = standardize_back(d_normed[h][:, piece] * gain, *units[t])
            gating = gating_ref[:, tile(t)]
            gated = update[h][:, piece] * gating
            outs.append(x_ref[:, tile(t)].astype(F32) + gated)
            kept_g[:, tile(t)] = (cot[t] * gated * (1.0 - gating)).astype(BF16)
    d_gated_ref[...] = mm(gate[1], kept_g[...], 1, 0)
    send_ref[...] = mixed[...].astype(BF16)
    weights_ref[0] = mm(normed_ref[...], kept_g[...], 1, 1)
    weights_ref[1] = mm(kept_n[...], kept_d[...], 1, 1)
    lanes_to_pairs(outs, pair_out_ref, pairs)


def projected_back(t, spare, fact_ref, kept_p):
    d_left, d_right = get_operands(t, spare)
    for part, d_out in enumerate((d_left, d_left, d_right, d_right)):
        rows = pl.ds(part * C, C)
        kept_p[rows, tile(t)] = (d_out * fact_ref[rows, tile(t)]).astype(BF16)


def both_back_kernel(
    recv_ref, fact_ref, d_gated1_ref, unit_ref, scale_ref, grad_ref, normed1_ref, weights1_ref,
    gating_ref, mix_unit_ref, mix_scale_ref, mix_normed_ref, gate_fact_ref, normed0_ref,
    gin, gmid, proj, gate, out_w, out_ready,
    send_ref, next_grad_ref, d_gated_ref, keep_ref, pair_out_ref,
    spare, kept_p, kept_g, kept_d, sem,
):
    copy = pltpu.make_async_copy(out_ready, pair_out_ref, sem)
    copy.start()
    spare[...] = recv_ref[...].astype(F32)
    gain_a = as_column(gin, 1)
    gain_b = as_column(gmid, 0)
    d_normed = []
    for h in range(2):
        for t, _ in inner(h):
            projected_back(t, spare, fact_ref, kept_p)
        d_normed.append(mm(proj[1], kept_p[:, wide(h)], 1, 0) + d_gated1_ref[:, wide(h)])
    d_mid = []
    for h in range(2):
        for t, piece in inner(h):
            d_x = standardize_back(
                d_normed[h][:, piece] * gain_a,
                unit_ref[:, tile(t)],
                scale_ref[pl.ds(0, 1), tile(t)],
            )
            grad = grad_ref[:, tile(t)] + d_x
            next_grad_ref[:, tile(t)] = grad
            kept_d[:, tile(t)] = (grad * gating_ref[:, tile(t)]).astype(BF16)
            kept_g[:, tile(t)] = (grad * gate_fact_ref[:, tile(t)]).astype(BF16)
        d_mid.append(mm(out_w[0], kept_d[:, wide(h)], 1, 0))
    weights = mm(normed1_ref[...], kept_p[...], 1, 1)
    for h in range(2):
        for t, piece in inner(h):
            spare[pl.ds(t, C, 8), :] = standardize_back(
                d_mid[h][:, piece] * gain_b,
                mix_unit_ref[:, tile(t)],
                mix_scale_ref[pl.ds(0, 1), tile(t)],
            )
            spare[pl.ds(TILES + t, C, 8), :] = weights[:, t * LANES : (t + 1) * LANES]
    d_gated_ref[...] = mm(gate[0], kept_g[...], 1, 0)
    send_ref[...] = spare[...].astype(BF16)
    keep_ref[0] = mm(normed0_ref[...], kept_g[...], 1, 1)
    keep_ref[1] = weights1_ref[0]
    keep_ref[2] = mm(mix_normed_ref[...], kept_d[...], 1, 1)
    keep_ref[3] = weights1_ref[1]
    copy.wait()


def last_back_kernel(
    recv_ref, fact_ref, normed_ref, keep_ref, d_gated_ref, unit_ref, scale_ref, grad_ref, gin, proj,
    send_ref, pair_grad_ref, spare, kept_p, pairs,
):
    spare[...] = recv_ref[...].astype(F32)
    gain = as_column(gin, 0)
    outs = []
    d_normed = []
    for h in range(2):
        for t, _ in inner(h):
            projected_back(t, spare, fact_ref, kept_p)
        d_normed.append(mm(proj[0], kept_p[:, wide(h)], 1, 0) + d_gated_ref[:, wide(h)])
    for h in range(2):
        for t, piece in inner(h):
            d_x = standardize_back(
                d_normed[h][:, piece] * gain,
                unit_ref[:, tile(t)],
                scale_ref[pl.ds(0, 1), tile(t)],
            )
            outs.append(grad_ref[:, tile(t)] + d_x)
    weights = mm(normed_ref[...], kept_p[...], 1, 1)
    for e in range(4):
        spare[pl.ds(e, C, 8), :] = weights[:, e * C : (e + 1) * C]
        spare[pl.ds(4 + e, C, 8), :] = keep_ref[e]
    send_ref[...] = spare[...].astype(BF16)
    lanes_to_pairs(outs, pair_grad_ref, pairs)


def whole(spare, first):
    return jnp.concatenate([spare[first], spare[first + 1]], axis=1)


def halves(hi, q):
    return pl.ds(q * LANES, LANES), tile(hi)


def second_rows(layer, q):
    return pl.ds(q, 64, 4) if layer == 0 else pl.ds((q % 2) * LANES + q // 2, 64, 2)


def take_operands(recv_ref, put):
    for hi in range(2):
        parts = [recv_ref[pl.ds((4 * hi + lo) * LANES, LANES), :] for lo in range(4)]
        for slot, block in enumerate(swap_slots(parts)):
            put(hi, slot, block)


def send_operands(send_ref, get):
    for hi in range(2):
        parts = [get(hi, slot) for slot in range(4)]
        for lo, block in enumerate(swap_slots(parts)):
            send_ref[pl.ds((4 * hi + lo) * LANES, LANES), :] = block


def send_mixture(layer, mixture, send_ref, spare):
    for hi in range(2):
        spare[hi] = mixture(hi)
    for hi in range(2):
        parts = [spare[hi, second_rows(layer, q), :].astype(BF16) for q in range(4)]
        for lo, block in enumerate(swap_slots(parts)):
            send_ref[pl.ds((4 * hi + lo) * 64, 64), :] = block


def outgoing_kernel(recv_ref, send_ref, left_ref, right_ref, spare):
    def put(hi, slot, block):
        (left_ref if slot < 2 else right_ref)[halves(hi, slot % 2)] = block

    take_operands(recv_ref, put)
    right = right_ref[...]
    send_mixture(0, lambda hi: mm(right, left_ref[:, tile(hi)], 0, 0), send_ref, spare)


def incoming_kernel(recv_ref, send_ref, left_ref, right_ref, spare):
    def put(hi, slot, block):
        if slot < 2:
            spare[hi, pl.ds(slot, LANES, 2), :] = block.astype(F32)
        else:
            right_ref[halves(hi, slot % 2)] = block

    take_operands(recv_ref, put)
    left = whole(spare, 0).astype(BF16)
    left_ref[...] = left
    mixture = mm(right_ref[...], left, 1, 1)
    send_mixture(1, lambda hi: mixture[:, hi * LANES : (hi + 1) * LANES], send_ref, spare)


def incoming_back_kernel(recv_ref, left_ref, right_ref, send_ref, spare, d_rows):
    for hi in range(2):
        parts = [recv_ref[pl.ds((4 * hi + lo) * 64, 64), :] for lo in range(4)]
        for q, block in enumerate(swap_slots(parts)):
            spare[hi, second_rows(1, q), :] = block.astype(F32)
    d_mix = whole(spare, 0).astype(BF16)
    d_left = mm(d_mix, right_ref[...], 0, 0)
    d_rows[...] = mm(d_mix, left_ref[...], 1, 0).astype(BF16)
    for hi in range(2):
        spare[hi] = d_left[:, hi * LANES : (hi + 1) * LANES]

    def get(hi, slot):
        if slot < 2:
            return spare[hi, pl.ds(slot, LANES, 2), :].astype(BF16)
        return d_rows[halves(hi, slot % 2)]

    send_operands(send_ref, get)


def outgoing_back_kernel(
    recv_ref, left_ref, right_ref, send_ref, sums_ref, arrived, spare, d_rows
):
    arrived[...] = recv_ref[...].astype(F32)
    for hi in range(2):
        parts = [
            jnp.concatenate(
                [arrived[pl.ds((4 * hi + lo) * LANES + jm, COLS, 8), :] for jm in range(4)], axis=0
            ).astype(BF16)
            for lo in range(4)
        ]
        for q, block in enumerate(swap_slots(parts)):
            for jm in range(4):
                spare[hi, pl.ds(4 * jm + q, COLS, COLS), :] = block[
                    jm * COLS : (jm + 1) * COLS, :
                ].astype(F32)
    d_mix = whole(spare, 0).astype(BF16)
    d_rows[0] = mm(right_ref[...], d_mix, 1, 0).astype(BF16)
    d_rows[1] = mm(left_ref[...], d_mix, 1, 1).astype(BF16)

    def get(hi, slot):
        rows, lanes = halves(hi, slot % 2)
        return d_rows[slot // 2, rows, lanes]

    send_operands(send_ref, get)
    total = jnp.sum(recv_ref[...].astype(F32).reshape(PEERS, 8, LANES), axis=0)
    sums_ref[...] = total[TILES:]


def collect_kernel(recv_ref, sums_ref, send_ref):
    total = jnp.sum(recv_ref[...].astype(F32).reshape(PEERS, 8, LANES), axis=0)
    block = [total[0:4], sums_ref[...], total[4:8]]
    both = jnp.concatenate(block + block, axis=0)
    send_ref[...] = (
        jnp.broadcast_to(both[None], (PEERS // 2, 2 * SUMS, LANES))
        .reshape(PEERS * SUMS, LANES)
        .astype(BF16)
    )


def spread_kernel(
    recv_ref, grad_ready, gin, gmid, proj, gate, out_w,
    pair_grad_ref, gin_ref, proj_ref, gate_ref, gmid_ref, out_ref,
    rows, gin_own, proj_own, gate_own, gmid_own, out_own, sems,
):
    copies = []

    def give(own, ref):
        copies.append(pltpu.make_async_copy(own, ref, sems.at[len(copies)]))
        copies[-1].start()

    give(grad_ready, pair_grad_ref)
    rows[...] = recv_ref[...].astype(F32) * (1.0 / TOKENS)
    lane = lane_index(C)
    totals = jnp.zeros((C, LANES), F32)
    for m in range(2):
        gated = rows[pl.ds(8 + m, C, SUMS), :]
        mixed = rows[pl.ds(10 + m, C, SUMS), :]
        total = gated * gate[m].astype(F32)
        for e in range(4):
            part = rows[pl.ds(4 * m + e, C, SUMS), :]
            proj_own[m, :, tile(e)] = part
            total = total + part * proj[m, :, tile(e)].astype(F32)
        give(proj_own.at[m], proj_ref.at[m])
        gate_own[m] = gated
        out_own[m] = mixed
        total_in = jnp.sum(total, axis=1, keepdims=True)
        total_mid = jnp.sum(mixed * out_w[m].astype(F32), axis=1, keepdims=True)
        totals = jnp.where(lane == m, total_in, jnp.where(lane == 2 + m, total_mid, totals))
    give(gate_own, gate_ref)
    give(out_own, out_ref)
    turned = totals.T
    gin_own[...] = turned[0:2] / gin[...]
    gmid_own[...] = turned[2:4] / gmid[...]
    give(gin_own, gin_ref)
    give(gmid_own, gmid_ref)
    for copy in copies:
        copy.wait()


def run(kernel, outs, scratch, args, away=()):
    spaces = [pl.ANY if k in away else pltpu.VMEM for k in range(len(outs))]
    return pl.pallas_call(
        kernel,
        out_shape=[jax.ShapeDtypeStruct(shape, dtype) for shape, dtype in outs],
        in_specs=[pl.BlockSpec(memory_space=pltpu.VMEM)] * len(args),
        out_specs=[pl.BlockSpec(memory_space=space) for space in spaces],
        scratch_shapes=[
            pltpu.VMEM(shape, dtype) if shape else pltpu.SemaphoreType.DMA(dtype)
            for shape, dtype in scratch
        ],
        compiler_params=pltpu.CompilerParams(vmem_limit_bytes=16 * 1024 * 1024),
        cost_estimate=pl.CostEstimate(flops=10**9, bytes_accessed=2**20, transcendentals=2**18),
    )(*args)


def exchange(values, rows):
    return lax.all_to_all(
        values.reshape(-1, rows, LANES), AXES, 0, 0, tiled=True
    ).reshape(values.shape)


def local(pair_in, token_mask, cotangent, gain_in, proj_w, gate_w, gain_mid, out_w):
    operand = ((PEERS * 8, LANES), BF16)
    single = ((PEERS * 4, LANES), BF16)
    sums = (PEERS * SUMS, LANES)
    plane = ((C, PLACE), F32)
    plane_b = ((C, PLACE), BF16)
    four = (4 * C, PLACE)
    scales = ((8, PLACE), F32)
    square = ((TOKENS, TOKENS), BF16)
    spare = ((PEERS * 8, LANES), F32)
    pairs = ((PLACE, C), F32)
    mixed = ((PEERS * 4, LANES), F32)
    half = ((2, TOKENS, LANES), F32)
    pair_shape = ((ROWS, COLS, C), BF16)

    saved = [plane, scales, plane_b, (four, F32), plane, plane_b]
    places = run(place_kernel, [((TOKENS, PLACE), BF16)] * 2, [], ())
    (
        send, unit0, scale0, normed0, fact0, gating0, x0,
        proj, gate, out, gin, gmid, proj_t, gate_t, out_t, valid,
    ) = run(
        first_kernel,
        [operand]
        + saved
        + [(a.shape, a.dtype) for a in (proj_w, gate_w, out_w, gain_in, gain_mid)]
        + [((2, 4 * C, C), BF16), ((2, C, C), BF16), ((2, C, C), BF16)]
        + [scales],
        [spare, pairs],
        (
            *places, token_mask.reshape(1, TOKENS), pair_in,
            proj_w, gate_w, out_w, gain_in, gain_mid,
        ),
    )
    send, left0, right0 = run(outgoing_kernel, [single, square, square], [half], (exchange(send, 8),))
    (
        send, unit1, scale1, normed1, fact1, gating1, x1,
        mix_unit0, mix_scale0, mix_normed0, gate_fact0,
    ) = run(
        middle_kernel, [operand] + saved + [plane, scales, plane_b, plane], [spare, mixed],
        (exchange(send, 4), x0, gating0, valid, gin, gmid, proj_t, gate_t, out_t),
    )
    send, left1, right1 = run(
        incoming_kernel, [single, square, square], [half], (exchange(send, 8),)
    )
    ready_out, send, grad1, d_gated1, weights1 = run(
        turn_kernel, [pair_shape, single, plane, plane, ((2, C, C), F32)],
        [mixed, pairs, plane_b, plane_b, plane_b],
        (exchange(send, 4), x1, gating1, normed1, cotangent, gmid, gate, out, out_t),
    )
    (send,) = run(
        incoming_back_kernel, [operand], [half, square],
        (exchange(send, 4), left1, right1),
    )
    send, grad0, d_gated0, keep, pair_out = run(
        both_back_kernel, [operand, plane, plane, ((4, C, C), F32), pair_shape],
        [spare, (four, BF16), plane_b, plane_b, (None, ())],
        (
            exchange(send, 8), fact1, d_gated1, unit1, scale1, grad1, normed1, weights1,
            gating0, mix_unit0, mix_scale0, mix_normed0, gate_fact0, normed0,
            gin, gmid, proj, gate, out, ready_out,
        ),
        (4,),
    )
    send, sums1 = run(
        outgoing_back_kernel, [operand, ((4, LANES), F32)],
        [spare, half, ((2, TOKENS, TOKENS), BF16)],
        (exchange(send, 8), left0, right0),
    )
    send, ready_grad = run(
        last_back_kernel, [operand, pair_shape], [spare, (four, BF16), pairs],
        (exchange(send, 8), fact0, normed0, keep, d_gated0, unit0, scale0, grad0, gin, proj),
    )
    (send,) = run(collect_kernel, [(sums, BF16)], [], (exchange(send, 8), sums1))
    grads = [(a.shape, F32) for a in (gain_in, proj_w, gate_w, gain_mid, out_w)]
    pair_grad, gin_grad, proj_grad, gate_grad, gmid_grad, out_grad = run(
        spread_kernel, [pair_shape] + grads, [(sums, F32)] + grads + [(None, (7,))],
        (exchange(send, 4), ready_grad, gin, gmid, proj, gate, out),
        range(6),
    )
    return pair_out, pair_grad, gin_grad, proj_grad, gate_grad, gmid_grad, out_grad


def solution(mesh):
    placed = (P("row", "col", None), P(), P("row", "col", None), P(), P(), P(), P(), P())
    return jax.shard_map(
        local,
        mesh=mesh,
        in_specs=placed,
        out_specs=(P("row", "col", None), P("row", "col", None), P(), P(), P(), P(), P()),
        check_vma=False,
    )
```

```python
import jax
import jax.numpy as jnp
from jax import lax
from jax.experimental import pallas as pl
from jax.experimental.pallas import tpu as pltpu
from jax.sharding import PartitionSpec as P

F32 = jnp.float32
BF16 = jnp.bfloat16
C = 128
LANES = 128
ROWS = 32
COLS = 16
TOKENS = 256
PLACE = ROWS * COLS
TILES = PLACE // LANES
PEERS = 128
AXES = ("row", "col")
SUMS = 12


def mm(a, b, a_dim, b_dim):
    return lax.dot_general(
        a.astype(BF16), b.astype(BF16), (((a_dim,), (b_dim,)), ((), ())), preferred_element_type=F32
    )


WIDE = PLACE // 2


def wide(h):
    return pl.ds(h * WIDE, WIDE)


def inner(h):
    return [(2 * h + k, slice(k * LANES, (k + 1) * LANES)) for k in range(2)]


def tile(t):
    return pl.ds(t * LANES, LANES)


def lane_index(rows):
    return lax.broadcasted_iota(jnp.int32, (rows, LANES), 1)


def swap_slots(parts):
    lane = lane_index(parts[0].shape[0])
    low = lane < 64
    even = (lane // 32) % 2 == 0
    turned = [pltpu.roll(part, 64, 1) for part in parts]
    first = [
        jnp.where(low, parts[0], turned[2]),
        jnp.where(low, parts[1], turned[3]),
        jnp.where(low, turned[0], parts[2]),
        jnp.where(low, turned[1], parts[3]),
    ]
    result = []
    for base in (0, 2):
        result.append(jnp.where(even, first[base], pltpu.roll(first[base + 1], 32, 1)))
        result.append(jnp.where(even, pltpu.roll(first[base], 96, 1), first[base + 1]))
    return result


def as_column(gain_ref, layer):
    return jnp.broadcast_to(gain_ref[pl.ds(layer, 1), :], (LANES, LANES)).T


def standardize(values):
    average = jnp.mean(values, axis=0, keepdims=True)
    centered = values - average
    variance = jnp.mean(centered * centered, axis=0, keepdims=True)
    scale = lax.rsqrt(variance + 1e-05)
    return centered * scale, scale


def standardize_back(d_unit, unit, scale):
    mean_d = jnp.mean(d_unit, axis=0, keepdims=True)
    mean_du = jnp.mean(d_unit * unit, axis=0, keepdims=True)
    return scale * (d_unit - mean_d - unit * mean_du)


def pairs_to_lanes(pairs_ref, spare):
    spare[...] = pairs_ref[...].astype(F32).reshape(PLACE, C)
    tiles = []
    for t in range(TILES):
        block = jnp.concatenate(
            [spare[pl.ds(4 * t + q, ROWS, COLS), :] for q in range(4)], axis=0
        )
        tiles.append(block.T)
    return tiles


def lanes_to_pairs(tiles, pairs_ref, spare):
    for t in range(TILES):
        block = tiles[t].T
        for q in range(4):
            spare[pl.ds(4 * t + q, ROWS, COLS), :] = block[q * ROWS : (q + 1) * ROWS, :]
    pairs_ref[...] = spare[...].reshape(ROWS, COLS, C).astype(pairs_ref.dtype)


def put_operands(t, left, right, spare):
    low = lane_index(C) < 64
    spare[pl.ds(2 * t, C, 8), :] = jnp.where(low, left, pltpu.roll(right, 64, 1))
    spare[pl.ds(2 * t + 1, C, 8), :] = jnp.where(low, pltpu.roll(left, 64, 1), right)


def get_operands(t, spare):
    low = lane_index(C) < 64
    even = spare[pl.ds(2 * t, C, 8), :].astype(BF16)
    odd = spare[pl.ds(2 * t + 1, C, 8), :].astype(BF16)
    left = jnp.where(low, even, pltpu.roll(odd, 64, 1))
    right = jnp.where(low, pltpu.roll(even, 64, 1), odd)
    return left, right


def front(h, tiles, gain, proj_t, gate_t, layer, spare, saved, valid):
    unit_ref, scale_ref, normed_ref, fact_ref, gating_ref = saved
    for (t, _), values in zip(inner(h), tiles):
        unit, scale = standardize(values)
        unit_ref[:, tile(t)] = unit
        scale_ref[:, tile(t)] = jnp.broadcast_to(scale, (8, LANES))
        normed_ref[:, tile(t)] = (unit * gain).astype(BF16)
    normed = normed_ref[:, wide(h)]
    parts = []
    for base in (0, 2):
        closed = mm(proj_t[layer, pl.ds(base * C, C), :], normed, 1, 0)
        value = mm(proj_t[layer, pl.ds((base + 1) * C, C), :], normed, 1, 0)
        opened = jax.nn.sigmoid(closed)
        operand = opened * value * valid
        fact_ref[pl.ds(base * C, C), wide(h)] = (operand * (1.0 - opened)).astype(BF16)
        fact_ref[pl.ds((base + 1) * C, C), wide(h)] = (opened * valid).astype(BF16)
        parts.append(operand)
    for t, piece in inner(h):
        put_operands(t, parts[0][:, piece], parts[1][:, piece], spare)
    gating_ref[:, wide(h)] = jax.nn.sigmoid(mm(gate_t[layer], normed, 1, 0))


def place_kernel(first_ref, second_ref):
    token = lax.broadcasted_iota(jnp.int32, (TOKENS, PLACE), 0)
    place = lax.broadcasted_iota(jnp.int32, (TOKENS, PLACE), 1)
    first = place % ROWS + ROWS * lax.axis_index("row")
    second = place // ROWS + COLS * lax.axis_index("col")
    first_ref[...] = (token == first).astype(F32).astype(BF16)
    second_ref[...] = (token == second).astype(F32).astype(BF16)


def first_kernel(
    first_ref, second_ref, tok, pair_ref, proj, gate, out_w, gin, gmid,
    send_ref, unit_ref, scale_ref, normed_ref, fact_ref, gating_ref, x_ref,
    proj_out, gate_out, out_out, gin_out, gmid_out, proj_t, gate_t, out_t,
    valid_ref, spare, pairs,
):
    token = jnp.broadcast_to(tok[...].astype(F32), (8, TOKENS))
    valid_ref[...] = mm(token, first_ref[...], 1, 0) * mm(token, second_ref[...], 1, 0)
    for m in range(2):
        proj_t[m] = proj[m].T
        gate_t[m] = gate[m].T
        out_t[m] = out_w[m].T
    gain = as_column(gin, 0)
    tiles = pairs_to_lanes(pair_ref, pairs)
    saved = (unit_ref, scale_ref, normed_ref, fact_ref, gating_ref)
    for t in range(TILES):
        x_ref[:, tile(t)] = tiles[t].astype(BF16)
    for h in range(2):
        valid = valid_ref[pl.ds(0, 1), wide(h)]
        front(h, tiles[2 * h : 2 * h + 2], gain, proj_t, gate_t, 0, spare, saved, valid)
    send_ref[...] = spare[...].astype(BF16)
    for given, kept in (
        (proj, proj_out), (gate, gate_out), (out_w, out_out),
        (gin, gin_out), (gmid, gmid_out),
    ):
        kept[...] = given[...]


def middle_kernel(
    mix_ref, x_ref, gating0_ref, valid_ref, gin, gmid, proj_t, gate_t, out_t,
    send_ref, unit_ref, scale_ref, normed_ref, fact_ref, gating_ref, next_ref,
    mix_unit_ref, mix_scale_ref, mix_normed_ref, gate_fact_ref, spare, mixed,
):
    mixed[...] = mix_ref[...].astype(F32)
    gain_a = as_column(gmid, 0)
    gain_b = as_column(gin, 1)
    saved = (unit_ref, scale_ref, normed_ref, fact_ref, gating_ref)
    updates = []
    for h in range(2):
        for t, _ in inner(h):
            unit, scale = standardize(mixed[pl.ds(t, C, TILES), :])
            mix_unit_ref[:, tile(t)] = unit
            mix_scale_ref[:, tile(t)] = jnp.broadcast_to(scale, (8, LANES))
            mix_normed_ref[:, tile(t)] = (unit * gain_a).astype(BF16)
        updates.append(mm(out_t[0], mix_normed_ref[:, wide(h)], 1, 0))
    for h in range(2):
        tiles = []
        for t, piece in inner(h):
            gating = gating0_ref[:, tile(t)]
            gated = updates[h][:, piece] * gating
            rounded = (x_ref[:, tile(t)].astype(F32) + gated).astype(BF16)
            next_ref[:, tile(t)] = rounded
            gate_fact_ref[:, tile(t)] = gated * (1.0 - gating)
            tiles.append(rounded.astype(F32))
        valid = valid_ref[pl.ds(0, 1), wide(h)]
        front(h, tiles, gain_b, proj_t, gate_t, 1, spare, saved, valid)
    send_ref[...] = spare[...].astype(BF16)


def turn_kernel(
    mix_ref, x_ref, gating_ref, normed_ref, cot_ref, gmid, gate, out_w, out_t,
    pair_out_ref, send_ref, grad_ref, d_gated_ref, weights_ref,
    mixed, pairs, kept_n, kept_g, kept_d,
):
    mixed[...] = mix_ref[...].astype(F32)
    gain = as_column(gmid, 1)
    cot = pairs_to_lanes(cot_ref, pairs)
    units, d_normed, update = [], [], []
    for h in range(2):
        for t, _ in inner(h):
            units.append(standardize(mixed[pl.ds(t, C, TILES), :]))
            kept_n[:, tile(t)] = (units[t][0] * gain).astype(BF16)
            grad_ref[:, tile(t)] = cot[t]
            kept_d[:, tile(t)] = (cot[t] * gating_ref[:, tile(t)]).astype(BF16)
        d_normed.append(mm(out_w[1], kept_d[:, wide(h)], 1, 0))
        update.append(mm(out_t[1], kept_n[:, wide(h)], 1, 0))
    outs = []
    for h in range(2):
        for t, piece in inner(h):
            mixed[pl.ds(t, C, TILES), :] = standardize_back(d_normed[h][:, piece] * gain, *units[t])
            gating = gating_ref[:, tile(t)]
            gated = update[h][:, piece] * gating
            outs.append(x_ref[:, tile(t)].astype(F32) + gated)
            kept_g[:, tile(t)] = (cot[t] * gated * (1.0 - gating)).astype(BF16)
    d_gated_ref[...] = mm(gate[1], kept_g[...], 1, 0)
    send_ref[...] = mixed[...].astype(BF16)
    weights_ref[0] = mm(normed_ref[...], kept_g[...], 1, 1)
    weights_ref[1] = mm(kept_n[...], kept_d[...], 1, 1)
    lanes_to_pairs(outs, pair_out_ref, pairs)


def projected_back(t, spare, fact_ref, kept_p):
    d_left, d_right = get_operands(t, spare)
    for part, d_out in enumerate((d_left, d_left, d_right, d_right)):
        rows = pl.ds(part * C, C)
        kept_p[rows, tile(t)] = d_out * fact_ref[rows, tile(t)]


def both_back_kernel(
    recv_ref, fact_ref, d_gated1_ref, unit_ref, scale_ref, grad_ref, normed1_ref, weights1_ref,
    gating_ref, mix_unit_ref, mix_scale_ref, mix_normed_ref, gate_fact_ref, normed0_ref,
    gin, gmid, proj, gate, out_w, out_ready,
    send_ref, next_grad_ref, d_gated_ref, keep_ref, pair_out_ref,
    spare, kept_p, kept_g, kept_d, sem,
):
    copy = pltpu.make_async_copy(out_ready, pair_out_ref, sem)
    copy.start()
    spare[...] = recv_ref[...].astype(F32)
    gain_a = as_column(gin, 1)
    gain_b = as_column(gmid, 0)
    d_normed = []
    for h in range(2):
        for t, _ in inner(h):
            projected_back(t, spare, fact_ref, kept_p)
        d_normed.append(mm(proj[1], kept_p[:, wide(h)], 1, 0) + d_gated1_ref[:, wide(h)])
    d_mid = []
    for h in range(2):
        for t, piece in inner(h):
            d_x = standardize_back(
                d_normed[h][:, piece] * gain_a,
                unit_ref[:, tile(t)],
                scale_ref[pl.ds(0, 1), tile(t)],
            )
            grad = grad_ref[:, tile(t)] + d_x
            next_grad_ref[:, tile(t)] = grad
            kept_d[:, tile(t)] = (grad * gating_ref[:, tile(t)]).astype(BF16)
            kept_g[:, tile(t)] = (grad * gate_fact_ref[:, tile(t)]).astype(BF16)
        d_mid.append(mm(out_w[0], kept_d[:, wide(h)], 1, 0))
    weights = mm(normed1_ref[...], kept_p[...], 1, 1)
    for h in range(2):
        for t, piece in inner(h):
            spare[pl.ds(t, C, 8), :] = standardize_back(
                d_mid[h][:, piece] * gain_b,
                mix_unit_ref[:, tile(t)],
                mix_scale_ref[pl.ds(0, 1), tile(t)],
            )
            spare[pl.ds(TILES + t, C, 8), :] = weights[:, t * LANES : (t + 1) * LANES]
    d_gated_ref[...] = mm(gate[0], kept_g[...], 1, 0)
    send_ref[...] = spare[...].astype(BF16)
    keep_ref[0] = mm(normed0_ref[...], kept_g[...], 1, 1)
    keep_ref[1] = weights1_ref[0]
    keep_ref[2] = mm(mix_normed_ref[...], kept_d[...], 1, 1)
    keep_ref[3] = weights1_ref[1]
    copy.wait()


def last_back_kernel(
    recv_ref, fact_ref, normed_ref, keep_ref, d_gated_ref, unit_ref, scale_ref, grad_ref, gin, proj,
    send_ref, pair_grad_ref, spare, kept_p, pairs,
):
    spare[...] = recv_ref[...].astype(F32)
    gain = as_column(gin, 0)
    outs = []
    d_normed = []
    for h in range(2):
        for t, _ in inner(h):
            projected_back(t, spare, fact_ref, kept_p)
        d_normed.append(mm(proj[0], kept_p[:, wide(h)], 1, 0) + d_gated_ref[:, wide(h)])
    for h in range(2):
        for t, piece in inner(h):
            d_x = standardize_back(
                d_normed[h][:, piece] * gain,
                unit_ref[:, tile(t)],
                scale_ref[pl.ds(0, 1), tile(t)],
            )
            outs.append(grad_ref[:, tile(t)] + d_x)
    normed = normed_ref[...]
    for e in range(4):
        spare[pl.ds(e, C, 8), :] = mm(normed, kept_p[tile(e), :], 1, 1)
        spare[pl.ds(4 + e, C, 8), :] = keep_ref[e]
    send_ref[...] = spare[...].astype(BF16)
    lanes_to_pairs(outs, pair_grad_ref, pairs)


def whole(spare, first):
    return jnp.concatenate([spare[first], spare[first + 1]], axis=1)


def halves(hi, q):
    return pl.ds(q * LANES, LANES), tile(hi)


def second_rows(layer, q):
    return pl.ds(q, 64, 4) if layer == 0 else pl.ds((q % 2) * LANES + q // 2, 64, 2)


def take_operands(recv_ref, put):
    for hi in range(2):
        parts = [recv_ref[pl.ds((4 * hi + lo) * LANES, LANES), :] for lo in range(4)]
        for slot, block in enumerate(swap_slots(parts)):
            put(hi, slot, block)


def send_operands(send_ref, get):
    for hi in range(2):
        parts = [get(hi, slot) for slot in range(4)]
        for lo, block in enumerate(swap_slots(parts)):
            send_ref[pl.ds((4 * hi + lo) * LANES, LANES), :] = block


def send_mixture(layer, mixture, send_ref, spare):
    for hi in range(2):
        spare[hi] = mixture(hi)
    for hi in range(2):
        parts = [spare[hi, second_rows(layer, q), :].astype(BF16) for q in range(4)]
        for lo, block in enumerate(swap_slots(parts)):
            send_ref[pl.ds((4 * hi + lo) * 64, 64), :] = block


def outgoing_kernel(recv_ref, send_ref, left_ref, right_ref, spare):
    def put(hi, slot, block):
        (left_ref if slot < 2 else right_ref)[halves(hi, slot % 2)] = block

    take_operands(recv_ref, put)
    right = right_ref[...]
    send_mixture(0, lambda hi: mm(right, left_ref[:, tile(hi)], 0, 0), send_ref, spare)


def incoming_kernel(recv_ref, send_ref, left_ref, right_ref, spare):
    def put(hi, slot, block):
        if slot < 2:
            spare[hi, pl.ds(slot, LANES, 2), :] = block.astype(F32)
        else:
            right_ref[halves(hi, slot % 2)] = block

    take_operands(recv_ref, put)
    left = whole(spare, 0).astype(BF16)
    left_ref[...] = left
    mixture = mm(right_ref[...], left, 1, 1)
    send_mixture(1, lambda hi: mixture[:, hi * LANES : (hi + 1) * LANES], send_ref, spare)


def incoming_back_kernel(recv_ref, left_ref, right_ref, send_ref, spare, d_rows):
    for hi in range(2):
        parts = [recv_ref[pl.ds((4 * hi + lo) * 64, 64), :] for lo in range(4)]
        for q, block in enumerate(swap_slots(parts)):
            spare[hi, second_rows(1, q), :] = block.astype(F32)
    d_mix = whole(spare, 0).astype(BF16)
    d_left = mm(d_mix, right_ref[...], 0, 0)
    d_rows[...] = mm(d_mix, left_ref[...], 1, 0).astype(BF16)
    for hi in range(2):
        spare[hi] = d_left[:, hi * LANES : (hi + 1) * LANES]

    def get(hi, slot):
        if slot < 2:
            return spare[hi, pl.ds(slot, LANES, 2), :].astype(BF16)
        return d_rows[halves(hi, slot % 2)]

    send_operands(send_ref, get)


def outgoing_back_kernel(
    recv_ref, left_ref, right_ref, send_ref, sums_ref, arrived, spare, d_rows
):
    arrived[...] = recv_ref[...].astype(F32)
    for hi in range(2):
        parts = [
            jnp.concatenate(
                [arrived[pl.ds((4 * hi + lo) * LANES + jm, COLS, 8), :] for jm in range(4)], axis=0
            ).astype(BF16)
            for lo in range(4)
        ]
        for q, block in enumerate(swap_slots(parts)):
            for jm in range(4):
                spare[hi, pl.ds(4 * jm + q, COLS, COLS), :] = block[
                    jm * COLS : (jm + 1) * COLS, :
                ].astype(F32)
    d_mix = whole(spare, 0).astype(BF16)
    d_rows[0] = mm(right_ref[...], d_mix, 1, 0).astype(BF16)
    d_rows[1] = mm(left_ref[...], d_mix, 1, 1).astype(BF16)

    def get(hi, slot):
        rows, lanes = halves(hi, slot % 2)
        return d_rows[slot // 2, rows, lanes]

    send_operands(send_ref, get)
    total = jnp.sum(recv_ref[...].astype(F32).reshape(PEERS, 8, LANES), axis=0)
    sums_ref[...] = total[TILES:]


def collect_kernel(recv_ref, sums_ref, send_ref):
    parts = recv_ref[...].astype(F32).reshape(PEERS, 8, LANES)
    while parts.shape[0] > 1:
        middle = parts.shape[0] // 2
        parts = parts[:middle] + parts[middle:]
    total = parts[0]
    block = [total[0:4], sums_ref[...], total[4:8]]
    both = jnp.concatenate(block + block, axis=0)
    send_ref[...] = (
        jnp.broadcast_to(both[None], (PEERS // 2, 2 * SUMS, LANES))
        .reshape(PEERS * SUMS, LANES)
        .astype(BF16)
    )


def spread_kernel(
    recv_ref, grad_ready, gin, gmid, proj, gate, out_w,
    pair_grad_ref, gin_ref, proj_ref, gate_ref, gmid_ref, out_ref,
    rows, gin_own, proj_own, gate_own, gmid_own, out_own, sems,
):
    copies = []

    def give(own, ref):
        copies.append(pltpu.make_async_copy(own, ref, sems.at[len(copies)]))
        copies[-1].start()

    give(grad_ready, pair_grad_ref)
    rows[...] = recv_ref[...].astype(F32) * (1.0 / TOKENS)
    lane = lane_index(C)
    totals = jnp.zeros((C, LANES), F32)
    for m in range(2):
        gated = rows[pl.ds(8 + m, C, SUMS), :]
        mixed = rows[pl.ds(10 + m, C, SUMS), :]
        total = gated * gate[m].astype(F32)
        for e in range(4):
            part = rows[pl.ds(4 * m + e, C, SUMS), :]
            proj_own[m, :, tile(e)] = part
            total = total + part * proj[m, :, tile(e)].astype(F32)
        give(proj_own.at[m], proj_ref.at[m])
        gate_own[m] = gated
        out_own[m] = mixed
        total_in = jnp.sum(total, axis=1, keepdims=True)
        total_mid = jnp.sum(mixed * out_w[m].astype(F32), axis=1, keepdims=True)
        totals = jnp.where(lane == m, total_in, jnp.where(lane == 2 + m, total_mid, totals))
    give(gate_own, gate_ref)
    give(out_own, out_ref)
    turned = totals.T
    gin_own[...] = turned[0:2] / gin[...]
    gmid_own[...] = turned[2:4] / gmid[...]
    give(gin_own, gin_ref)
    give(gmid_own, gmid_ref)
    for copy in copies:
        copy.wait()


def run(kernel, outs, scratch, args, away=()):
    spaces = [pl.ANY if k in away else pltpu.VMEM for k in range(len(outs))]
    return pl.pallas_call(
        kernel,
        out_shape=[jax.ShapeDtypeStruct(shape, dtype) for shape, dtype in outs],
        in_specs=[pl.BlockSpec(memory_space=pltpu.VMEM)] * len(args),
        out_specs=[pl.BlockSpec(memory_space=space) for space in spaces],
        scratch_shapes=[
            pltpu.VMEM(shape, dtype) if shape else pltpu.SemaphoreType.DMA(dtype)
            for shape, dtype in scratch
        ],
        compiler_params=pltpu.CompilerParams(vmem_limit_bytes=16 * 1024 * 1024),
        cost_estimate=pl.CostEstimate(flops=10**9, bytes_accessed=2**20, transcendentals=2**18),
    )(*args)


def exchange(values, rows):
    return lax.all_to_all(
        values.reshape(-1, rows, LANES), AXES, 0, 0, tiled=True
    ).reshape(values.shape)


def local(pair_in, token_mask, cotangent, gain_in, proj_w, gate_w, gain_mid, out_w):
    operand = ((PEERS * 8, LANES), BF16)
    single = ((PEERS * 4, LANES), BF16)
    sums = (PEERS * SUMS, LANES)
    plane = ((C, PLACE), F32)
    plane_b = ((C, PLACE), BF16)
    four = (4 * C, PLACE)
    scales = ((8, PLACE), F32)
    square = ((TOKENS, TOKENS), BF16)
    spare = ((PEERS * 8, LANES), F32)
    pairs = ((PLACE, C), F32)
    mixed = ((PEERS * 4, LANES), F32)
    half = ((2, TOKENS, LANES), F32)
    pair_shape = ((ROWS, COLS, C), BF16)

    saved = [plane, scales, plane_b, (four, BF16), plane, plane_b]
    places = run(place_kernel, [((TOKENS, PLACE), BF16)] * 2, [], ())
    (
        send, unit0, scale0, normed0, fact0, gating0, x0,
        proj, gate, out, gin, gmid, proj_t, gate_t, out_t, valid,
    ) = run(
        first_kernel,
        [operand]
        + saved
        + [(a.shape, a.dtype) for a in (proj_w, gate_w, out_w, gain_in, gain_mid)]
        + [((2, 4 * C, C), BF16), ((2, C, C), BF16), ((2, C, C), BF16)]
        + [scales],
        [spare, pairs],
        (
            *places, token_mask.reshape(1, TOKENS), pair_in,
            proj_w, gate_w, out_w, gain_in, gain_mid,
        ),
    )
    send, left0, right0 = run(outgoing_kernel, [single, square, square], [half], (exchange(send, 8),))
    (
        send, unit1, scale1, normed1, fact1, gating1, x1,
        mix_unit0, mix_scale0, mix_normed0, gate_fact0,
    ) = run(
        middle_kernel, [operand] + saved + [plane, scales, plane_b, plane], [spare, mixed],
        (exchange(send, 4), x0, gating0, valid, gin, gmid, proj_t, gate_t, out_t),
    )
    send, left1, right1 = run(
        incoming_kernel, [single, square, square], [half], (exchange(send, 8),)
    )
    ready_out, send, grad1, d_gated1, weights1 = run(
        turn_kernel, [pair_shape, single, plane, plane, ((2, C, C), F32)],
        [mixed, pairs, plane_b, plane_b, plane_b],
        (exchange(send, 4), x1, gating1, normed1, cotangent, gmid, gate, out, out_t),
    )
    (send,) = run(
        incoming_back_kernel, [operand], [half, square],
        (exchange(send, 4), left1, right1),
    )
    send, grad0, d_gated0, keep, pair_out = run(
        both_back_kernel, [operand, plane, plane, ((4, C, C), F32), pair_shape],
        [spare, (four, BF16), plane_b, plane_b, (None, ())],
        (
            exchange(send, 8), fact1, d_gated1, unit1, scale1, grad1, normed1, weights1,
            gating0, mix_unit0, mix_scale0, mix_normed0, gate_fact0, normed0,
            gin, gmid, proj, gate, out, ready_out,
        ),
        (4,),
    )
    send, sums1 = run(
        outgoing_back_kernel, [operand, ((4, LANES), F32)],
        [spare, half, ((2, TOKENS, TOKENS), BF16)],
        (exchange(send, 8), left0, right0),
    )
    send, ready_grad = run(
        last_back_kernel, [operand, pair_shape], [spare, (four, BF16), pairs],
        (exchange(send, 8), fact0, normed0, keep, d_gated0, unit0, scale0, grad0, gin, proj),
    )
    (send,) = run(collect_kernel, [(sums, BF16)], [], (exchange(send, 8), sums1))
    grads = [(a.shape, F32) for a in (gain_in, proj_w, gate_w, gain_mid, out_w)]
    pair_grad, gin_grad, proj_grad, gate_grad, gmid_grad, out_grad = run(
        spread_kernel, [pair_shape] + grads, [(sums, F32)] + grads + [(None, (7,))],
        (exchange(send, 4), ready_grad, gin, gmid, proj, gate, out),
        range(6),
    )
    return pair_out, pair_grad, gin_grad, proj_grad, gate_grad, gmid_grad, out_grad


def solution(mesh):
    placed = (P("row", "col", None), P(), P("row", "col", None), P(), P(), P(), P(), P())
    return jax.shard_map(
        local,
        mesh=mesh,
        in_specs=placed,
        out_specs=(P("row", "col", None), P("row", "col", None), P(), P(), P(), P(), P()),
        check_vma=False,
    )
```

```python
import jax
import jax.numpy as jnp
from jax import lax
from jax.experimental import pallas as pl
from jax.experimental.pallas import tpu as pltpu
from jax.sharding import PartitionSpec as P

F32 = jnp.float32
BF16 = jnp.bfloat16
C = 128
LANES = 128
ROWS = 32
COLS = 16
TOKENS = 256
PLACE = ROWS * COLS
TILES = PLACE // LANES
PEERS = 128
AXES = ("row", "col")
SUMS = 12


def mm(a, b, a_dim, b_dim):
    return lax.dot_general(
        a.astype(BF16), b.astype(BF16), (((a_dim,), (b_dim,)), ((), ())), preferred_element_type=F32
    )


WIDE = PLACE // 2


def wide(h):
    return pl.ds(h * WIDE, WIDE)


def inner(h):
    return [(2 * h + k, slice(k * LANES, (k + 1) * LANES)) for k in range(2)]


def tile(t):
    return pl.ds(t * LANES, LANES)


def lane_index(rows):
    return lax.broadcasted_iota(jnp.int32, (rows, LANES), 1)


def swap_slots(parts):
    lane = lane_index(parts[0].shape[0])
    low = lane < 64
    even = (lane // 32) % 2 == 0
    turned = [pltpu.roll(part, 64, 1) for part in parts]
    first = [
        jnp.where(low, parts[0], turned[2]),
        jnp.where(low, parts[1], turned[3]),
        jnp.where(low, turned[0], parts[2]),
        jnp.where(low, turned[1], parts[3]),
    ]
    result = []
    for base in (0, 2):
        result.append(jnp.where(even, first[base], pltpu.roll(first[base + 1], 32, 1)))
        result.append(jnp.where(even, pltpu.roll(first[base], 96, 1), first[base + 1]))
    return result


def as_column(gain_ref, layer):
    return jnp.broadcast_to(gain_ref[pl.ds(layer, 1), :], (LANES, LANES)).T


def standardize(values):
    average = jnp.mean(values, axis=0, keepdims=True)
    centered = values - average
    variance = jnp.mean(centered * centered, axis=0, keepdims=True)
    scale = lax.rsqrt(variance + 1e-05)
    return centered * scale, scale


def standardize_back(d_unit, unit, scale):
    mean_d = jnp.mean(d_unit, axis=0, keepdims=True)
    mean_du = jnp.mean(d_unit * unit, axis=0, keepdims=True)
    return scale * (d_unit - mean_d - unit * mean_du)


def pairs_to_lanes(pairs_ref, spare):
    spare[...] = pairs_ref[...].astype(F32).reshape(PLACE, C)
    tiles = []
    for t in range(TILES):
        block = jnp.concatenate(
            [spare[pl.ds(4 * t + q, ROWS, COLS), :] for q in range(4)], axis=0
        )
        tiles.append(block.T)
    return tiles


def lanes_to_pairs(tiles, pairs_ref, spare):
    for t in range(TILES):
        block = tiles[t].T
        for q in range(4):
            spare[pl.ds(4 * t + q, ROWS, COLS), :] = block[q * ROWS : (q + 1) * ROWS, :]
    pairs_ref[...] = spare[...].reshape(ROWS, COLS, C).astype(pairs_ref.dtype)


def put_operands(t, left, right, spare):
    low = lane_index(C) < 64
    spare[pl.ds(2 * t, C, 8), :] = jnp.where(low, left, pltpu.roll(right, 64, 1))
    spare[pl.ds(2 * t + 1, C, 8), :] = jnp.where(low, pltpu.roll(left, 64, 1), right)


def get_operands(t, spare):
    low = lane_index(C) < 64
    even = spare[pl.ds(2 * t, C, 8), :]
    odd = spare[pl.ds(2 * t + 1, C, 8), :]
    left = jnp.where(low, even, pltpu.roll(odd, 64, 1))
    right = jnp.where(low, pltpu.roll(even, 64, 1), odd)
    return left, right


def front(h, tiles, gain, proj_t, gate_t, layer, spare, saved, valid):
    unit_ref, scale_ref, normed_ref, fact_ref, gating_ref = saved
    for (t, _), values in zip(inner(h), tiles):
        unit, scale = standardize(values)
        unit_ref[:, tile(t)] = unit
        scale_ref[:, tile(t)] = jnp.broadcast_to(scale, (8, LANES))
        normed_ref[:, tile(t)] = (unit * gain).astype(BF16)
    normed = normed_ref[:, wide(h)]
    parts = []
    for base in (0, 2):
        closed = mm(proj_t[layer, pl.ds(base * C, C), :], normed, 1, 0)
        value = mm(proj_t[layer, pl.ds((base + 1) * C, C), :], normed, 1, 0)
        opened = jax.nn.sigmoid(closed)
        operand = opened * value * valid
        fact_ref[pl.ds(base * C, C), wide(h)] = operand * (1.0 - opened)
        fact_ref[pl.ds((base + 1) * C, C), wide(h)] = opened * valid
        parts.append(operand)
    for t, piece in inner(h):
        put_operands(t, parts[0][:, piece], parts[1][:, piece], spare)
    gating_ref[:, wide(h)] = jax.nn.sigmoid(mm(gate_t[layer], normed, 1, 0))


def place_kernel(first_ref, second_ref):
    token = lax.broadcasted_iota(jnp.int32, (TOKENS, PLACE), 0)
    place = lax.broadcasted_iota(jnp.int32, (TOKENS, PLACE), 1)
    first = place % ROWS + ROWS * lax.axis_index("row")
    second = place // ROWS + COLS * lax.axis_index("col")
    first_ref[...] = (token == first).astype(F32).astype(BF16)
    second_ref[...] = (token == second).astype(F32).astype(BF16)


def first_kernel(
    first_ref, second_ref, tok, pair_ref, proj, gate, out_w, gin, gmid,
    send_ref, unit_ref, scale_ref, normed_ref, fact_ref, gating_ref, x_ref,
    proj_out, gate_out, out_out, gin_out, gmid_out, proj_t, gate_t, out_t,
    valid_ref, spare, pairs,
):
    token = jnp.broadcast_to(tok[...].astype(F32), (8, TOKENS))
    valid_ref[...] = mm(token, first_ref[...], 1, 0) * mm(token, second_ref[...], 1, 0)
    for m in range(2):
        proj_t[m] = proj[m].T
        gate_t[m] = gate[m].T
        out_t[m] = out_w[m].T
    gain = as_column(gin, 0)
    tiles = pairs_to_lanes(pair_ref, pairs)
    saved = (unit_ref, scale_ref, normed_ref, fact_ref, gating_ref)
    for t in range(TILES):
        x_ref[:, tile(t)] = tiles[t].astype(BF16)
    for h in range(2):
        valid = valid_ref[pl.ds(0, 1), wide(h)]
        front(h, tiles[2 * h : 2 * h + 2], gain, proj_t, gate_t, 0, spare, saved, valid)
    send_ref[...] = spare[...].astype(BF16)
    for given, kept in (
        (proj, proj_out), (gate, gate_out), (out_w, out_out),
        (gin, gin_out), (gmid, gmid_out),
    ):
        kept[...] = given[...]


def middle_kernel(
    mix_ref, x_ref, gating0_ref, valid_ref, gin, gmid, proj_t, gate_t, out_t,
    send_ref, unit_ref, scale_ref, normed_ref, fact_ref, gating_ref, next_ref,
    mix_unit_ref, mix_scale_ref, mix_normed_ref, gate_fact_ref, spare, mixed,
):
    mixed[...] = mix_ref[...].astype(F32)
    gain_a = as_column(gmid, 0)
    gain_b = as_column(gin, 1)
    saved = (unit_ref, scale_ref, normed_ref, fact_ref, gating_ref)
    updates = []
    for h in range(2):
        for t, _ in inner(h):
            unit, scale = standardize(mixed[pl.ds(t, C, TILES), :])
            mix_unit_ref[:, tile(t)] = unit
            mix_scale_ref[:, tile(t)] = jnp.broadcast_to(scale, (8, LANES))
            mix_normed_ref[:, tile(t)] = (unit * gain_a).astype(BF16)
        updates.append(mm(out_t[0], mix_normed_ref[:, wide(h)], 1, 0))
    for h in range(2):
        tiles = []
        for t, piece in inner(h):
            gating = gating0_ref[:, tile(t)]
            gated = updates[h][:, piece] * gating
            rounded = (x_ref[:, tile(t)].astype(F32) + gated).astype(BF16)
            next_ref[:, tile(t)] = rounded
            gate_fact_ref[:, tile(t)] = gated * (1.0 - gating)
            tiles.append(rounded.astype(F32))
        valid = valid_ref[pl.ds(0, 1), wide(h)]
        front(h, tiles, gain_b, proj_t, gate_t, 1, spare, saved, valid)
    send_ref[...] = spare[...].astype(BF16)


def turn_kernel(
    mix_ref, x_ref, gating_ref, normed_ref, cot_ref, gmid, gate, out_w, out_t,
    pair_out_ref, send_ref, grad_ref, d_gated_ref, weights_ref,
    mixed, pairs, kept_n, kept_g, kept_d,
):
    mixed[...] = mix_ref[...].astype(F32)
    gain = as_column(gmid, 1)
    cot = pairs_to_lanes(cot_ref, pairs)
    units, d_normed, update = [], [], []
    for h in range(2):
        for t, _ in inner(h):
            units.append(standardize(mixed[pl.ds(t, C, TILES), :]))
            kept_n[:, tile(t)] = (units[t][0] * gain).astype(BF16)
            grad_ref[:, tile(t)] = cot[t]
            kept_d[:, tile(t)] = (cot[t] * gating_ref[:, tile(t)]).astype(BF16)
        d_normed.append(mm(out_w[1], kept_d[:, wide(h)], 1, 0))
        update.append(mm(out_t[1], kept_n[:, wide(h)], 1, 0))
    outs = []
    for h in range(2):
        for t, piece in inner(h):
            mixed[pl.ds(t, C, TILES), :] = standardize_back(d_normed[h][:, piece] * gain, *units[t])
            gating = gating_ref[:, tile(t)]
            gated = update[h][:, piece] * gating
            outs.append(x_ref[:, tile(t)].astype(F32) + gated)
            kept_g[:, tile(t)] = (cot[t] * gated * (1.0 - gating)).astype(BF16)
    d_gated_ref[...] = mm(gate[1], kept_g[...], 1, 0)
    send_ref[...] = mixed[...].astype(BF16)
    weights_ref[0] = mm(normed_ref[...], kept_g[...], 1, 1)
    weights_ref[1] = mm(kept_n[...], kept_d[...], 1, 1)
    lanes_to_pairs(outs, pair_out_ref, pairs)


def projected_back(t, spare, fact_ref, kept_p):
    d_left, d_right = get_operands(t, spare)
    for part, d_out in enumerate((d_left, d_left, d_right, d_right)):
        rows = pl.ds(part * C, C)
        kept_p[rows, tile(t)] = (d_out * fact_ref[rows, tile(t)]).astype(BF16)


def both_back_kernel(
    recv_ref, fact_ref, d_gated1_ref, unit_ref, scale_ref, grad_ref, normed1_ref, weights1_ref,
    gating_ref, mix_unit_ref, mix_scale_ref, mix_normed_ref, gate_fact_ref, normed0_ref,
    gin, gmid, proj, gate, out_w, out_ready,
    send_ref, next_grad_ref, d_gated_ref, keep_ref, pair_out_ref,
    spare, kept_p, kept_g, kept_d, sem,
):
    copy = pltpu.make_async_copy(out_ready, pair_out_ref, sem)
    copy.start()
    spare[...] = recv_ref[...].astype(F32)
    gain_a = as_column(gin, 1)
    gain_b = as_column(gmid, 0)
    d_normed = []
    for h in range(2):
        for t, _ in inner(h):
            projected_back(t, spare, fact_ref, kept_p)
        d_normed.append(mm(proj[1], kept_p[:, wide(h)], 1, 0) + d_gated1_ref[:, wide(h)])
    d_mid = []
    for h in range(2):
        for t, piece in inner(h):
            d_x = standardize_back(
                d_normed[h][:, piece] * gain_a,
                unit_ref[:, tile(t)],
                scale_ref[pl.ds(0, 1), tile(t)],
            )
            grad = grad_ref[:, tile(t)] + d_x
            next_grad_ref[:, tile(t)] = grad
            kept_d[:, tile(t)] = (grad * gating_ref[:, tile(t)]).astype(BF16)
            kept_g[:, tile(t)] = (grad * gate_fact_ref[:, tile(t)]).astype(BF16)
        d_mid.append(mm(out_w[0], kept_d[:, wide(h)], 1, 0))
    normed1 = normed1_ref[...]
    for h in range(2):
        for t, piece in inner(h):
            spare[pl.ds(t, C, 8), :] = standardize_back(
                d_mid[h][:, piece] * gain_b,
                mix_unit_ref[:, tile(t)],
                mix_scale_ref[pl.ds(0, 1), tile(t)],
            )
            spare[pl.ds(TILES + t, C, 8), :] = mm(normed1, kept_p[tile(t), :], 1, 1)
    d_gated_ref[...] = mm(gate[0], kept_g[...], 1, 0)
    send_ref[...] = spare[...].astype(BF16)
    keep_ref[0] = mm(normed0_ref[...], kept_g[...], 1, 1)
    keep_ref[1] = weights1_ref[0]
    keep_ref[2] = mm(mix_normed_ref[...], kept_d[...], 1, 1)
    keep_ref[3] = weights1_ref[1]
    copy.wait()


def last_back_kernel(
    recv_ref, fact_ref, normed_ref, keep_ref, d_gated_ref, unit_ref, scale_ref, grad_ref, gin, proj,
    send_ref, pair_grad_ref, spare, kept_p, pairs,
):
    spare[...] = recv_ref[...].astype(F32)
    gain = as_column(gin, 0)
    outs = []
    d_normed = []
    for h in range(2):
        for t, _ in inner(h):
            projected_back(t, spare, fact_ref, kept_p)
        d_normed.append(mm(proj[0], kept_p[:, wide(h)], 1, 0) + d_gated_ref[:, wide(h)])
    for h in range(2):
        for t, piece in inner(h):
            d_x = standardize_back(
                d_normed[h][:, piece] * gain,
                unit_ref[:, tile(t)],
                scale_ref[pl.ds(0, 1), tile(t)],
            )
            outs.append(grad_ref[:, tile(t)] + d_x)
    normed = normed_ref[...]
    for e in range(4):
        spare[pl.ds(e, C, 8), :] = mm(normed, kept_p[tile(e), :], 1, 1)
        spare[pl.ds(4 + e, C, 8), :] = keep_ref[e]
    send_ref[...] = spare[...].astype(BF16)
    lanes_to_pairs(outs, pair_grad_ref, pairs)


def whole(spare, first):
    return jnp.concatenate([spare[first], spare[first + 1]], axis=1)


def halves(hi, q):
    return pl.ds(q * LANES, LANES), tile(hi)


def second_rows(layer, q):
    return pl.ds(q, 64, 4) if layer == 0 else pl.ds((q % 2) * LANES + q // 2, 64, 2)


def take_operands(recv_ref, put):
    for hi in range(2):
        parts = [recv_ref[pl.ds((4 * hi + lo) * LANES, LANES), :] for lo in range(4)]
        for slot, block in enumerate(swap_slots(parts)):
            put(hi, slot, block)


def send_operands(send_ref, get):
    for hi in range(2):
        parts = [get(hi, slot) for slot in range(4)]
        for lo, block in enumerate(swap_slots(parts)):
            send_ref[pl.ds((4 * hi + lo) * LANES, LANES), :] = block


def send_mixture(layer, mixture, send_ref, spare):
    for hi in range(2):
        spare[hi] = mixture(hi)
    for hi in range(2):
        parts = [spare[hi, second_rows(layer, q), :].astype(BF16) for q in range(4)]
        for lo, block in enumerate(swap_slots(parts)):
            send_ref[pl.ds((4 * hi + lo) * 64, 64), :] = block


def outgoing_kernel(recv_ref, send_ref, left_ref, right_ref, spare):
    def put(hi, slot, block):
        (left_ref if slot < 2 else right_ref)[halves(hi, slot % 2)] = block

    take_operands(recv_ref, put)
    right = right_ref[...]
    send_mixture(0, lambda hi: mm(right, left_ref[:, tile(hi)], 0, 0), send_ref, spare)


def incoming_kernel(recv_ref, send_ref, left_ref, right_ref, spare):
    def put(hi, slot, block):
        if slot < 2:
            spare[hi, pl.ds(slot, LANES, 2), :] = block.astype(F32)
        else:
            right_ref[halves(hi, slot % 2)] = block

    take_operands(recv_ref, put)
    left = whole(spare, 0).astype(BF16)
    left_ref[...] = left
    mixture = mm(right_ref[...], left, 1, 1)
    send_mixture(1, lambda hi: mixture[:, hi * LANES : (hi + 1) * LANES], send_ref, spare)


def incoming_back_kernel(recv_ref, left_ref, right_ref, send_ref, spare, d_rows):
    for hi in range(2):
        parts = [recv_ref[pl.ds((4 * hi + lo) * 64, 64), :] for lo in range(4)]
        for q, block in enumerate(swap_slots(parts)):
            spare[hi, second_rows(1, q), :] = block.astype(F32)
    d_mix = whole(spare, 0).astype(BF16)
    d_left = mm(d_mix, right_ref[...], 0, 0)
    d_rows[...] = mm(d_mix, left_ref[...], 1, 0).astype(BF16)
    for hi in range(2):
        spare[hi] = d_left[:, hi * LANES : (hi + 1) * LANES]

    def get(hi, slot):
        if slot < 2:
            return spare[hi, pl.ds(slot, LANES, 2), :].astype(BF16)
        return d_rows[halves(hi, slot % 2)]

    send_operands(send_ref, get)


def outgoing_back_kernel(
    recv_ref, left_ref, right_ref, send_ref, sums_ref, arrived, spare, d_rows
):
    arrived[...] = recv_ref[...].astype(F32)
    for hi in range(2):
        parts = [
            jnp.concatenate(
                [arrived[pl.ds((4 * hi + lo) * LANES + jm, COLS, 8), :] for jm in range(4)], axis=0
            ).astype(BF16)
            for lo in range(4)
        ]
        for q, block in enumerate(swap_slots(parts)):
            for jm in range(4):
                spare[hi, pl.ds(4 * jm + q, COLS, COLS), :] = block[
                    jm * COLS : (jm + 1) * COLS, :
                ].astype(F32)
    d_mix = whole(spare, 0).astype(BF16)
    d_rows[0] = mm(right_ref[...], d_mix, 1, 0).astype(BF16)
    d_rows[1] = mm(left_ref[...], d_mix, 1, 1).astype(BF16)

    def get(hi, slot):
        rows, lanes = halves(hi, slot % 2)
        return d_rows[slot // 2, rows, lanes]

    send_operands(send_ref, get)
    total = jnp.sum(recv_ref[...].astype(F32).reshape(PEERS, 8, LANES), axis=0)
    sums_ref[...] = total[TILES:]


def collect_kernel(recv_ref, sums_ref, send_ref):
    parts = recv_ref[...].astype(F32).reshape(PEERS, 8, LANES)
    while parts.shape[0] > 1:
        middle = parts.shape[0] // 2
        parts = parts[:middle] + parts[middle:]
    total = parts[0]
    block = [total[0:4], sums_ref[...], total[4:8]]
    both = jnp.concatenate(block + block, axis=0)
    send_ref[...] = (
        jnp.broadcast_to(both[None], (PEERS // 2, 2 * SUMS, LANES))
        .reshape(PEERS * SUMS, LANES)
        .astype(BF16)
    )


def spread_kernel(
    recv_ref, grad_ready, gin, gmid, proj, gate, out_w,
    pair_grad_ref, gin_ref, proj_ref, gate_ref, gmid_ref, out_ref,
    rows, gin_own, proj_own, gate_own, gmid_own, out_own, sems,
):
    copies = []

    def give(own, ref):
        copies.append(pltpu.make_async_copy(own, ref, sems.at[len(copies)]))
        copies[-1].start()

    give(grad_ready, pair_grad_ref)
    rows[...] = recv_ref[...].astype(F32) * (1.0 / TOKENS)
    lane = lane_index(C)
    totals = jnp.zeros((C, LANES), F32)
    for m in range(2):
        gated = rows[pl.ds(8 + m, C, SUMS), :]
        mixed = rows[pl.ds(10 + m, C, SUMS), :]
        total = gated * gate[m].astype(F32)
        for e in range(4):
            part = rows[pl.ds(4 * m + e, C, SUMS), :]
            proj_own[m, :, tile(e)] = part
            total = total + part * proj[m, :, tile(e)].astype(F32)
        give(proj_own.at[m], proj_ref.at[m])
        gate_own[m] = gated
        out_own[m] = mixed
        total_in = jnp.sum(total, axis=1, keepdims=True)
        total_mid = jnp.sum(mixed * out_w[m].astype(F32), axis=1, keepdims=True)
        totals = jnp.where(lane == m, total_in, jnp.where(lane == 2 + m, total_mid, totals))
    give(gate_own, gate_ref)
    give(out_own, out_ref)
    turned = totals.T
    gin_own[...] = turned[0:2] / gin[...]
    gmid_own[...] = turned[2:4] / gmid[...]
    give(gin_own, gin_ref)
    give(gmid_own, gmid_ref)
    for copy in copies:
        copy.wait()


def run(kernel, outs, scratch, args, away=()):
    spaces = [pl.ANY if k in away else pltpu.VMEM for k in range(len(outs))]
    return pl.pallas_call(
        kernel,
        out_shape=[jax.ShapeDtypeStruct(shape, dtype) for shape, dtype in outs],
        in_specs=[pl.BlockSpec(memory_space=pltpu.VMEM)] * len(args),
        out_specs=[pl.BlockSpec(memory_space=space) for space in spaces],
        scratch_shapes=[
            pltpu.VMEM(shape, dtype) if shape else pltpu.SemaphoreType.DMA(dtype)
            for shape, dtype in scratch
        ],
        compiler_params=pltpu.CompilerParams(vmem_limit_bytes=16 * 1024 * 1024),
        cost_estimate=pl.CostEstimate(flops=10**9, bytes_accessed=2**20, transcendentals=2**18),
    )(*args)


def exchange(values, rows):
    return lax.all_to_all(
        values.reshape(-1, rows, LANES), AXES, 0, 0, tiled=True
    ).reshape(values.shape)


def local(pair_in, token_mask, cotangent, gain_in, proj_w, gate_w, gain_mid, out_w):
    operand = ((PEERS * 8, LANES), BF16)
    single = ((PEERS * 4, LANES), BF16)
    sums = (PEERS * SUMS, LANES)
    plane = ((C, PLACE), F32)
    plane_b = ((C, PLACE), BF16)
    four = (4 * C, PLACE)
    scales = ((8, PLACE), F32)
    square = ((TOKENS, TOKENS), BF16)
    spare = ((PEERS * 8, LANES), F32)
    pairs = ((PLACE, C), F32)
    mixed = ((PEERS * 4, LANES), F32)
    half = ((2, TOKENS, LANES), F32)
    pair_shape = ((ROWS, COLS, C), BF16)

    saved = [plane, scales, plane_b, (four, F32), plane, plane_b]
    places = run(place_kernel, [((TOKENS, PLACE), BF16)] * 2, [], ())
    (
        send, unit0, scale0, normed0, fact0, gating0, x0,
        proj, gate, out, gin, gmid, proj_t, gate_t, out_t, valid,
    ) = run(
        first_kernel,
        [operand]
        + saved
        + [(a.shape, a.dtype) for a in (proj_w, gate_w, out_w, gain_in, gain_mid)]
        + [((2, 4 * C, C), BF16), ((2, C, C), BF16), ((2, C, C), BF16)]
        + [scales],
        [spare, pairs],
        (
            *places, token_mask.reshape(1, TOKENS), pair_in,
            proj_w, gate_w, out_w, gain_in, gain_mid,
        ),
    )
    send, left0, right0 = run(outgoing_kernel, [single, square, square], [half], (exchange(send, 8),))
    (
        send, unit1, scale1, normed1, fact1, gating1, x1,
        mix_unit0, mix_scale0, mix_normed0, gate_fact0,
    ) = run(
        middle_kernel, [operand] + saved + [plane, scales, plane_b, plane], [spare, mixed],
        (exchange(send, 4), x0, gating0, valid, gin, gmid, proj_t, gate_t, out_t),
    )
    send, left1, right1 = run(
        incoming_kernel, [single, square, square], [half], (exchange(send, 8),)
    )
    ready_out, send, grad1, d_gated1, weights1 = run(
        turn_kernel, [pair_shape, single, plane, plane, ((2, C, C), F32)],
        [mixed, pairs, plane_b, plane_b, plane_b],
        (exchange(send, 4), x1, gating1, normed1, cotangent, gmid, gate, out, out_t),
    )
    (send,) = run(
        incoming_back_kernel, [operand], [half, square],
        (exchange(send, 4), left1, right1),
    )
    send, grad0, d_gated0, keep, pair_out = run(
        both_back_kernel, [operand, plane, plane, ((4, C, C), F32), pair_shape],
        [spare, (four, BF16), plane_b, plane_b, (None, ())],
        (
            exchange(send, 8), fact1, d_gated1, unit1, scale1, grad1, normed1, weights1,
            gating0, mix_unit0, mix_scale0, mix_normed0, gate_fact0, normed0,
            gin, gmid, proj, gate, out, ready_out,
        ),
        (4,),
    )
    send, sums1 = run(
        outgoing_back_kernel, [operand, ((4, LANES), F32)],
        [spare, half, ((2, TOKENS, TOKENS), BF16)],
        (exchange(send, 8), left0, right0),
    )
    send, ready_grad = run(
        last_back_kernel, [operand, pair_shape], [spare, (four, BF16), pairs],
        (exchange(send, 8), fact0, normed0, keep, d_gated0, unit0, scale0, grad0, gin, proj),
    )
    (send,) = run(collect_kernel, [(sums, BF16)], [], (exchange(send, 8), sums1))
    grads = [(a.shape, F32) for a in (gain_in, proj_w, gate_w, gain_mid, out_w)]
    pair_grad, gin_grad, proj_grad, gate_grad, gmid_grad, out_grad = run(
        spread_kernel, [pair_shape] + grads, [(sums, F32)] + grads + [(None, (7,))],
        (exchange(send, 4), ready_grad, gin, gmid, proj, gate, out),
        range(6),
    )
    return pair_out, pair_grad, gin_grad, proj_grad, gate_grad, gmid_grad, out_grad


def solution(mesh):
    placed = (P("row", "col", None), P(), P("row", "col", None), P(), P(), P(), P(), P())
    return jax.shard_map(
        local,
        mesh=mesh,
        in_specs=placed,
        out_specs=(P("row", "col", None), P("row", "col", None), P(), P(), P(), P(), P()),
        check_vma=False,
    )
```

```python
import jax
import jax.numpy as jnp
from jax import lax
from jax.experimental import pallas as pl
from jax.experimental.pallas import tpu as pltpu
from jax.sharding import PartitionSpec as P

F32 = jnp.float32
BF16 = jnp.bfloat16
C = 128
LANES = 128
ROWS = 32
COLS = 16
TOKENS = 256
PLACE = ROWS * COLS
TILES = PLACE // LANES
PEERS = 128
AXES = ("row", "col")
SUMS = 12


def mm(a, b, a_dim, b_dim):
    return lax.dot_general(
        a.astype(BF16), b.astype(BF16), (((a_dim,), (b_dim,)), ((), ())), preferred_element_type=F32
    )


WIDE = PLACE // 2


def wide(h):
    return pl.ds(h * WIDE, WIDE)


def inner(h):
    return [(2 * h + k, slice(k * LANES, (k + 1) * LANES)) for k in range(2)]


def tile(t):
    return pl.ds(t * LANES, LANES)


def lane_index(rows):
    return lax.broadcasted_iota(jnp.int32, (rows, LANES), 1)


def swap_slots(parts):
    lane = lane_index(parts[0].shape[0])
    low = lane < 64
    even = (lane // 32) % 2 == 0
    turned = [pltpu.roll(part, 64, 1) for part in parts]
    first = [
        jnp.where(low, parts[0], turned[2]),
        jnp.where(low, parts[1], turned[3]),
        jnp.where(low, turned[0], parts[2]),
        jnp.where(low, turned[1], parts[3]),
    ]
    result = []
    for base in (0, 2):
        result.append(jnp.where(even, first[base], pltpu.roll(first[base + 1], 32, 1)))
        result.append(jnp.where(even, pltpu.roll(first[base], 96, 1), first[base + 1]))
    return result


def as_column(gain_ref, layer):
    return jnp.broadcast_to(gain_ref[pl.ds(layer, 1), :], (LANES, LANES)).T


def standardize(values):
    average = jnp.mean(values, axis=0, keepdims=True)
    centered = values - average
    variance = jnp.mean(centered * centered, axis=0, keepdims=True)
    scale = lax.rsqrt(variance + 1e-05)
    return centered * scale, scale


def standardize_back(d_unit, unit, scale):
    mean_d = jnp.mean(d_unit, axis=0, keepdims=True)
    mean_du = jnp.mean(d_unit * unit, axis=0, keepdims=True)
    return scale * (d_unit - mean_d - unit * mean_du)


def pairs_to_lanes(pairs_ref, spare):
    spare[...] = pairs_ref[...].astype(F32).reshape(PLACE, C)
    tiles = []
    for t in range(TILES):
        block = jnp.concatenate(
            [spare[pl.ds(4 * t + q, ROWS, COLS), :] for q in range(4)], axis=0
        )
        tiles.append(block.T)
    return tiles


def lanes_to_pairs(tiles, pairs_ref, spare):
    for t in range(TILES):
        block = tiles[t].T
        for q in range(4):
            spare[pl.ds(4 * t + q, ROWS, COLS), :] = block[q * ROWS : (q + 1) * ROWS, :]
    pairs_ref[...] = spare[...].reshape(ROWS, COLS, C).astype(pairs_ref.dtype)


def put_operands(t, left, right, spare):
    low = lane_index(C) < 64
    spare[pl.ds(2 * t, C, 8), :] = jnp.where(low, left, pltpu.roll(right, 64, 1))
    spare[pl.ds(2 * t + 1, C, 8), :] = jnp.where(low, pltpu.roll(left, 64, 1), right)


def get_operands(t, spare, dtype):
    low = lane_index(C) < 64
    even = spare[pl.ds(2 * t, C, 8), :].astype(dtype)
    odd = spare[pl.ds(2 * t + 1, C, 8), :].astype(dtype)
    left = jnp.where(low, even, pltpu.roll(odd, 64, 1))
    right = jnp.where(low, pltpu.roll(even, 64, 1), odd)
    return left, right


def front(h, tiles, gain, proj_t, gate_t, layer, spare, saved, valid):
    unit_ref, scale_ref, normed_ref, fact_ref, gating_ref = saved
    for (t, _), values in zip(inner(h), tiles):
        unit, scale = standardize(values)
        unit_ref[:, tile(t)] = unit
        scale_ref[:, tile(t)] = jnp.broadcast_to(scale, (8, LANES))
        normed_ref[:, tile(t)] = (unit * gain).astype(BF16)
    normed = normed_ref[:, wide(h)]
    parts = []
    for base in (0, 2):
        closed = mm(proj_t[layer, pl.ds(base * C, C), :], normed, 1, 0)
        value = mm(proj_t[layer, pl.ds((base + 1) * C, C), :], normed, 1, 0)
        opened = jax.nn.sigmoid(closed)
        operand = opened * value * valid
        fact_ref[pl.ds(base * C, C), wide(h)] = (operand * (1.0 - opened)).astype(fact_ref.dtype)
        fact_ref[pl.ds((base + 1) * C, C), wide(h)] = (opened * valid).astype(fact_ref.dtype)
        parts.append(operand)
    for t, piece in inner(h):
        put_operands(t, parts[0][:, piece], parts[1][:, piece], spare)
    gating_ref[:, wide(h)] = jax.nn.sigmoid(mm(gate_t[layer], normed, 1, 0))


def place_kernel(first_ref, second_ref):
    token = lax.broadcasted_iota(jnp.int32, (TOKENS, PLACE), 0)
    place = lax.broadcasted_iota(jnp.int32, (TOKENS, PLACE), 1)
    first = place % ROWS + ROWS * lax.axis_index("row")
    second = place // ROWS + COLS * lax.axis_index("col")
    first_ref[...] = (token == first).astype(F32).astype(BF16)
    second_ref[...] = (token == second).astype(F32).astype(BF16)


def first_kernel(
    first_ref, second_ref, tok, pair_ref, proj, gate, out_w, gin, gmid,
    send_ref, unit_ref, scale_ref, normed_ref, fact_ref, gating_ref, x_ref,
    proj_out, gate_out, out_out, gin_out, gmid_out, proj_t, gate_t, out_t,
    valid_ref, spare, pairs,
):
    token = jnp.broadcast_to(tok[...].astype(F32), (8, TOKENS))
    valid_ref[...] = mm(token, first_ref[...], 1, 0) * mm(token, second_ref[...], 1, 0)
    for m in range(2):
        proj_t[m] = proj[m].T
        gate_t[m] = gate[m].T
        out_t[m] = out_w[m].T
    gain = as_column(gin, 0)
    tiles = pairs_to_lanes(pair_ref, pairs)
    saved = (unit_ref, scale_ref, normed_ref, fact_ref, gating_ref)
    for t in range(TILES):
        x_ref[:, tile(t)] = tiles[t].astype(BF16)
    for h in range(2):
        valid = valid_ref[pl.ds(0, 1), wide(h)]
        front(h, tiles[2 * h : 2 * h + 2], gain, proj_t, gate_t, 0, spare, saved, valid)
    send_ref[...] = spare[...].astype(BF16)
    for given, kept in (
        (proj, proj_out), (gate, gate_out), (out_w, out_out),
        (gin, gin_out), (gmid, gmid_out),
    ):
        kept[...] = given[...]


def middle_kernel(
    mix_ref, x_ref, gating0_ref, valid_ref, gin, gmid, proj_t, gate_t, out_t,
    send_ref, unit_ref, scale_ref, normed_ref, fact_ref, gating_ref, next_ref,
    mix_unit_ref, mix_scale_ref, mix_normed_ref, gate_fact_ref, spare, mixed,
):
    mixed[...] = mix_ref[...].astype(F32)
    gain_a = as_column(gmid, 0)
    gain_b = as_column(gin, 1)
    saved = (unit_ref, scale_ref, normed_ref, fact_ref, gating_ref)
    updates = []
    for h in range(2):
        for t, _ in inner(h):
            unit, scale = standardize(mixed[pl.ds(t, C, TILES), :])
            mix_unit_ref[:, tile(t)] = unit
            mix_scale_ref[:, tile(t)] = jnp.broadcast_to(scale, (8, LANES))
            mix_normed_ref[:, tile(t)] = (unit * gain_a).astype(BF16)
        updates.append(mm(out_t[0], mix_normed_ref[:, wide(h)], 1, 0))
    for h in range(2):
        tiles = []
        for t, piece in inner(h):
            gating = gating0_ref[:, tile(t)]
            gated = updates[h][:, piece] * gating
            rounded = (x_ref[:, tile(t)].astype(F32) + gated).astype(BF16)
            next_ref[:, tile(t)] = rounded
            gate_fact_ref[:, tile(t)] = gated * (1.0 - gating)
            tiles.append(rounded.astype(F32))
        valid = valid_ref[pl.ds(0, 1), wide(h)]
        front(h, tiles, gain_b, proj_t, gate_t, 1, spare, saved, valid)
    send_ref[...] = spare[...].astype(BF16)


def turn_kernel(
    mix_ref, x_ref, gating_ref, normed_ref, cot_ref, gmid, gate, out_w, out_t,
    pair_out_ref, send_ref, grad_ref, d_gated_ref, weights_ref,
    mixed, pairs, kept_n, kept_g, kept_d,
):
    mixed[...] = mix_ref[...].astype(F32)
    gain = as_column(gmid, 1)
    cot = pairs_to_lanes(cot_ref, pairs)
    units, d_normed, update = [], [], []
    for h in range(2):
        for t, _ in inner(h):
            units.append(standardize(mixed[pl.ds(t, C, TILES), :]))
            kept_n[:, tile(t)] = (units[t][0] * gain).astype(BF16)
            grad_ref[:, tile(t)] = cot[t]
            kept_d[:, tile(t)] = (cot[t] * gating_ref[:, tile(t)]).astype(BF16)
        d_normed.append(mm(out_w[1], kept_d[:, wide(h)], 1, 0))
        update.append(mm(out_t[1], kept_n[:, wide(h)], 1, 0))
    outs = []
    for h in range(2):
        for t, piece in inner(h):
            mixed[pl.ds(t, C, TILES), :] = standardize_back(d_normed[h][:, piece] * gain, *units[t])
            gating = gating_ref[:, tile(t)]
            gated = update[h][:, piece] * gating
            outs.append(x_ref[:, tile(t)].astype(F32) + gated)
            kept_g[:, tile(t)] = (cot[t] * gated * (1.0 - gating)).astype(BF16)
    d_gated_ref[...] = mm(gate[1], kept_g[...], 1, 0)
    send_ref[...] = mixed[...].astype(BF16)
    weights_ref[0] = mm(normed_ref[...], kept_g[...], 1, 1)
    weights_ref[1] = mm(kept_n[...], kept_d[...], 1, 1)
    lanes_to_pairs(outs, pair_out_ref, pairs)


def projected_back(t, spare, fact_ref, kept_p):
    d_left, d_right = get_operands(t, spare, fact_ref.dtype)
    for part, d_out in enumerate((d_left, d_left, d_right, d_right)):
        rows = pl.ds(part * C, C)
        kept_p[rows, tile(t)] = (d_out * fact_ref[rows, tile(t)]).astype(BF16)


def both_back_kernel(
    recv_ref, fact_ref, d_gated1_ref, unit_ref, scale_ref, grad_ref, normed1_ref, weights1_ref,
    gating_ref, mix_unit_ref, mix_scale_ref, mix_normed_ref, gate_fact_ref, normed0_ref,
    gin, gmid, proj, gate, out_w, out_ready,
    send_ref, next_grad_ref, d_gated_ref, keep_ref, pair_out_ref,
    spare, kept_p, kept_g, kept_d, sem,
):
    copy = pltpu.make_async_copy(out_ready, pair_out_ref, sem)
    copy.start()
    spare[...] = recv_ref[...].astype(F32)
    gain_a = as_column(gin, 1)
    gain_b = as_column(gmid, 0)
    d_normed = []
    for h in range(2):
        for t, _ in inner(h):
            projected_back(t, spare, fact_ref, kept_p)
        d_normed.append(mm(proj[1], kept_p[:, wide(h)], 1, 0) + d_gated1_ref[:, wide(h)])
    d_mid = []
    for h in range(2):
        for t, piece in inner(h):
            d_x = standardize_back(
                d_normed[h][:, piece] * gain_a,
                unit_ref[:, tile(t)],
                scale_ref[pl.ds(0, 1), tile(t)],
            )
            grad = grad_ref[:, tile(t)] + d_x
            next_grad_ref[:, tile(t)] = grad
            kept_d[:, tile(t)] = (grad * gating_ref[:, tile(t)]).astype(BF16)
            kept_g[:, tile(t)] = (grad * gate_fact_ref[:, tile(t)]).astype(BF16)
        d_mid.append(mm(out_w[0], kept_d[:, wide(h)], 1, 0))
    normed1 = normed1_ref[...]
    for h in range(2):
        for t, piece in inner(h):
            spare[pl.ds(t, C, 8), :] = standardize_back(
                d_mid[h][:, piece] * gain_b,
                mix_unit_ref[:, tile(t)],
                mix_scale_ref[pl.ds(0, 1), tile(t)],
            )
            spare[pl.ds(TILES + t, C, 8), :] = mm(normed1, kept_p[tile(t), :], 1, 1)
    d_gated_ref[...] = mm(gate[0], kept_g[...], 1, 0)
    send_ref[...] = spare[...].astype(BF16)
    keep_ref[0] = mm(normed0_ref[...], kept_g[...], 1, 1)
    keep_ref[1] = weights1_ref[0]
    keep_ref[2] = mm(mix_normed_ref[...], kept_d[...], 1, 1)
    keep_ref[3] = weights1_ref[1]
    copy.wait()


def last_back_kernel(
    recv_ref, fact_ref, normed_ref, keep_ref, d_gated_ref, unit_ref, scale_ref, grad_ref, gin, proj,
    send_ref, pair_grad_ref, spare, kept_p, pairs,
):
    spare[...] = recv_ref[...].astype(F32)
    gain = as_column(gin, 0)
    outs = []
    d_normed = []
    for h in range(2):
        for t, _ in inner(h):
            projected_back(t, spare, fact_ref, kept_p)
        d_normed.append(mm(proj[0], kept_p[:, wide(h)], 1, 0) + d_gated_ref[:, wide(h)])
    for h in range(2):
        for t, piece in inner(h):
            d_x = standardize_back(
                d_normed[h][:, piece] * gain,
                unit_ref[:, tile(t)],
                scale_ref[pl.ds(0, 1), tile(t)],
            )
            outs.append(grad_ref[:, tile(t)] + d_x)
    normed = normed_ref[...]
    for e in range(4):
        spare[pl.ds(e, C, 8), :] = mm(normed, kept_p[tile(e), :], 1, 1)
        spare[pl.ds(4 + e, C, 8), :] = keep_ref[e]
    send_ref[...] = spare[...].astype(BF16)
    lanes_to_pairs(outs, pair_grad_ref, pairs)


def whole(spare, first):
    return jnp.concatenate([spare[first], spare[first + 1]], axis=1)


def halves(hi, q):
    return pl.ds(q * LANES, LANES), tile(hi)


def second_rows(layer, q):
    return pl.ds(q, 64, 4) if layer == 0 else pl.ds((q % 2) * LANES + q // 2, 64, 2)


def take_operands(recv_ref, put):
    for hi in range(2):
        parts = [recv_ref[pl.ds((4 * hi + lo) * LANES, LANES), :] for lo in range(4)]
        for slot, block in enumerate(swap_slots(parts)):
            put(hi, slot, block)


def send_operands(send_ref, get):
    for hi in range(2):
        parts = [get(hi, slot) for slot in range(4)]
        for lo, block in enumerate(swap_slots(parts)):
            send_ref[pl.ds((4 * hi + lo) * LANES, LANES), :] = block


def send_mixture(layer, mixture, send_ref, spare):
    for hi in range(2):
        spare[hi] = mixture(hi)
    for hi in range(2):
        parts = [spare[hi, second_rows(layer, q), :].astype(BF16) for q in range(4)]
        for lo, block in enumerate(swap_slots(parts)):
            send_ref[pl.ds((4 * hi + lo) * 64, 64), :] = block


def outgoing_kernel(recv_ref, send_ref, left_ref, right_ref, spare):
    def put(hi, slot, block):
        (left_ref if slot < 2 else right_ref)[halves(hi, slot % 2)] = block

    take_operands(recv_ref, put)
    right = right_ref[...]
    send_mixture(0, lambda hi: mm(right, left_ref[:, tile(hi)], 0, 0), send_ref, spare)


def incoming_kernel(recv_ref, send_ref, left_ref, right_ref, spare):
    def put(hi, slot, block):
        if slot < 2:
            spare[hi, pl.ds(slot, LANES, 2), :] = block.astype(F32)
        else:
            right_ref[halves(hi, slot % 2)] = block

    take_operands(recv_ref, put)
    left = whole(spare, 0).astype(BF16)
    left_ref[...] = left
    mixture = mm(right_ref[...], left, 1, 1)
    send_mixture(1, lambda hi: mixture[:, hi * LANES : (hi + 1) * LANES], send_ref, spare)


def incoming_back_kernel(recv_ref, left_ref, right_ref, send_ref, spare, d_rows):
    for hi in range(2):
        parts = [recv_ref[pl.ds((4 * hi + lo) * 64, 64), :] for lo in range(4)]
        for q, block in enumerate(swap_slots(parts)):
            spare[hi, second_rows(1, q), :] = block.astype(F32)
    d_mix = whole(spare, 0).astype(BF16)
    d_left = mm(d_mix, right_ref[...], 0, 0)
    d_rows[...] = mm(d_mix, left_ref[...], 1, 0).astype(BF16)
    for hi in range(2):
        spare[hi] = d_left[:, hi * LANES : (hi + 1) * LANES]

    def get(hi, slot):
        if slot < 2:
            return spare[hi, pl.ds(slot, LANES, 2), :].astype(BF16)
        return d_rows[halves(hi, slot % 2)]

    send_operands(send_ref, get)


def outgoing_back_kernel(
    recv_ref, left_ref, right_ref, send_ref, sums_ref, arrived, spare, d_rows
):
    arrived[...] = recv_ref[...].astype(F32)
    for hi in range(2):
        parts = [
            jnp.concatenate(
                [arrived[pl.ds((4 * hi + lo) * LANES + jm, COLS, 8), :] for jm in range(4)], axis=0
            ).astype(BF16)
            for lo in range(4)
        ]
        for q, block in enumerate(swap_slots(parts)):
            for jm in range(4):
                spare[hi, pl.ds(4 * jm + q, COLS, COLS), :] = block[
                    jm * COLS : (jm + 1) * COLS, :
                ].astype(F32)
    d_mix = whole(spare, 0).astype(BF16)
    d_rows[0] = mm(right_ref[...], d_mix, 1, 0).astype(BF16)
    d_rows[1] = mm(left_ref[...], d_mix, 1, 1).astype(BF16)

    def get(hi, slot):
        rows, lanes = halves(hi, slot % 2)
        return d_rows[slot // 2, rows, lanes]

    send_operands(send_ref, get)
    total = jnp.sum(recv_ref[...].astype(F32).reshape(PEERS, 8, LANES), axis=0)
    sums_ref[...] = total[TILES:]


def collect_kernel(recv_ref, sums_ref, send_ref):
    parts = recv_ref[...].astype(F32).reshape(PEERS, 8, LANES)
    while parts.shape[0] > 1:
        middle = parts.shape[0] // 2
        parts = parts[:middle] + parts[middle:]
    total = parts[0]
    block = [total[0:4], sums_ref[...], total[4:8]]
    both = jnp.concatenate(block + block, axis=0)
    send_ref[...] = (
        jnp.broadcast_to(both[None], (PEERS // 2, 2 * SUMS, LANES))
        .reshape(PEERS * SUMS, LANES)
        .astype(BF16)
    )


def spread_kernel(
    recv_ref, grad_ready, gin, gmid, proj, gate, out_w,
    pair_grad_ref, gin_ref, proj_ref, gate_ref, gmid_ref, out_ref,
    rows, gin_own, proj_own, gate_own, gmid_own, out_own, sems,
):
    copies = []

    def give(own, ref):
        copies.append(pltpu.make_async_copy(own, ref, sems.at[len(copies)]))
        copies[-1].start()

    give(grad_ready, pair_grad_ref)
    rows[...] = recv_ref[...].astype(F32) * (1.0 / TOKENS)
    lane = lane_index(C)
    totals = jnp.zeros((C, LANES), F32)
    for m in range(2):
        gated = rows[pl.ds(8 + m, C, SUMS), :]
        mixed = rows[pl.ds(10 + m, C, SUMS), :]
        total = gated * gate[m].astype(F32)
        for e in range(4):
            part = rows[pl.ds(4 * m + e, C, SUMS), :]
            proj_own[m, :, tile(e)] = part
            total = total + part * proj[m, :, tile(e)].astype(F32)
        give(proj_own.at[m], proj_ref.at[m])
        gate_own[m] = gated
        out_own[m] = mixed
        total_in = jnp.sum(total, axis=1, keepdims=True)
        total_mid = jnp.sum(mixed * out_w[m].astype(F32), axis=1, keepdims=True)
        totals = jnp.where(lane == m, total_in, jnp.where(lane == 2 + m, total_mid, totals))
    give(gate_own, gate_ref)
    give(out_own, out_ref)
    turned = totals.T
    gin_own[...] = turned[0:2] / gin[...]
    gmid_own[...] = turned[2:4] / gmid[...]
    give(gin_own, gin_ref)
    give(gmid_own, gmid_ref)
    for copy in copies:
        copy.wait()


def run(kernel, outs, scratch, args, away=()):
    spaces = [pl.ANY if k in away else pltpu.VMEM for k in range(len(outs))]
    return pl.pallas_call(
        kernel,
        out_shape=[jax.ShapeDtypeStruct(shape, dtype) for shape, dtype in outs],
        in_specs=[pl.BlockSpec(memory_space=pltpu.VMEM)] * len(args),
        out_specs=[pl.BlockSpec(memory_space=space) for space in spaces],
        scratch_shapes=[
            pltpu.VMEM(shape, dtype) if shape else pltpu.SemaphoreType.DMA(dtype)
            for shape, dtype in scratch
        ],
        compiler_params=pltpu.CompilerParams(vmem_limit_bytes=16 * 1024 * 1024),
        cost_estimate=pl.CostEstimate(flops=10**9, bytes_accessed=2**20, transcendentals=2**18),
    )(*args)


def exchange(values, rows):
    return lax.all_to_all(
        values.reshape(-1, rows, LANES), AXES, 0, 0, tiled=True
    ).reshape(values.shape)


def local(pair_in, token_mask, cotangent, gain_in, proj_w, gate_w, gain_mid, out_w):
    operand = ((PEERS * 8, LANES), BF16)
    single = ((PEERS * 4, LANES), BF16)
    sums = (PEERS * SUMS, LANES)
    plane = ((C, PLACE), F32)
    plane_b = ((C, PLACE), BF16)
    four = (4 * C, PLACE)
    scales = ((8, PLACE), F32)
    square = ((TOKENS, TOKENS), BF16)
    spare = ((PEERS * 8, LANES), F32)
    pairs = ((PLACE, C), F32)
    mixed = ((PEERS * 4, LANES), F32)
    half = ((2, TOKENS, LANES), F32)
    pair_shape = ((ROWS, COLS, C), BF16)

    saved0 = [plane, scales, plane_b, (four, BF16), plane, plane_b]
    saved1 = [plane, scales, plane_b, (four, F32), plane, plane_b]
    places = run(place_kernel, [((TOKENS, PLACE), BF16)] * 2, [], ())
    (
        send, unit0, scale0, normed0, fact0, gating0, x0,
        proj, gate, out, gin, gmid, proj_t, gate_t, out_t, valid,
    ) = run(
        first_kernel,
        [operand]
        + saved0
        + [(a.shape, a.dtype) for a in (proj_w, gate_w, out_w, gain_in, gain_mid)]
        + [((2, 4 * C, C), BF16), ((2, C, C), BF16), ((2, C, C), BF16)]
        + [scales],
        [spare, pairs],
        (
            *places, token_mask.reshape(1, TOKENS), pair_in,
            proj_w, gate_w, out_w, gain_in, gain_mid,
        ),
    )
    send, left0, right0 = run(outgoing_kernel, [single, square, square], [half], (exchange(send, 8),))
    (
        send, unit1, scale1, normed1, fact1, gating1, x1,
        mix_unit0, mix_scale0, mix_normed0, gate_fact0,
    ) = run(
        middle_kernel, [operand] + saved1 + [plane, scales, plane_b, plane], [spare, mixed],
        (exchange(send, 4), x0, gating0, valid, gin, gmid, proj_t, gate_t, out_t),
    )
    send, left1, right1 = run(
        incoming_kernel, [single, square, square], [half], (exchange(send, 8),)
    )
    ready_out, send, grad1, d_gated1, weights1 = run(
        turn_kernel, [pair_shape, single, plane, plane, ((2, C, C), F32)],
        [mixed, pairs, plane_b, plane_b, plane_b],
        (exchange(send, 4), x1, gating1, normed1, cotangent, gmid, gate, out, out_t),
    )
    (send,) = run(
        incoming_back_kernel, [operand], [half, square],
        (exchange(send, 4), left1, right1),
    )
    send, grad0, d_gated0, keep, pair_out = run(
        both_back_kernel, [operand, plane, plane, ((4, C, C), F32), pair_shape],
        [spare, (four, BF16), plane_b, plane_b, (None, ())],
        (
            exchange(send, 8), fact1, d_gated1, unit1, scale1, grad1, normed1, weights1,
            gating0, mix_unit0, mix_scale0, mix_normed0, gate_fact0, normed0,
            gin, gmid, proj, gate, out, ready_out,
        ),
        (4,),
    )
    send, sums1 = run(
        outgoing_back_kernel, [operand, ((4, LANES), F32)],
        [spare, half, ((2, TOKENS, TOKENS), BF16)],
        (exchange(send, 8), left0, right0),
    )
    send, ready_grad = run(
        last_back_kernel, [operand, pair_shape], [spare, (four, BF16), pairs],
        (exchange(send, 8), fact0, normed0, keep, d_gated0, unit0, scale0, grad0, gin, proj),
    )
    (send,) = run(collect_kernel, [(sums, BF16)], [], (exchange(send, 8), sums1))
    grads = [(a.shape, F32) for a in (gain_in, proj_w, gate_w, gain_mid, out_w)]
    pair_grad, gin_grad, proj_grad, gate_grad, gmid_grad, out_grad = run(
        spread_kernel, [pair_shape] + grads, [(sums, F32)] + grads + [(None, (7,))],
        (exchange(send, 4), ready_grad, gin, gmid, proj, gate, out),
        range(6),
    )
    return pair_out, pair_grad, gin_grad, proj_grad, gate_grad, gmid_grad, out_grad


def solution(mesh):
    placed = (P("row", "col", None), P(), P("row", "col", None), P(), P(), P(), P(), P())
    return jax.shard_map(
        local,
        mesh=mesh,
        in_specs=placed,
        out_specs=(P("row", "col", None), P("row", "col", None), P(), P(), P(), P(), P()),
        check_vma=False,
    )
```

```python
import jax
import jax.numpy as jnp
from jax import lax
from jax.experimental import pallas as pl
from jax.experimental.pallas import tpu as pltpu
from jax.sharding import PartitionSpec as P

F32 = jnp.float32
BF16 = jnp.bfloat16
C = 128
LANES = 128
ROWS = 32
COLS = 16
TOKENS = 256
PLACE = ROWS * COLS
TILES = PLACE // LANES
PEERS = 128
AXES = ("row", "col")
SUMS = 12


def mm(a, b, a_dim, b_dim):
    return lax.dot_general(
        a.astype(BF16), b.astype(BF16), (((a_dim,), (b_dim,)), ((), ())), preferred_element_type=F32
    )


WIDE = PLACE // 2


def wide(h):
    return pl.ds(h * WIDE, WIDE)


def inner(h):
    return [(2 * h + k, slice(k * LANES, (k + 1) * LANES)) for k in range(2)]


def tile(t):
    return pl.ds(t * LANES, LANES)


def lane_index(rows):
    return lax.broadcasted_iota(jnp.int32, (rows, LANES), 1)


def swap_slots(parts):
    lane = lane_index(parts[0].shape[0])
    low = lane < 64
    even = (lane // 32) % 2 == 0
    turned = [pltpu.roll(part, 64, 1) for part in parts]
    first = [
        jnp.where(low, parts[0], turned[2]),
        jnp.where(low, parts[1], turned[3]),
        jnp.where(low, turned[0], parts[2]),
        jnp.where(low, turned[1], parts[3]),
    ]
    result = []
    for base in (0, 2):
        result.append(jnp.where(even, first[base], pltpu.roll(first[base + 1], 32, 1)))
        result.append(jnp.where(even, pltpu.roll(first[base], 96, 1), first[base + 1]))
    return result


def as_column(gain_ref, layer):
    return jnp.broadcast_to(gain_ref[pl.ds(layer, 1), :], (LANES, LANES)).T


def standardize(values):
    average = jnp.mean(values, axis=0, keepdims=True)
    centered = values - average
    variance = jnp.mean(centered * centered, axis=0, keepdims=True)
    scale = lax.rsqrt(variance + 1e-05)
    return centered * scale, scale


def standardize_back(d_unit, unit, scale):
    mean_d = jnp.mean(d_unit, axis=0, keepdims=True)
    mean_du = jnp.mean(d_unit * unit, axis=0, keepdims=True)
    return scale * (d_unit - mean_d - unit * mean_du)


def pairs_to_lanes(pairs_ref, spare):
    spare[...] = pairs_ref[...].astype(F32).reshape(PLACE, C)
    tiles = []
    for t in range(TILES):
        block = jnp.concatenate(
            [spare[pl.ds(4 * t + q, ROWS, COLS), :] for q in range(4)], axis=0
        )
        tiles.append(block.T)
    return tiles


def lanes_to_pairs(tiles, pairs_ref, spare):
    for t in range(TILES):
        block = tiles[t].T
        for q in range(4):
            spare[pl.ds(4 * t + q, ROWS, COLS), :] = block[q * ROWS : (q + 1) * ROWS, :]
    pairs_ref[...] = spare[...].reshape(ROWS, COLS, C).astype(pairs_ref.dtype)


def put_operands(t, left, right, spare):
    low = lane_index(C) < 64
    spare[pl.ds(2 * t, C, 8), :] = jnp.where(low, left, pltpu.roll(right, 64, 1))
    spare[pl.ds(2 * t + 1, C, 8), :] = jnp.where(low, pltpu.roll(left, 64, 1), right)


def get_operands(t, spare, dtype):
    low = lane_index(C) < 64
    even = spare[pl.ds(2 * t, C, 8), :].astype(dtype)
    odd = spare[pl.ds(2 * t + 1, C, 8), :].astype(dtype)
    left = jnp.where(low, even, pltpu.roll(odd, 64, 1))
    right = jnp.where(low, pltpu.roll(even, 64, 1), odd)
    return left, right


def front(h, tiles, gain, proj_t, gate_t, layer, spare, saved, valid):
    unit_ref, scale_ref, normed_ref, fact_ref, gating_ref = saved
    for (t, _), values in zip(inner(h), tiles):
        unit, scale = standardize(values)
        unit_ref[:, tile(t)] = unit
        scale_ref[:, tile(t)] = jnp.broadcast_to(scale, (8, LANES))
        normed_ref[:, tile(t)] = (unit * gain).astype(BF16)
    normed = normed_ref[:, wide(h)]
    parts = []
    for base in (0, 2):
        closed = mm(proj_t[layer, pl.ds(base * C, C), :], normed, 1, 0)
        value = mm(proj_t[layer, pl.ds((base + 1) * C, C), :], normed, 1, 0)
        opened = jax.nn.sigmoid(closed)
        operand = opened * value * valid
        fact_ref[pl.ds(base * C, C), wide(h)] = (operand * (1.0 - opened)).astype(fact_ref.dtype)
        fact_ref[pl.ds((base + 1) * C, C), wide(h)] = (opened * valid).astype(fact_ref.dtype)
        parts.append(operand)
    for t, piece in inner(h):
        put_operands(t, parts[0][:, piece], parts[1][:, piece], spare)
    gating_ref[:, wide(h)] = jax.nn.sigmoid(mm(gate_t[layer], normed, 1, 0))


def place_kernel(first_ref, second_ref):
    token = lax.broadcasted_iota(jnp.int32, (TOKENS, PLACE), 0)
    place = lax.broadcasted_iota(jnp.int32, (TOKENS, PLACE), 1)
    first = place % ROWS + ROWS * lax.axis_index("row")
    second = place // ROWS + COLS * lax.axis_index("col")
    first_ref[...] = (token == first).astype(F32).astype(BF16)
    second_ref[...] = (token == second).astype(F32).astype(BF16)


def first_kernel(
    first_ref, second_ref, tok, pair_ref, proj, gate, out_w, gin, gmid,
    send_ref, unit_ref, scale_ref, normed_ref, fact_ref, gating_ref, x_ref,
    proj_out, gate_out, out_out, gin_out, gmid_out, proj_t, gate_t, out_t,
    valid_ref, spare, pairs,
):
    token = jnp.broadcast_to(tok[...].astype(F32), (8, TOKENS))
    valid_ref[...] = mm(token, first_ref[...], 1, 0) * mm(token, second_ref[...], 1, 0)
    for m in range(2):
        proj_t[m] = proj[m].T
        gate_t[m] = gate[m].T
        out_t[m] = out_w[m].T
    gain = as_column(gin, 0)
    tiles = pairs_to_lanes(pair_ref, pairs)
    saved = (unit_ref, scale_ref, normed_ref, fact_ref, gating_ref)
    for t in range(TILES):
        x_ref[:, tile(t)] = tiles[t].astype(BF16)
    for h in range(2):
        valid = valid_ref[pl.ds(0, 1), wide(h)]
        front(h, tiles[2 * h : 2 * h + 2], gain, proj_t, gate_t, 0, spare, saved, valid)
    send_ref[...] = spare[...].astype(BF16)
    for given, kept in (
        (proj, proj_out), (gate, gate_out), (out_w, out_out),
        (gin, gin_out), (gmid, gmid_out),
    ):
        kept[...] = given[...]


def middle_kernel(
    mix_ref, x_ref, gating0_ref, valid_ref, gin, gmid, proj_t, gate_t, out_t,
    send_ref, unit_ref, scale_ref, normed_ref, fact_ref, gating_ref, next_ref,
    mix_unit_ref, mix_scale_ref, mix_normed_ref, gate_fact_ref, spare, mixed,
):
    mixed[...] = mix_ref[...].astype(F32)
    gain_a = as_column(gmid, 0)
    gain_b = as_column(gin, 1)
    saved = (unit_ref, scale_ref, normed_ref, fact_ref, gating_ref)
    updates = []
    for h in range(2):
        for t, _ in inner(h):
            unit, scale = standardize(mixed[pl.ds(t, C, TILES), :])
            mix_unit_ref[:, tile(t)] = unit
            mix_scale_ref[:, tile(t)] = jnp.broadcast_to(scale, (8, LANES))
            mix_normed_ref[:, tile(t)] = (unit * gain_a).astype(BF16)
        updates.append(mm(out_t[0], mix_normed_ref[:, wide(h)], 1, 0))
    for h in range(2):
        tiles = []
        for t, piece in inner(h):
            gating = gating0_ref[:, tile(t)]
            gated = updates[h][:, piece] * gating
            rounded = (x_ref[:, tile(t)].astype(F32) + gated).astype(BF16)
            next_ref[:, tile(t)] = rounded
            gate_fact_ref[:, tile(t)] = gated * (1.0 - gating)
            tiles.append(rounded.astype(F32))
        valid = valid_ref[pl.ds(0, 1), wide(h)]
        front(h, tiles, gain_b, proj_t, gate_t, 1, spare, saved, valid)
    send_ref[...] = spare[...].astype(BF16)


def turn_kernel(
    mix_ref, x_ref, gating_ref, normed_ref, cot_ref, gmid, gate, out_w, out_t,
    pair_out_ref, send_ref, grad_ref, d_gated_ref, weights_ref,
    mixed, pairs, kept_n, kept_g, kept_d,
):
    mixed[...] = mix_ref[...].astype(F32)
    gain = as_column(gmid, 1)
    cot = pairs_to_lanes(cot_ref, pairs)
    units, d_normed, update = [], [], []
    for h in range(2):
        for t, _ in inner(h):
            units.append(standardize(mixed[pl.ds(t, C, TILES), :]))
            kept_n[:, tile(t)] = (units[t][0] * gain).astype(BF16)
            grad_ref[:, tile(t)] = cot[t].astype(BF16)
            kept_d[:, tile(t)] = (cot[t] * gating_ref[:, tile(t)]).astype(BF16)
        d_normed.append(mm(out_w[1], kept_d[:, wide(h)], 1, 0))
        update.append(mm(out_t[1], kept_n[:, wide(h)], 1, 0))
    outs = []
    for h in range(2):
        for t, piece in inner(h):
            mixed[pl.ds(t, C, TILES), :] = standardize_back(d_normed[h][:, piece] * gain, *units[t])
            gating = gating_ref[:, tile(t)]
            gated = update[h][:, piece] * gating
            outs.append(x_ref[:, tile(t)].astype(F32) + gated)
            kept_g[:, tile(t)] = (cot[t] * gated * (1.0 - gating)).astype(BF16)
    d_gated_ref[...] = mm(gate[1], kept_g[...], 1, 0)
    send_ref[...] = mixed[...].astype(BF16)
    weights_ref[0] = mm(normed_ref[...], kept_g[...], 1, 1)
    weights_ref[1] = mm(kept_n[...], kept_d[...], 1, 1)
    lanes_to_pairs(outs, pair_out_ref, pairs)


def projected_back(t, spare, fact_ref, kept_p):
    d_left, d_right = get_operands(t, spare, fact_ref.dtype)
    for part, d_out in enumerate((d_left, d_left, d_right, d_right)):
        rows = pl.ds(part * C, C)
        kept_p[rows, tile(t)] = (d_out * fact_ref[rows, tile(t)]).astype(BF16)


def both_back_kernel(
    recv_ref, fact_ref, d_gated1_ref, unit_ref, scale_ref, grad_ref, normed1_ref, weights1_ref,
    gating_ref, mix_unit_ref, mix_scale_ref, mix_normed_ref, gate_fact_ref, normed0_ref,
    gin, gmid, proj, gate, out_w, out_ready,
    send_ref, next_grad_ref, d_gated_ref, keep_ref, pair_out_ref,
    spare, kept_p, kept_g, kept_d, sem,
):
    copy = pltpu.make_async_copy(out_ready, pair_out_ref, sem)
    copy.start()
    spare[...] = recv_ref[...].astype(F32)
    gain_a = as_column(gin, 1)
    gain_b = as_column(gmid, 0)
    d_normed = []
    for h in range(2):
        for t, _ in inner(h):
            projected_back(t, spare, fact_ref, kept_p)
        d_normed.append(mm(proj[1], kept_p[:, wide(h)], 1, 0) + d_gated1_ref[:, wide(h)])
    d_mid = []
    for h in range(2):
        for t, piece in inner(h):
            d_x = standardize_back(
                d_normed[h][:, piece] * gain_a,
                unit_ref[:, tile(t)],
                scale_ref[pl.ds(0, 1), tile(t)],
            )
            grad = grad_ref[:, tile(t)].astype(F32) + d_x
            next_grad_ref[:, tile(t)] = grad
            kept_d[:, tile(t)] = (grad * gating_ref[:, tile(t)]).astype(BF16)
            kept_g[:, tile(t)] = (grad * gate_fact_ref[:, tile(t)]).astype(BF16)
        d_mid.append(mm(out_w[0], kept_d[:, wide(h)], 1, 0))
    normed1 = normed1_ref[...]
    for h in range(2):
        for t, piece in inner(h):
            spare[pl.ds(t, C, 8), :] = standardize_back(
                d_mid[h][:, piece] * gain_b,
                mix_unit_ref[:, tile(t)],
                mix_scale_ref[pl.ds(0, 1), tile(t)],
            )
            spare[pl.ds(TILES + t, C, 8), :] = mm(normed1, kept_p[tile(t), :], 1, 1)
    d_gated_ref[...] = mm(gate[0], kept_g[...], 1, 0)
    send_ref[...] = spare[...].astype(BF16)
    keep_ref[0] = mm(normed0_ref[...], kept_g[...], 1, 1)
    keep_ref[1] = weights1_ref[0]
    keep_ref[2] = mm(mix_normed_ref[...], kept_d[...], 1, 1)
    keep_ref[3] = weights1_ref[1]
    copy.wait()


def last_back_kernel(
    recv_ref, fact_ref, normed_ref, keep_ref, d_gated_ref, unit_ref, scale_ref, grad_ref, gin, proj,
    send_ref, pair_grad_ref, spare, kept_p, pairs,
):
    spare[...] = recv_ref[...].astype(F32)
    gain = as_column(gin, 0)
    outs = []
    d_normed = []
    for h in range(2):
        for t, _ in inner(h):
            projected_back(t, spare, fact_ref, kept_p)
        d_normed.append(mm(proj[0], kept_p[:, wide(h)], 1, 0) + d_gated_ref[:, wide(h)])
    for h in range(2):
        for t, piece in inner(h):
            d_x = standardize_back(
                d_normed[h][:, piece] * gain,
                unit_ref[:, tile(t)],
                scale_ref[pl.ds(0, 1), tile(t)],
            )
            outs.append(grad_ref[:, tile(t)] + d_x)
    normed = normed_ref[...]
    for e in range(4):
        spare[pl.ds(e, C, 8), :] = mm(normed, kept_p[tile(e), :], 1, 1)
        spare[pl.ds(4 + e, C, 8), :] = keep_ref[e]
    send_ref[...] = spare[...].astype(BF16)
    lanes_to_pairs(outs, pair_grad_ref, pairs)


def whole(spare, first):
    return jnp.concatenate([spare[first], spare[first + 1]], axis=1)


def halves(hi, q):
    return pl.ds(q * LANES, LANES), tile(hi)


def second_rows(layer, q):
    return pl.ds(q, 64, 4) if layer == 0 else pl.ds((q % 2) * LANES + q // 2, 64, 2)


def take_operands(recv_ref, put):
    for hi in range(2):
        parts = [recv_ref[pl.ds((4 * hi + lo) * LANES, LANES), :] for lo in range(4)]
        for slot, block in enumerate(swap_slots(parts)):
            put(hi, slot, block)


def send_operands(send_ref, get):
    for hi in range(2):
        parts = [get(hi, slot) for slot in range(4)]
        for lo, block in enumerate(swap_slots(parts)):
            send_ref[pl.ds((4 * hi + lo) * LANES, LANES), :] = block


def send_mixture(layer, mixture, send_ref, spare):
    for hi in range(2):
        spare[hi] = mixture(hi)
    for hi in range(2):
        parts = [spare[hi, second_rows(layer, q), :].astype(BF16) for q in range(4)]
        for lo, block in enumerate(swap_slots(parts)):
            send_ref[pl.ds((4 * hi + lo) * 64, 64), :] = block


def outgoing_kernel(recv_ref, send_ref, left_ref, right_ref, spare):
    def put(hi, slot, block):
        (left_ref if slot < 2 else right_ref)[halves(hi, slot % 2)] = block

    take_operands(recv_ref, put)
    right = right_ref[...]
    send_mixture(0, lambda hi: mm(right, left_ref[:, tile(hi)], 0, 0), send_ref, spare)


def incoming_kernel(recv_ref, send_ref, left_ref, right_ref, spare):
    def put(hi, slot, block):
        if slot < 2:
            spare[hi, pl.ds(slot, LANES, 2), :] = block.astype(F32)
        else:
            right_ref[halves(hi, slot % 2)] = block

    take_operands(recv_ref, put)
    left = whole(spare, 0).astype(BF16)
    left_ref[...] = left
    mixture = mm(right_ref[...], left, 1, 1)
    send_mixture(1, lambda hi: mixture[:, hi * LANES : (hi + 1) * LANES], send_ref, spare)


def incoming_back_kernel(recv_ref, left_ref, right_ref, send_ref, spare, d_rows):
    for hi in range(2):
        parts = [recv_ref[pl.ds((4 * hi + lo) * 64, 64), :] for lo in range(4)]
        for q, block in enumerate(swap_slots(parts)):
            spare[hi, second_rows(1, q), :] = block.astype(F32)
    d_mix = whole(spare, 0).astype(BF16)
    d_left = mm(d_mix, right_ref[...], 0, 0)
    d_rows[...] = mm(d_mix, left_ref[...], 1, 0).astype(BF16)
    for hi in range(2):
        spare[hi] = d_left[:, hi * LANES : (hi + 1) * LANES]

    def get(hi, slot):
        if slot < 2:
            return spare[hi, pl.ds(slot, LANES, 2), :].astype(BF16)
        return d_rows[halves(hi, slot % 2)]

    send_operands(send_ref, get)


def outgoing_back_kernel(
    recv_ref, left_ref, right_ref, send_ref, sums_ref, arrived, spare, d_rows
):
    arrived[...] = recv_ref[...].astype(F32)
    for hi in range(2):
        parts = [
            jnp.concatenate(
                [arrived[pl.ds((4 * hi + lo) * LANES + jm, COLS, 8), :] for jm in range(4)], axis=0
            ).astype(BF16)
            for lo in range(4)
        ]
        for q, block in enumerate(swap_slots(parts)):
            for jm in range(4):
                spare[hi, pl.ds(4 * jm + q, COLS, COLS), :] = block[
                    jm * COLS : (jm + 1) * COLS, :
                ].astype(F32)
    d_mix = whole(spare, 0).astype(BF16)
    d_rows[0] = mm(right_ref[...], d_mix, 1, 0).astype(BF16)
    d_rows[1] = mm(left_ref[...], d_mix, 1, 1).astype(BF16)

    def get(hi, slot):
        rows, lanes = halves(hi, slot % 2)
        return d_rows[slot // 2, rows, lanes]

    send_operands(send_ref, get)
    total = jnp.sum(recv_ref[...].astype(F32).reshape(PEERS, 8, LANES), axis=0)
    sums_ref[...] = total[TILES:]


def collect_kernel(recv_ref, sums_ref, send_ref):
    parts = recv_ref[...].astype(F32).reshape(PEERS, 8, LANES)
    while parts.shape[0] > 1:
        middle = parts.shape[0] // 2
        parts = parts[:middle] + parts[middle:]
    total = parts[0]
    block = [total[0:4], sums_ref[...], total[4:8]]
    both = jnp.concatenate(block + block, axis=0)
    send_ref[...] = (
        jnp.broadcast_to(both[None], (PEERS // 2, 2 * SUMS, LANES))
        .reshape(PEERS * SUMS, LANES)
        .astype(BF16)
    )


def spread_kernel(
    recv_ref, grad_ready, gin, gmid, proj, gate, out_w,
    pair_grad_ref, gin_ref, proj_ref, gate_ref, gmid_ref, out_ref,
    rows, gin_own, proj_own, gate_own, gmid_own, out_own, sems,
):
    copies = []

    def give(own, ref):
        copies.append(pltpu.make_async_copy(own, ref, sems.at[len(copies)]))
        copies[-1].start()

    give(grad_ready, pair_grad_ref)
    rows[...] = recv_ref[...].astype(F32) * (1.0 / TOKENS)
    lane = lane_index(C)
    totals = jnp.zeros((C, LANES), F32)
    for m in range(2):
        gated = rows[pl.ds(8 + m, C, SUMS), :]
        mixed = rows[pl.ds(10 + m, C, SUMS), :]
        total = gated * gate[m].astype(F32)
        for e in range(4):
            part = rows[pl.ds(4 * m + e, C, SUMS), :]
            proj_own[m, :, tile(e)] = part
            total = total + part * proj[m, :, tile(e)].astype(F32)
        give(proj_own.at[m], proj_ref.at[m])
        gate_own[m] = gated
        out_own[m] = mixed
        total_in = jnp.sum(total, axis=1, keepdims=True)
        total_mid = jnp.sum(mixed * out_w[m].astype(F32), axis=1, keepdims=True)
        totals = jnp.where(lane == m, total_in, jnp.where(lane == 2 + m, total_mid, totals))
    give(gate_own, gate_ref)
    give(out_own, out_ref)
    turned = totals.T
    gin_own[...] = turned[0:2] / gin[...]
    gmid_own[...] = turned[2:4] / gmid[...]
    give(gin_own, gin_ref)
    give(gmid_own, gmid_ref)
    for copy in copies:
        copy.wait()


def run(kernel, outs, scratch, args, away=()):
    spaces = [pl.ANY if k in away else pltpu.VMEM for k in range(len(outs))]
    return pl.pallas_call(
        kernel,
        out_shape=[jax.ShapeDtypeStruct(shape, dtype) for shape, dtype in outs],
        in_specs=[pl.BlockSpec(memory_space=pltpu.VMEM)] * len(args),
        out_specs=[pl.BlockSpec(memory_space=space) for space in spaces],
        scratch_shapes=[
            pltpu.VMEM(shape, dtype) if shape else pltpu.SemaphoreType.DMA(dtype)
            for shape, dtype in scratch
        ],
        compiler_params=pltpu.CompilerParams(vmem_limit_bytes=16 * 1024 * 1024),
        cost_estimate=pl.CostEstimate(flops=10**9, bytes_accessed=2**20, transcendentals=2**18),
    )(*args)


def exchange(values, rows):
    return lax.all_to_all(
        values.reshape(-1, rows, LANES), AXES, 0, 0, tiled=True
    ).reshape(values.shape)


def local(pair_in, token_mask, cotangent, gain_in, proj_w, gate_w, gain_mid, out_w):
    operand = ((PEERS * 8, LANES), BF16)
    single = ((PEERS * 4, LANES), BF16)
    sums = (PEERS * SUMS, LANES)
    plane = ((C, PLACE), F32)
    plane_b = ((C, PLACE), BF16)
    four = (4 * C, PLACE)
    scales = ((8, PLACE), F32)
    square = ((TOKENS, TOKENS), BF16)
    spare = ((PEERS * 8, LANES), F32)
    pairs = ((PLACE, C), F32)
    mixed = ((PEERS * 4, LANES), F32)
    half = ((2, TOKENS, LANES), F32)
    pair_shape = ((ROWS, COLS, C), BF16)

    saved0 = [plane, scales, plane_b, (four, BF16), plane, plane_b]
    saved1 = [plane, scales, plane_b, (four, F32), plane, plane_b]
    places = run(place_kernel, [((TOKENS, PLACE), BF16)] * 2, [], ())
    (
        send, unit0, scale0, normed0, fact0, gating0, x0,
        proj, gate, out, gin, gmid, proj_t, gate_t, out_t, valid,
    ) = run(
        first_kernel,
        [operand]
        + saved0
        + [(a.shape, a.dtype) for a in (proj_w, gate_w, out_w, gain_in, gain_mid)]
        + [((2, 4 * C, C), BF16), ((2, C, C), BF16), ((2, C, C), BF16)]
        + [scales],
        [spare, pairs],
        (
            *places, token_mask.reshape(1, TOKENS), pair_in,
            proj_w, gate_w, out_w, gain_in, gain_mid,
        ),
    )
    send, left0, right0 = run(outgoing_kernel, [single, square, square], [half], (exchange(send, 8),))
    (
        send, unit1, scale1, normed1, fact1, gating1, x1,
        mix_unit0, mix_scale0, mix_normed0, gate_fact0,
    ) = run(
        middle_kernel, [operand] + saved1 + [plane, scales, plane_b, plane], [spare, mixed],
        (exchange(send, 4), x0, gating0, valid, gin, gmid, proj_t, gate_t, out_t),
    )
    send, left1, right1 = run(
        incoming_kernel, [single, square, square], [half], (exchange(send, 8),)
    )
    ready_out, send, grad1, d_gated1, weights1 = run(
        turn_kernel, [pair_shape, single, plane_b, plane, ((2, C, C), F32)],
        [mixed, pairs, plane_b, plane_b, plane_b],
        (exchange(send, 4), x1, gating1, normed1, cotangent, gmid, gate, out, out_t),
    )
    (send,) = run(
        incoming_back_kernel, [operand], [half, square],
        (exchange(send, 4), left1, right1),
    )
    send, grad0, d_gated0, keep, pair_out = run(
        both_back_kernel, [operand, plane, plane, ((4, C, C), F32), pair_shape],
        [spare, (four, BF16), plane_b, plane_b, (None, ())],
        (
            exchange(send, 8), fact1, d_gated1, unit1, scale1, grad1, normed1, weights1,
            gating0, mix_unit0, mix_scale0, mix_normed0, gate_fact0, normed0,
            gin, gmid, proj, gate, out, ready_out,
        ),
        (4,),
    )
    send, sums1 = run(
        outgoing_back_kernel, [operand, ((4, LANES), F32)],
        [spare, half, ((2, TOKENS, TOKENS), BF16)],
        (exchange(send, 8), left0, right0),
    )
    send, ready_grad = run(
        last_back_kernel, [operand, pair_shape], [spare, (four, BF16), pairs],
        (exchange(send, 8), fact0, normed0, keep, d_gated0, unit0, scale0, grad0, gin, proj),
    )
    (send,) = run(collect_kernel, [(sums, BF16)], [], (exchange(send, 8), sums1))
    grads = [(a.shape, F32) for a in (gain_in, proj_w, gate_w, gain_mid, out_w)]
    pair_grad, gin_grad, proj_grad, gate_grad, gmid_grad, out_grad = run(
        spread_kernel, [pair_shape] + grads, [(sums, F32)] + grads + [(None, (7,))],
        (exchange(send, 4), ready_grad, gin, gmid, proj, gate, out),
        range(6),
    )
    return pair_out, pair_grad, gin_grad, proj_grad, gate_grad, gmid_grad, out_grad


def solution(mesh):
    placed = (P("row", "col", None), P(), P("row", "col", None), P(), P(), P(), P(), P())
    return jax.shard_map(
        local,
        mesh=mesh,
        in_specs=placed,
        out_specs=(P("row", "col", None), P("row", "col", None), P(), P(), P(), P(), P()),
        check_vma=False,
    )
```
